128 devices in a mesh: ctx: 16 (over y, z_lo, core), fsdp: 8 (over x, z_hi).
Axes of the slice: x: 4, y: 4, z: 4 (z_hi: 2, z_lo: 2; z = z_hi * 2 + z_lo), core: 2. Of those that a mesh axis runs over, the one named last changes fastest.
Arguments:
- tokens: bfloat16 [8, 2048, 2048], P('fsdp', 'ctx'), may hold values from -6 to 6
- cotangent: bfloat16 [8, 2048, 2048], P('fsdp', 'ctx'), may hold values from -6 to 6
- block_order: int32 [32], replicated, may hold values from 0 to 31, as said below
- positions: int32 [8, 2048], P('fsdp', 'ctx'), may hold values from 0 to 4094, as said below
- ln_gain: bfloat16 [2048], P('fsdp'), may hold values from 0.5 to 1.5
- ln_bias: bfloat16 [2048], P('fsdp'), may hold values from -4 to 4
- w_qkv: bfloat16 [2048, 6144], P('fsdp'), may hold values from -0.1875 to 0.1875
- b_qkv: bfloat16 [6144], P('fsdp'), may hold values from -4 to 4
- w_dense: bfloat16 [2048, 2048], P('fsdp'), may hold values from -1 to 1
- b_dense: bfloat16 [2048], P('fsdp'), may hold values from -4 to 4
- w_fc1: bfloat16 [2048, 8192], P('fsdp'), may hold values from -0.125 to 0.125
- b_fc1: bfloat16 [8192], P('fsdp'), may hold values from -6 to 6
- w_fc2: bfloat16 [8192, 2048], P('fsdp'), may hold values from -0.0625 to 0.0625
- b_fc2: bfloat16 [2048], P('fsdp'), may hold values from -4 to 4
Outputs:
- output: bfloat16 [8, 2048, 2048], P('fsdp', 'ctx')
- input_grad: float32 [8, 2048, 2048], P('fsdp', 'ctx')
- grad_ln_gain: float32 [2048], P('fsdp')
- grad_ln_bias: float32 [2048], P('fsdp')
- grad_w_qkv: float32 [2048, 6144], P('fsdp')
- grad_b_qkv: float32 [6144], P('fsdp')
- grad_w_dense: float32 [2048, 2048], P('fsdp')
- grad_b_dense: float32 [2048], P('fsdp')
- grad_w_fc1: float32 [2048, 8192], P('fsdp')
- grad_b_fc1: float32 [8192], P('fsdp')
- grad_w_fc2: float32 [8192, 2048], P('fsdp')
- grad_b_fc2: float32 [2048], P('fsdp')
The draws below stay inside these ranges and needn't reach their ends.
Inputs may be any that keep to these rules, and one draw needn't show every extreme that they name: `block_order`: a permutation of the block numbers; the two stored blocks of each ctx device (entries 2c and 2c + 1) add up to 31, in either order. Taken in the initial token order of each sequence, positions start at 0, rise by 1 to 3 from token to token, and the last token's position is 4094.
All inputs are finite; a program needn't handle non-finite values.
Results may differ from the reference program's by a relative error of at most 0.024.
Values may be sent and summed in bfloat16 or wider, within the bound.
A program may use at most 512 MiB of HBM per device.

```python
import math
import jax
import jax.numpy as jnp
from jax import lax

D = 2048
HEADS = 32
HEAD_DIM = 64
ROTARY = 32
FF = 8192
SEQ = 2048
SEQS = 8
BLK = 64
N_CTX = 16


def shared_layout(key):
    turned = jax.random.permutation(jax.random.fold_in(key, 11), N_CTX).astype(jnp.int32)
    flipped = jax.random.randint(jax.random.fold_in(key, 12), (N_CTX,), 0, 2)
    mirror = 2 * N_CTX - 1 - turned
    first_block = jnp.where(flipped == 1, mirror, turned)
    second_block = jnp.where(flipped == 1, turned, mirror)
    return jnp.stack([first_block, second_block], axis=1).reshape(2 * N_CTX).astype(jnp.int32)


def draw_block_order(key, part):
    return shared_layout(key)


def draw_positions(key, part):
    layout = shared_layout(key)
    key = jax.random.fold_in(key, 5)
    paired = jax.random.randint(key, (SEQS, SEQ // 2), 1, 4).astype(jnp.int32)
    pairs = jnp.stack([paired, 4 - paired], axis=2).reshape(SEQS, SEQ)
    first_col = jnp.ones((SEQS, 1), jnp.int32)
    last_col = jnp.full((SEQS, 1), 2, jnp.int32)
    steps_drawn = jnp.concatenate([first_col, pairs[:, :SEQ - 2], last_col], axis=1)
    initial = jnp.cumsum(steps_drawn, axis=1) - 1
    stored_rows = (layout[:, None] * BLK + jnp.arange(BLK, dtype=jnp.int32)[None, :]).reshape(SEQ)
    return initial[:, stored_rows].astype(jnp.int32)


def shard_levels(stream_key, extent, pieces, low, top_value):
    def one(axis_at, blocks):
        draws = jax.random.uniform(jax.random.fold_in(jax.random.fold_in(stream_key, 6), axis_at), (blocks,), jnp.float32, low / len(pieces), top_value / len(pieces))
        return jnp.repeat(jnp.exp(draws), extent[axis_at] // blocks).reshape((-1,) + (1,) * (len(extent) - axis_at - 1))

    loudness = one(*pieces[0])
    for cut in pieces[1:]:
        loudness = loudness * one(*cut)
    return loudness


def noise(rng, extent, deviation, most, cuts=(), held_as=jnp.bfloat16):
    values = deviation * jax.random.normal(rng, extent, jnp.float32)
    if cuts:
        values = values * shard_levels(rng, extent, cuts, -0.22, 0.18)
    return jnp.clip(values, -most, most).astype(held_as)


def setup_inputs(seed: int = 0) -> dict:
    splits = jax.random.split(jax.random.key(seed), 15)
    tokens = noise(splits[0], (SEQS, SEQ, D), 1.0, 6.0, ((0, 8), (1, 16)))
    cotangent = noise(splits[1], (SEQS, SEQ, D), 1.0, 6.0, ((0, 8), (1, 16)))
    block_order = draw_block_order(jax.random.fold_in(splits[14], 71), 0)
    positions = draw_positions(jax.random.fold_in(splits[14], 71), 0)
    ln_gain = jnp.clip(1.0 + 0.1 * jax.random.normal(splits[4], (D,), jnp.float32), 0.5, 1.5).astype(jnp.bfloat16)
    ln_bias = noise(splits[5], (D,), 0.3, 4.0, ((0, 8),))
    w_qkv = noise(splits[6], (D, 3 * D), (D // 2) ** -0.5, 0.1875, ((0, 8),))
    b_qkv = noise(splits[7], (3 * D,), 0.3, 4.0, ((0, 8),))
    w_dense = noise(splits[8], (D, D), (D // 64) ** -0.5, 1.0, ((0, 8),))
    b_dense = noise(splits[9], (D,), 0.3, 4.0, ((0, 8),))
    w_fc1 = noise(splits[10], (D, FF), D ** -0.5, 0.125, ((0, 8),))
    b_fc1 = noise(splits[11], (FF,), 0.5, 6.0, ((0, 8),))
    w_fc2 = noise(splits[12], (FF, D), FF ** -0.5, 0.0625, ((0, 8),))
    b_fc2 = noise(splits[13], (D,), 0.3, 4.0, ((0, 8),))
    return {"tokens": tokens, "cotangent": cotangent, "block_order": block_order, "positions": positions, "ln_gain": ln_gain, "ln_bias": ln_bias, "w_qkv": w_qkv, "b_qkv": b_qkv, "w_dense": w_dense, "b_dense": b_dense, "w_fc1": w_fc1, "b_fc1": b_fc1, "w_fc2": w_fc2, "b_fc2": b_fc2}


NORM_EPS = 1e-05
ROPE_BASE = 10000.0
GELU_COEF = 0.7978845608028654

@jax.custom_vjp
def low(v):
    return lax.optimization_barrier(v.astype(jnp.bfloat16)).astype(jnp.float32)

@jax.custom_vjp
def low_back(v):
    return v

def low_keep(v):
    return (low(v), None)

def low_pass(kept, grad):
    return (grad,)

def back_keep(v):
    return (v, None)

def back_low(kept, grad):
    return (low(grad),)
low.defvjp(low_keep, low_pass)
low_back.defvjp(back_keep, back_low)

def gelu_tanh(values):
    return 0.5 * values * (1.0 + jnp.tanh(GELU_COEF * (values + 0.044715 * values * values * values)))

def angles(positions):
    frequency = ROPE_BASE ** (-(jnp.arange(ROTARY // 2, dtype=jnp.float32) * (2.0 / ROTARY)))
    turned = positions.astype(jnp.float32)[..., None] * frequency
    return (jnp.cos(turned)[..., None, :], jnp.sin(turned)[..., None, :])

def rotate(headed, cosine, sines):
    half_rot = cosine.shape[-1]
    first_half = headed[..., :half_rot]
    second_half = headed[..., half_rot:2 * half_rot]
    rest_dims = headed[..., 2 * half_rot:]
    return jnp.concatenate([first_half * cosine - second_half * sines, second_half * cosine + first_half * sines, rest_dims], axis=-1)

def attend(queries, keys_rot, values_low, anchor):
    span = math.gcd(SEQ, 512)

    def one_block(parts):
        query_block, query_anchor = parts
        raw_scores = jnp.einsum('qhd,khd->hqk', query_block, keys_rot, precision=lax.Precision.HIGHEST)
        scores = low_back(raw_scores * HEAD_DIM ** (-0.5))
        allowed = anchor[None, None, :] <= query_anchor[None, :, None]
        masked = jnp.where(allowed, scores, -1e+30)
        weights = jnp.exp(masked - lax.optimization_barrier(jnp.max(masked, axis=-1, keepdims=True)))
        probs = low(weights / lax.optimization_barrier(jnp.sum(weights, axis=-1, keepdims=True)))
        return jnp.einsum('hqk,khd->qhd', probs, values_low, precision=lax.Precision.HIGHEST)
    blocks_out = lax.map(jax.checkpoint(one_block), (queries.reshape(SEQ // span, span, HEADS, HEAD_DIM), anchor.reshape(SEQ // span, span)))
    return blocks_out.reshape(SEQ, HEADS, HEAD_DIM)

def layer_forward(inputs, ln_gain, ln_bias, w_qkv, b_qkv, w_dense, b_dense, w_fc1, b_fc1, w_fc2, b_fc2, anchor, cosine, sines):
    centre_mean = lax.optimization_barrier(jnp.mean(inputs, axis=-1, keepdims=True))
    centered = inputs - centre_mean
    variance = lax.optimization_barrier(jnp.mean(centered * centered, axis=-1, keepdims=True))
    normed = centered * lax.rsqrt(variance + NORM_EPS)
    hidden = low(normed * ln_gain + ln_bias)
    projected = low_back(jnp.einsum('std,de->ste', hidden, w_qkv, precision=lax.Precision.HIGHEST) + b_qkv)
    head_shape = (SEQS, SEQ, HEADS, HEAD_DIM)
    queries = low(rotate(projected[..., :D].reshape(head_shape), cosine, sines))
    keys_rot = low(rotate(projected[..., D:2 * D].reshape(head_shape), cosine, sines))
    values_low = low(projected[..., 2 * D:].reshape(head_shape))

    def per_sequence(parts):
        return attend(parts[0], parts[1], parts[2], anchor)
    attended = lax.map(per_sequence, (queries, keys_rot, values_low))
    attended = low(low_back(attended.reshape(SEQS, SEQ, D)))
    up_value = low_back(jnp.einsum('std,de->ste', hidden, w_fc1, precision=lax.Precision.HIGHEST) + b_fc1)
    activated = low(gelu_tanh(up_value))
    attn_branch = jnp.einsum('std,de->ste', attended, w_dense, precision=lax.Precision.HIGHEST) + b_dense
    mlp_branch = jnp.einsum('stf,fe->ste', activated, w_fc2, precision=lax.Precision.HIGHEST) + b_fc2
    return inputs + attn_branch + mlp_branch

def reference(tokens, cotangent, block_order, positions, ln_gain, ln_bias, w_qkv, b_qkv, w_dense, b_dense, w_fc1, b_fc1, w_fc2, b_fc2):
    offsets = jnp.arange(BLK, dtype=jnp.int32)
    anchor = (block_order.astype(jnp.int32)[:, None] * BLK + offsets[None, :]).reshape(SEQ).astype(jnp.int32)
    cosine, sines = angles(positions)
    params = tuple((weights_in.astype(jnp.float32) for weights_in in (tokens, ln_gain, ln_bias, w_qkv, b_qkv, w_dense, b_dense, w_fc1, b_fc1, w_fc2, b_fc2)))

    def closed(*floats):
        return layer_forward(*floats, anchor, cosine, sines)
    result, pullback = jax.vjp(closed, *params)
    gradients = pullback(cotangent.astype(jnp.float32))
    return (result.astype(jnp.bfloat16), gradients[0], gradients[1], gradients[2], gradients[3], gradients[4], gradients[5], gradients[6], gradients[7], gradients[8], gradients[9], gradients[10])
```

```python
import functools

import jax
import jax.numpy as jnp
from jax import lax
from jax.experimental import pallas as pl
from jax.experimental.pallas import tpu as pltpu
from jax.sharding import PartitionSpec as P

HEAD_DIM = 64
ROTARY = 32
NORM_EPS = 1e-05
ROPE_BASE = 10000.0
GELU_COEF = 0.7978845608028654
F32 = jnp.float32
BF16 = jnp.bfloat16
STRIP = 256
NT = (((1,), (1,)), ((), ()))
TN = (((0,), (0,)), ((), ()))


def attention_kernel(
    block, where, q_in, k_in, v_in, g_in, o_out, dq_out, dk_out, dv_out,
    qs, ks, vs, gs, os, dqs, dks, dvs, score, weight,
):
    rows = q_in.shape[0]
    blocks = rows // block

    def collect(at, carry):
        src = pl.ds(pl.multiple_of(where[at] * block, block), block)
        dst = pl.ds(pl.multiple_of(at * block, block), block)
        qs[dst, :] = q_in[src, :]
        ks[dst, :] = k_in[src, :]
        vs[dst, :] = v_in[src, :]
        gs[dst, :] = g_in[src, :]
        return carry

    lax.fori_loop(0, blocks, collect, 0)
    dks[...] = jnp.zeros_like(dks)
    dvs[...] = jnp.zeros_like(dvs)
    heads = q_in.shape[1] // HEAD_DIM
    scale = HEAD_DIM ** (-0.5)
    q_pos = lax.broadcasted_iota(jnp.int32, (STRIP, STRIP), 0)
    k_pos = lax.broadcasted_iota(jnp.int32, (STRIP, STRIP), 1)
    diagonal = k_pos <= q_pos
    for strip in range(rows // STRIP):
        here = slice(strip * STRIP, (strip + 1) * STRIP)
        for head in range(heads):
            cols = slice(head * HEAD_DIM, (head + 1) * HEAD_DIM)
            query = qs[here, cols] * jnp.asarray(scale, BF16)
            grad = gs[here, cols].astype(F32)
            peak = jnp.full((STRIP, 128), -1e30, F32)
            for chunk in range(strip + 1):
                there = slice(chunk * STRIP, (chunk + 1) * STRIP)
                part = lax.dot_general(query, ks[there, cols], NT, preferred_element_type=F32)
                if chunk == strip:
                    part = jnp.where(diagonal, part, -1e30)
                score[chunk] = part
                for lane in range(0, STRIP, 128):
                    peak = jnp.maximum(peak, part[:, lane : lane + 128])
            peak = jnp.max(peak, axis=1, keepdims=True)
            mass = jnp.zeros((STRIP, 128), F32)
            mixed = jnp.zeros((STRIP, HEAD_DIM), F32)
            for chunk in range(strip + 1):
                there = slice(chunk * STRIP, (chunk + 1) * STRIP)
                part = jnp.exp(score[chunk] - peak)
                score[chunk] = part
                for lane in range(0, STRIP, 128):
                    mass = mass + part[:, lane : lane + 128]
                low = part.astype(BF16)
                weight[chunk] = low
                mixed = mixed + jnp.dot(low, vs[there, cols], preferred_element_type=F32)
            inverse = 1.0 / jnp.sum(mass, axis=1, keepdims=True)
            mixed = mixed * inverse
            os[here, cols] = mixed.astype(BF16)
            grad = (grad * inverse).astype(BF16)
            centre = jnp.sum(grad.astype(F32) * mixed, axis=1, keepdims=True)
            d_query = jnp.zeros((STRIP, HEAD_DIM), F32)
            for chunk in range(strip + 1):
                there = slice(chunk * STRIP, (chunk + 1) * STRIP)
                part = lax.dot_general(grad, vs[there, cols], NT, preferred_element_type=F32)
                d_score = (score[chunk] * (part - centre)).astype(BF16)
                d_query = d_query + jnp.dot(d_score, ks[there, cols], preferred_element_type=F32)
                dks[there, cols] += lax.dot_general(
                    d_score, query, TN, preferred_element_type=F32
                )
                dvs[there, cols] += lax.dot_general(
                    weight[chunk], grad, TN, preferred_element_type=F32
                )
            dqs[here, cols] = d_query * scale

    def spread(at, carry):
        dst = pl.ds(pl.multiple_of(where[at] * block, block), block)
        src = pl.ds(pl.multiple_of(at * block, block), block)
        o_out[dst, :] = os[src, :]
        dq_out[dst, :] = dqs[src, :]
        dk_out[dst, :] = dks[src, :]
        dv_out[dst, :] = dvs[src, :]
        return carry

    lax.fori_loop(0, blocks, spread, 0)


def attention(where, block, queries, keys, values, grads):
    rows, width = queries.shape
    vmem = pl.BlockSpec(memory_space=pltpu.VMEM)
    smem = pl.BlockSpec(memory_space=pltpu.SMEM)
    wide = jax.ShapeDtypeStruct((rows, width), F32)
    chunks = rows // STRIP
    return pl.pallas_call(
        functools.partial(attention_kernel, block),
        out_shape=(jax.ShapeDtypeStruct((rows, width), BF16), wide, wide, wide),
        in_specs=[smem, vmem, vmem, vmem, vmem],
        out_specs=(vmem, vmem, vmem, vmem),
        scratch_shapes=[pltpu.VMEM((rows, width), BF16)] * 5
        + [pltpu.VMEM((rows, width), F32)] * 3
        + [pltpu.VMEM((chunks, STRIP, STRIP), F32), pltpu.VMEM((chunks, STRIP, STRIP), BF16)],
        compiler_params=pltpu.CompilerParams(vmem_limit_bytes=48 * 1024 * 1024),
        cost_estimate=pl.CostEstimate(
            flops=6 * rows * rows * width,
            bytes_accessed=rows * width * 22,
            transcendentals=rows * rows * width // HEAD_DIM // 2,
        ),
    )(where, queries, keys, values, grads)


def gelu_tanh(values):
    return (
        0.5 * values * (1.0 + jnp.tanh(GELU_COEF * (values + 0.044715 * values * values * values)))
    )


def turn_tables(positions, width):
    half = ROTARY // 2
    frequency = ROPE_BASE ** (-(jnp.arange(half, dtype=F32) * (2.0 / ROTARY)))
    turned = positions.astype(F32)[:, None] * frequency
    cosine, sine = jnp.cos(turned), jnp.sin(turned)
    rest = jnp.zeros((positions.shape[0], HEAD_DIM - ROTARY), F32)
    none = jnp.zeros_like(sine)
    heads = width // HEAD_DIM
    same = jnp.concatenate([cosine, cosine, rest + 1.0] * heads, axis=1)
    after = jnp.concatenate([-sine, none, rest] * heads, axis=1)
    before = jnp.concatenate([none, sine, rest] * heads, axis=1)
    return same, after, before


def turn(values, tables, back):
    same, after, before = tables
    half = ROTARY // 2
    moved = jnp.roll(values, -half, axis=1) * after + jnp.roll(values, half, axis=1) * before
    return values * same - moved if back else values * same + moved


def on_device(
    tokens, cotangent, block_order, positions, ln_gain, ln_bias, w_qkv, b_qkv, w_dense, b_dense,
    w_fc1, b_fc1, w_fc2, b_fc2,
):
    ctx, fsdp = lax.axis_size("ctx"), lax.axis_size("fsdp")
    c, f = lax.axis_index("ctx"), lax.axis_index("fsdp")
    share = ctx // fsdp
    rows, width = tokens.shape[1:]
    seq = rows * ctx
    ff = w_fc1.shape[1]
    own_width, own_ff = width // ctx, ff // ctx
    own_rows = width // fsdp
    tokens = tokens.reshape(rows, width)
    cotangent = cotangent.reshape(rows, width)
    swap = [
        (cs * fsdp + fs, (share * fs + cs % share) * fsdp + cs // share)
        for cs in range(ctx)
        for fs in range(fsdp)
    ]

    small = jnp.concatenate([ln_gain, ln_bias, b_qkv, b_fc1, b_dense, b_fc2])
    small = lax.all_gather(small, "fsdp", axis=0)
    small_at, at = [], 0
    for piece in (ln_gain, ln_bias, b_qkv, b_fc1, b_dense, b_fc2):
        small_at.append(small[:, at : at + piece.shape[0]].reshape(-1).astype(F32))
        at += piece.shape[0]
    gain, shift, bias_qkv, bias_fc1, bias_dense, bias_fc2 = small_at
    in_rows = jnp.concatenate(
        [
            lax.dynamic_slice_in_dim(w_qkv, part * width + c * own_width, own_width, 1)
            for part in range(3)
        ]
        + [lax.dynamic_slice_in_dim(w_fc1, c * own_ff, own_ff, 1)],
        axis=1,
    )
    w_in = lax.all_gather(in_rows, "fsdp", axis=0, tiled=True)
    out_rows = jnp.concatenate(
        [
            lax.dynamic_slice_in_dim(w_dense, lax.rem(c, share) * own_width, own_width, 0),
            lax.dynamic_slice_in_dim(w_fc2, lax.rem(c, share) * own_ff, own_ff, 0),
        ],
        axis=0,
    )
    w_out = lax.ppermute(out_rows, ("ctx", "fsdp"), swap)
    own_bias_qkv = jnp.concatenate(
        [
            lax.dynamic_slice_in_dim(bias_qkv, part * width + c * own_width, own_width, 0)
            for part in range(3)
        ]
    )
    own_bias_fc1 = lax.dynamic_slice_in_dim(bias_fc1, c * own_ff, own_ff, 0)

    x_all = lax.all_gather(tokens, "ctx", axis=0, tiled=True)
    g_all = lax.all_gather(cotangent, "ctx", axis=0, tiled=True)
    pos_all = lax.all_gather(positions.reshape(rows), "ctx", axis=0, tiled=True)
    x_f = x_all.astype(F32)
    mean = jnp.mean(x_f, axis=1, keepdims=True)
    centred = x_f - mean
    inverse = lax.rsqrt(jnp.mean(centred * centred, axis=1, keepdims=True) + NORM_EPS)
    hidden = (centred * inverse * gain + shift).astype(BF16)

    cut = 3 * own_width
    projected = jnp.dot(hidden, w_in[:, :cut], preferred_element_type=F32) + own_bias_qkv
    up_value = jnp.dot(hidden, w_in[:, cut:], preferred_element_type=F32) + own_bias_fc1
    activated = gelu_tanh(up_value).astype(BF16)
    tables = turn_tables(pos_all, own_width)
    queries = turn(projected[:, :own_width], tables, False).astype(BF16)
    keys = turn(projected[:, own_width : 2 * own_width], tables, False).astype(BF16)
    values = projected[:, 2 * own_width :].astype(BF16)
    d_attended = lax.dot_general(g_all, w_out[:own_width], NT, preferred_element_type=F32)
    d_attended = d_attended.astype(BF16)
    d_act = lax.dot_general(g_all, w_out[own_width:], NT, preferred_element_type=F32)
    d_up = jax.vjp(gelu_tanh, up_value)[1](d_act)[0].astype(BF16)

    def scatter(term):
        return lax.psum_scatter(term.astype(BF16), "fsdp", scatter_dimension=0, tiled=True)

    def from_ctx(piece):
        return lax.all_gather(piece, "ctx", axis=0)

    def swapped(piece):
        return from_ctx(lax.ppermute(piece, ("ctx", "fsdp"), swap))

    def rows_of(pieces, amount):
        pieces = pieces.astype(F32).reshape(fsdp, share, amount // fsdp, width)
        return pieces.transpose(1, 0, 2, 3).reshape(share * amount, width)

    grad_fc1 = from_ctx(scatter(lax.dot_general(hidden, d_up, TN, preferred_element_type=F32)))
    grad_fc2 = swapped(scatter(lax.dot_general(activated, g_all, TN, preferred_element_type=F32)))

    blocks = block_order.shape[0]
    where = jnp.argsort(block_order).astype(jnp.int32)
    attended, d_query, d_key, d_value = attention(
        where, seq // blocks, queries, keys, values, d_attended
    )
    d_projected = jnp.concatenate(
        [turn(d_query, tables, True), turn(d_key, tables, True), d_value], axis=1
    ).astype(BF16)

    grad_qkv = from_ctx(
        scatter(lax.dot_general(hidden, d_projected, TN, preferred_element_type=F32))
    )
    grad_dense = swapped(scatter(lax.dot_general(attended, g_all, TN, preferred_element_type=F32)))

    branches = jnp.dot(attended, w_out[:own_width], preferred_element_type=F32) + jnp.dot(
        activated, w_out[own_width:], preferred_element_type=F32
    )
    branches = lax.psum_scatter(branches.astype(BF16), "ctx", scatter_dimension=0, tiled=True)
    x_own = tokens.astype(F32)
    result = x_own + branches.astype(F32) + bias_dense + bias_fc2

    d_hidden = lax.dot_general(
        d_projected, w_in[:, :cut], NT, preferred_element_type=F32
    ) + lax.dot_general(d_up, w_in[:, cut:], NT, preferred_element_type=F32)
    part_gain = jnp.sum(d_hidden * (centred * inverse), axis=0)
    part_shift = jnp.sum(d_hidden, axis=0)
    d_hidden = lax.psum_scatter(
        d_hidden.astype(BF16), "ctx", scatter_dimension=0, tiled=True
    ).astype(F32)
    own_mean = jnp.mean(x_own, axis=1, keepdims=True)
    own_centred = x_own - own_mean
    own_inverse = lax.rsqrt(jnp.mean(own_centred * own_centred, axis=1, keepdims=True) + NORM_EPS)
    normed = own_centred * own_inverse
    scaled = d_hidden * gain
    input_grad = cotangent.astype(F32) + own_inverse * (
        scaled
        - jnp.mean(scaled, axis=1, keepdims=True)
        - normed * jnp.mean(scaled * normed, axis=1, keepdims=True)
    )

    vector = jnp.concatenate(
        [
            part_gain,
            part_shift,
            jnp.sum(cotangent.astype(F32), axis=0),
            jnp.sum(d_projected.astype(F32), axis=0),
            jnp.sum(d_up.astype(F32), axis=0),
        ]
    )
    vector = lax.all_gather(vector, "ctx", axis=0)
    sums = jnp.sum(vector[:, : 3 * width], axis=0)
    columns = vector[:, 3 * width : 3 * width + cut].reshape(ctx, 3, own_width)
    columns = columns.transpose(1, 0, 2).reshape(3 * width)
    units = vector[:, 3 * width + cut :].reshape(ff)
    pieces = [sums[:width], sums[width : 2 * width], sums[2 * width :], columns, units]
    pieces = jnp.concatenate([piece.reshape(fsdp, -1) for piece in pieces], axis=1)
    pieces = lax.psum_scatter(pieces, "fsdp", scatter_dimension=0, tiled=True).reshape(-1)
    cuts = [own_rows, 2 * own_rows, 3 * own_rows, 3 * own_rows + 3 * width // fsdp]
    d_gain, d_shift, d_bias, d_bias_qkv, d_bias_fc1 = jnp.split(pieces, cuts)

    out_fc1 = grad_fc1.transpose(1, 0, 2).astype(F32).reshape(own_rows, ff)
    out_qkv = grad_qkv.reshape(ctx, own_rows, 3, own_width).transpose(1, 2, 0, 3)
    out_qkv = out_qkv.astype(F32).reshape(own_rows, 3 * width)
    return (
        result.astype(BF16).reshape(1, rows, width),
        input_grad.reshape(1, rows, width),
        d_gain,
        d_shift,
        out_qkv,
        d_bias_qkv,
        rows_of(grad_dense, own_width),
        d_bias,
        out_fc1,
        d_bias_fc1,
        rows_of(grad_fc2, own_ff),
        d_bias,
    )


def solution(mesh):
    split = P("fsdp", "ctx", None)
    matrix = P("fsdp", None)
    vector = P("fsdp")
    return jax.shard_map(
        on_device,
        mesh=mesh,
        in_specs=(split, split, P(), P("fsdp", "ctx"), vector, vector)
        + (matrix, vector) * 4,
        out_specs=(split, split, vector, vector) + (matrix, vector) * 4,
        check_vma=False,
    )
```

```python
import functools

import jax
import jax.numpy as jnp
from jax import lax
from jax.experimental import pallas as pl
from jax.experimental.pallas import tpu as pltpu
from jax.sharding import PartitionSpec as P

HEAD_DIM = 64
ROTARY = 32
NORM_EPS = 1e-05
ROPE_BASE = 10000.0
GELU_COEF = 0.7978845608028654
F32 = jnp.float32
BF16 = jnp.bfloat16
STRIP = 256
NT = (((1,), (1,)), ((), ()))
TN = (((0,), (0,)), ((), ()))


def attention_kernel(
    block, where, q_in, k_in, v_in, g_in, o_out, dq_out, dk_out, dv_out,
    qs, ks, vs, gs, os, dqs, dks, dvs, score, weight,
):
    rows = q_in.shape[0]
    blocks = rows // block

    def collect(at, carry):
        src = pl.ds(pl.multiple_of(where[at] * block, block), block)
        dst = pl.ds(pl.multiple_of(at * block, block), block)
        qs[dst, :] = q_in[src, :]
        ks[dst, :] = k_in[src, :]
        vs[dst, :] = v_in[src, :]
        gs[dst, :] = g_in[src, :]
        return carry

    lax.fori_loop(0, blocks, collect, 0)
    dks[...] = jnp.zeros_like(dks)
    dvs[...] = jnp.zeros_like(dvs)
    heads = q_in.shape[1] // HEAD_DIM
    scale = HEAD_DIM ** (-0.5)
    q_pos = lax.broadcasted_iota(jnp.int32, (STRIP, STRIP), 0)
    k_pos = lax.broadcasted_iota(jnp.int32, (STRIP, STRIP), 1)
    diagonal = k_pos <= q_pos
    for strip in range(rows // STRIP):
        here = slice(strip * STRIP, (strip + 1) * STRIP)
        for head in range(heads):
            cols = slice(head * HEAD_DIM, (head + 1) * HEAD_DIM)
            query = qs[here, cols] * jnp.asarray(scale, BF16)
            grad = gs[here, cols].astype(F32)
            peak = jnp.full((STRIP, 128), -1e30, F32)
            for chunk in range(strip + 1):
                there = slice(chunk * STRIP, (chunk + 1) * STRIP)
                part = lax.dot_general(query, ks[there, cols], NT, preferred_element_type=F32)
                if chunk == strip:
                    part = jnp.where(diagonal, part, -1e30)
                score[chunk] = part
                for lane in range(0, STRIP, 128):
                    peak = jnp.maximum(peak, part[:, lane : lane + 128])
            peak = jnp.max(peak, axis=1, keepdims=True)
            mass = jnp.zeros((STRIP, 128), F32)
            mixed = jnp.zeros((STRIP, HEAD_DIM), F32)
            for chunk in range(strip + 1):
                there = slice(chunk * STRIP, (chunk + 1) * STRIP)
                part = jnp.exp(score[chunk] - peak)
                score[chunk] = part
                for lane in range(0, STRIP, 128):
                    mass = mass + part[:, lane : lane + 128]
                low = part.astype(BF16)
                weight[chunk] = low
                mixed = mixed + jnp.dot(low, vs[there, cols], preferred_element_type=F32)
            inverse = 1.0 / jnp.sum(mass, axis=1, keepdims=True)
            mixed = mixed * inverse
            os[here, cols] = mixed.astype(BF16)
            grad = (grad * inverse).astype(BF16)
            centre = jnp.sum(grad.astype(F32) * mixed, axis=1, keepdims=True)
            d_query = jnp.zeros((STRIP, HEAD_DIM), F32)
            for chunk in range(strip + 1):
                there = slice(chunk * STRIP, (chunk + 1) * STRIP)
                part = lax.dot_general(grad, vs[there, cols], NT, preferred_element_type=F32)
                d_score = (score[chunk] * (part - centre)).astype(BF16)
                d_query = d_query + jnp.dot(d_score, ks[there, cols], preferred_element_type=F32)
                dks[there, cols] += lax.dot_general(
                    d_score, query, TN, preferred_element_type=F32
                )
                dvs[there, cols] += lax.dot_general(
                    weight[chunk], grad, TN, preferred_element_type=F32
                )
            dqs[here, cols] = d_query * scale

    def spread(at, carry):
        dst = pl.ds(pl.multiple_of(where[at] * block, block), block)
        src = pl.ds(pl.multiple_of(at * block, block), block)
        o_out[dst, :] = os[src, :]
        dq_out[dst, :] = dqs[src, :]
        dk_out[dst, :] = dks[src, :]
        dv_out[dst, :] = dvs[src, :]
        return carry

    lax.fori_loop(0, blocks, spread, 0)


def attention(where, block, queries, keys, values, grads):
    rows, width = queries.shape
    vmem = pl.BlockSpec(memory_space=pltpu.VMEM)
    smem = pl.BlockSpec(memory_space=pltpu.SMEM)
    wide = jax.ShapeDtypeStruct((rows, width), F32)
    chunks = rows // STRIP
    return pl.pallas_call(
        functools.partial(attention_kernel, block),
        out_shape=(jax.ShapeDtypeStruct((rows, width), BF16), wide, wide, wide),
        in_specs=[smem, vmem, vmem, vmem, vmem],
        out_specs=(vmem, vmem, vmem, vmem),
        scratch_shapes=[pltpu.VMEM((rows, width), BF16)] * 5
        + [pltpu.VMEM((rows, width), F32)] * 3
        + [pltpu.VMEM((chunks, STRIP, STRIP), F32), pltpu.VMEM((chunks, STRIP, STRIP), BF16)],
        compiler_params=pltpu.CompilerParams(vmem_limit_bytes=48 * 1024 * 1024),
        cost_estimate=pl.CostEstimate(
            flops=6 * rows * rows * width,
            bytes_accessed=rows * width * 22,
            transcendentals=rows * rows * width // HEAD_DIM // 2,
        ),
    )(where, queries, keys, values, grads)


MESH = pl.DeviceIdType.MESH


class Place:
    def __init__(self):
        self.c, self.f = lax.axis_index("ctx"), lax.axis_index("fsdp")
        self.y, self.z, self.core = self.c // 4, (self.c // 2) % 2, self.c % 2
        self.x, self.half = self.f // 2, self.f % 2

    def block(self, dy, flip, other=False):
        core = 1 - self.core if other else self.core
        return ((self.y + dy) % 4) * 4 + (1 - self.z if flip else self.z) * 2 + core

    def shard(self, dx, flip):
        return ((self.x + dx) % 4) * 2 + (1 - self.half if flip else self.half)

    def to_ctx(self, dy, flip, other=False):
        return (self.block(dy, flip, other), self.f)

    def to_fsdp(self, dx, flip):
        return (self.c, self.shard(dx, flip))

    def to_swap(self):
        return (2 * self.f + self.c % 2, self.c // 2)


class Post:
    def __init__(self, place, send, recv):
        self.place, self.send, self.recv, self.started = place, send, recv, []

    def copy(self, source, target, device):
        at = len(self.started)
        copy = pltpu.make_async_remote_copy(
            src_ref=source, dst_ref=target, send_sem=self.send.at[at], recv_sem=self.recv.at[at],
            device_id=device, device_id_type=MESH,
        )
        self.started.append(copy)
        copy.start()
        return copy

    def greet(self):
        place = self.place
        barrier = pltpu.get_barrier_semaphore()
        partners = [
            place.to_ctx(1, False), place.to_ctx(-1, False), place.to_ctx(0, True),
            place.to_ctx(0, False, True), place.to_fsdp(1, False), place.to_fsdp(-1, False),
            place.to_fsdp(0, True),
        ]
        for partner in partners:
            pl.semaphore_signal(barrier, inc=1, device_id=partner, device_id_type=MESH)
        swap = place.to_swap()
        same = jnp.logical_and(swap[0] == place.c, swap[1] == place.f)

        @pl.when(jnp.logical_not(same))
        def _():
            pl.semaphore_signal(barrier, inc=1, device_id=swap, device_id_type=MESH)

        pl.semaphore_wait(barrier, len(partners) + jnp.where(same, 0, 1))

    def close(self):
        for copy in self.started:
            copy.wait_send()


def gather_ctx(post, own, buf, cut):
    place = post.place
    here = post.place.block(0, False)
    crossed = []

    def send(at, *to):
        return post.copy(buf.at[at], buf.at[at], place.to_ctx(*to))

    def cross(at):
        crossed.append(post.copy(buf.at[at], buf.at[at], place.to_ctx(0, False, True)))

    def first(*to):
        return post.copy(own, buf.at[here], place.to_ctx(*to))

    to_pair = first(0, True)
    to_next, to_last = first(1, False), first(-1, False)
    crossed.append(first(0, False, True))
    yield
    to_pair.wait_recv()
    pair = place.block(0, True)
    pair_next, pair_last = send(pair, 1, False), send(pair, -1, False)
    cross(pair)
    yield
    to_next.wait_recv()
    last = place.block(-1, False)
    low = post.copy(
        buf.at[last, pl.ds(0, cut)], buf.at[last, pl.ds(0, cut)], place.to_ctx(1, False)
    )
    cross(last)
    to_last.wait_recv()
    after = place.block(1, False)
    rest = buf.shape[1] - cut
    high = post.copy(
        buf.at[after, pl.ds(cut, rest)], buf.at[after, pl.ds(cut, rest)], place.to_ctx(-1, False)
    )
    cross(after)
    yield
    low.wait_recv()
    high.wait_recv()
    far = place.block(2, False)
    pair_far = send(far, 0, True)
    cross(far)
    yield
    pair_next.wait_recv()
    cross(place.block(-1, True))
    pair_last.wait_recv()
    cross(place.block(1, True))
    yield
    pair_far.wait_recv()
    cross(place.block(2, True))
    yield
    for copy in crossed:
        copy.wait_recv()


def gather_fsdp(post, own, buf, cut):
    place = post.place
    here = place.shard(0, False)
    rest = buf.shape[1] - cut

    def whole(at, dx):
        return post.copy(buf.at[at], buf.at[at], place.to_fsdp(dx, False))

    def lower(at):
        piece = buf.at[at, pl.ds(0, cut)]
        return post.copy(piece, piece, place.to_fsdp(1, False))

    def upper(at):
        piece = buf.at[at, pl.ds(cut, rest)]
        return post.copy(piece, piece, place.to_fsdp(-1, False))

    to_pair = post.copy(own, buf.at[here], place.to_fsdp(0, True))
    to_next = post.copy(own, buf.at[here], place.to_fsdp(1, False))
    to_last = post.copy(own, buf.at[here], place.to_fsdp(-1, False))
    yield
    to_next.wait_recv()
    low = lower(place.shard(-1, False))
    to_last.wait_recv()
    high = upper(place.shard(1, False))
    yield
    to_pair.wait_recv()
    pair = place.shard(0, True)
    pair_next, pair_last = whole(pair, 1), whole(pair, -1)
    yield
    pair_next.wait_recv()
    pair_low = lower(place.shard(-1, True))
    pair_last.wait_recv()
    pair_high = upper(place.shard(1, True))
    yield
    for copy in (low, high, pair_low, pair_high):
        copy.wait_recv()


def add_into(target, *parts):
    step = 16
    rows = target.shape[0]

    def body(at, carry):
        take = pl.ds(pl.multiple_of(at * step, step), step)
        total = parts[0][take, :].astype(F32)
        for part in parts[1:]:
            total = total + part[take, :].astype(F32)
        target[take, :] = total.astype(target.dtype)
        return carry

    lax.fori_loop(0, rows // step, body, 0)


def reduce_ctx(post, part, core, pair_in, half_in, ring_in, cross_in, last_in, total):
    place = post.place
    order = [(2, True), (1, True), (-1, True), (2, False), (1, False), (-1, False), (0, True), (0, False)]
    crossed = [
        post.copy(part.at[place.block(*to, True)], core.at[at], place.to_ctx(0, False, True))
        for at, to in enumerate(order)
    ]
    cut = half_in.shape[1]

    def own(at):
        crossed[at].wait_recv()
        return part.at[place.block(*order[at])]

    yield
    add_into(core.at[0], own(0), core.at[0])
    far = post.copy(core.at[0], pair_in, place.to_ctx(0, True))
    add_into(core.at[1], own(1), core.at[1])
    cross_next = post.copy(core.at[1], cross_in.at[0], place.to_ctx(1, False))
    add_into(core.at[2], own(2), core.at[2])
    cross_last = post.copy(core.at[2], cross_in.at[1], place.to_ctx(-1, False))
    for at in (3, 4, 5, 6):
        add_into(core.at[at], own(at), core.at[at])
    yield
    far.wait_recv()
    add_into(core.at[3], core.at[3], pair_in)
    low = post.copy(core.at[3, pl.ds(0, cut)], half_in.at[0], place.to_ctx(1, False))
    high = post.copy(core.at[3, pl.ds(cut, cut)], half_in.at[1], place.to_ctx(-1, False))
    yield
    cross_next.wait_recv()
    cross_last.wait_recv()
    add_into(core.at[6], core.at[6], cross_in.at[0], cross_in.at[1])
    last = post.copy(core.at[6], last_in, place.to_ctx(0, True))
    yield
    low.wait_recv()
    add_into(core.at[4, pl.ds(0, cut)], core.at[4, pl.ds(0, cut)], half_in.at[0])
    ring_next = post.copy(core.at[4], ring_in.at[0], place.to_ctx(1, False))
    high.wait_recv()
    add_into(core.at[5, pl.ds(cut, cut)], core.at[5, pl.ds(cut, cut)], half_in.at[1])
    ring_last = post.copy(core.at[5], ring_in.at[1], place.to_ctx(-1, False))
    yield
    last.wait_recv()
    ring_next.wait_recv()
    ring_last.wait_recv()
    add_into(total, own(7), core.at[7], ring_in.at[0], ring_in.at[1], last_in)


def reduce_fsdp(post, part, hold, low_in, high_in, ring_in, pair_in, total):
    place = post.place
    cut, rest = low_in.shape[1], high_in.shape[1]
    lower, upper = pl.ds(0, cut), pl.ds(cut, rest)
    halves = []
    for side, flip in enumerate((True, False)):
        far = place.shard(2, flip)
        low = post.copy(part.at[far, lower], low_in.at[side], place.to_fsdp(1, False))
        high = post.copy(part.at[far, upper], high_in.at[side], place.to_fsdp(-1, False))
        halves.append((low, high))
    yield
    rings = []
    for side, flip in enumerate((True, False)):
        low, high = halves[side]
        after, before = place.shard(1, flip), place.shard(-1, flip)
        low.wait_recv()
        add_into(hold.at[side, lower], part.at[after, lower], low_in.at[side])
        add_into(hold.at[side, upper], part.at[after, upper])
        to_next = post.copy(hold.at[side], ring_in.at[side, 0], place.to_fsdp(1, False))
        high.wait_recv()
        add_into(hold.at[2 + side, lower], part.at[before, lower])
        add_into(hold.at[2 + side, upper], part.at[before, upper], high_in.at[side])
        to_last = post.copy(hold.at[2 + side], ring_in.at[side, 1], place.to_fsdp(-1, False))
        rings.append((to_next, to_last))
        yield
    for copy in rings[0]:
        copy.wait_recv()
    add_into(hold.at[4], part.at[place.shard(0, True)], ring_in.at[0, 0], ring_in.at[0, 1])
    across = post.copy(hold.at[4], pair_in, place.to_fsdp(0, True))
    yield
    for copy in rings[1]:
        copy.wait_recv()
    across.wait_recv()
    add_into(total, part.at[place.shard(0, False)], ring_in.at[1, 0], ring_in.at[1, 1], pair_in)


def run(*flows):
    flows = list(flows)
    while flows:
        flows = [flow for flow in flows if next(flow, flows) is not flows]


class Swap:
    def __init__(self, place, source, target, send, recv, local):
        device = place.to_swap()
        self.same = jnp.logical_and(device[0] == place.c, device[1] == place.f)
        self.away = pltpu.make_async_remote_copy(
            src_ref=source, dst_ref=target, send_sem=send, recv_sem=recv, device_id=device,
            device_id_type=MESH,
        )
        self.stay = pltpu.make_async_copy(source, target, local)
        pl.when(jnp.logical_not(self.same))(lambda: self.away.start())
        pl.when(self.same)(lambda: self.stay.start())

    def wait(self):
        pl.when(jnp.logical_not(self.same))(lambda: self.away.wait())
        pl.when(self.same)(lambda: self.stay.wait())


def gather_kernel(
    x_in, g_in, pos_in, in_rows, out_rows, small_in,
    x_all, g_all, pos_all, w_in, w_out, small_all,
    piece, send, recv, local, swap_send, swap_recv,
):
    place = Place()
    post = Post(place, send, recv)
    post.greet()
    swap = Swap(place, out_rows, piece, swap_send, swap_recv, local.at[6])
    here, shard = place.block(0, False), place.shard(0, False)
    keeps = []
    for own, buf, at in (
        (x_in, x_all, here), (g_in, g_all, here), (pos_in, pos_all, here), (in_rows, w_in, shard),
        (small_in, small_all, shard),
    ):
        keeps.append(pltpu.make_async_copy(own, buf.at[at], local.at[len(keeps)]))
        keeps[-1].start()
    x_flow = gather_ctx(post, x_in, x_all, x_in.shape[0] // 2)
    in_flow = gather_fsdp(post, in_rows, w_in, in_rows.shape[0] // 2)
    next(x_flow)
    next(in_flow)
    pos_flow = gather_ctx(post, pos_in, pos_all, 8)
    next(pos_flow)
    small_flow = gather_fsdp(post, small_in, small_all, 16)
    next(small_flow)
    next(x_flow)
    swap.wait()
    out_flow = gather_fsdp(post, piece, w_out, 48)
    next(out_flow)
    keeps.append(pltpu.make_async_copy(piece, w_out.at[shard], local.at[5]))
    keeps[-1].start()
    next(x_flow)
    next(in_flow)
    g_flow = gather_ctx(post, g_in, g_all, g_in.shape[0] // 2)
    run(x_flow, in_flow, g_flow, out_flow, pos_flow, small_flow)
    for keep in keeps:
        keep.wait()
    post.close()


def gather(tokens, cotangent, positions, in_rows, out_rows, small, ctx, fsdp):
    many = 3 * 16 + 3 * 9
    shapes = [
        jax.ShapeDtypeStruct((count,) + array.shape, array.dtype)
        for count, array in (
            (ctx, tokens), (ctx, cotangent), (ctx, positions), (fsdp, in_rows), (fsdp, out_rows),
            (fsdp, small),
        )
    ]
    whole = pl.BlockSpec(memory_space=pl.ANY)
    return pl.pallas_call(
        gather_kernel,
        out_shape=tuple(shapes),
        in_specs=[whole] * 6,
        out_specs=(whole,) * 6,
        scratch_shapes=[
            pltpu.VMEM(out_rows.shape, out_rows.dtype),
            pltpu.SemaphoreType.DMA((many,)),
            pltpu.SemaphoreType.DMA((many,)),
            pltpu.SemaphoreType.DMA((7,)),
            pltpu.SemaphoreType.DMA,
            pltpu.SemaphoreType.DMA,
        ],
        compiler_params=pltpu.CompilerParams(
            collective_id=0, has_side_effects=True, vmem_limit_bytes=16 * 1024 * 1024
        ),
        name="gather",
    )(tokens, cotangent, positions, in_rows, out_rows, small)


def reduce_kernel(
    out_part, hid_part, in_grad, out_grad, vector_in,
    out_total, hid_total, in_all, out_all, vector_all,
    core_a, pair_a, half_a, ring_a, cross_a, last_a,
    core_b, pair_b, half_b, ring_b, cross_b, last_b,
    in_hold, in_low, in_high, in_ring, in_pair, in_sum,
    out_hold, out_low, out_high, out_ring, out_pair, out_sum, out_piece,
    vector_shards, vector_sum,
    send, recv, local, swap_send, swap_recv,
):
    place = Place()
    post = Post(place, send, recv)
    post.greet()
    here, shard = place.block(0, False), place.shard(0, False)
    keeps = []

    def keep(source, target):
        keeps.append(pltpu.make_async_copy(source, target, local.at[len(keeps)]))
        keeps[-1].start()

    def in_flow():
        yield from reduce_fsdp(post, in_grad, in_hold, in_low, in_high, in_ring, in_pair, in_sum)
        keep(in_sum, in_all.at[here])
        yield from gather_ctx(post, in_sum, in_all, in_sum.shape[0] // 2)

    def out_flow():
        yield from reduce_fsdp(
            post, out_grad, out_hold, out_low, out_high, out_ring, out_pair, out_sum
        )
        swap = Swap(place, out_sum, out_piece, swap_send, swap_recv, local.at[4])
        yield
        swap.wait()
        keep(out_piece, out_all.at[here])
        yield from gather_ctx(post, out_piece, out_all, 48)

    def vector_flow():
        keep(vector_in, vector_shards.at[shard])
        mine = keeps[-1]
        yield from gather_fsdp(post, vector_in, vector_shards, 8)
        mine.wait()
        total = vector_shards[0]
        for at in range(1, vector_shards.shape[0]):
            total = total + vector_shards[at]
        vector_sum[...] = total
        keep(vector_sum, vector_all.at[here])
        yield from gather_ctx(post, vector_sum, vector_all, 8)

    run(
        in_flow(),
        out_flow(),
        reduce_ctx(post, out_part, core_a, pair_a, half_a, ring_a, cross_a, last_a, out_total),
        reduce_ctx(post, hid_part, core_b, pair_b, half_b, ring_b, cross_b, last_b, hid_total),
        vector_flow(),
    )
    for at, kept in enumerate(keeps):
        if at != 0:
            kept.wait()
    post.close()


def reduce(out_part, hid_part, in_grad, out_grad, vector):
    ctx, rows, width = out_part.shape
    whole, vmem = pl.BlockSpec(memory_space=pl.ANY), pl.BlockSpec(memory_space=pltpu.VMEM)

    def low(*shape):
        return pltpu.VMEM(shape, BF16)

    def ctx_scratch():
        return [
            low(ctx // 2, rows, width), low(rows, width), low(2, rows // 2, width),
            low(2, rows, width), low(2, rows, width), low(rows, width),
        ]

    def fsdp_scratch(part, cut):
        depth, columns = part.shape[1:]
        return [
            low(5, depth, columns), low(2, cut, columns), low(2, depth - cut, columns),
            low(2, 2, depth, columns), low(depth, columns), low(depth, columns),
        ]

    many = 2 * 16 + 2 * 9 + 2 * 16 + 9 + 16
    total = jax.ShapeDtypeStruct((rows, width), F32)
    return pl.pallas_call(
        reduce_kernel,
        out_shape=(
            total,
            total,
            jax.ShapeDtypeStruct((ctx,) + in_grad.shape[1:], BF16),
            jax.ShapeDtypeStruct((ctx,) + out_grad.shape[1:], BF16),
            jax.ShapeDtypeStruct((ctx,) + vector.shape, F32),
        ),
        in_specs=[vmem] * 5,
        out_specs=(vmem, vmem, whole, whole, whole),
        scratch_shapes=ctx_scratch()
        + ctx_scratch()
        + fsdp_scratch(in_grad, in_grad.shape[1] // 2)
        + fsdp_scratch(out_grad, 48)
        + [
            low(*out_grad.shape[1:]),
            pltpu.VMEM((in_grad.shape[0],) + vector.shape, F32),
            pltpu.VMEM(vector.shape, F32),
            pltpu.SemaphoreType.DMA((many,)),
            pltpu.SemaphoreType.DMA((many,)),
            pltpu.SemaphoreType.DMA((5,)),
            pltpu.SemaphoreType.DMA,
            pltpu.SemaphoreType.DMA,
        ],
        compiler_params=pltpu.CompilerParams(
            collective_id=1, has_side_effects=True, vmem_limit_bytes=60 * 1024 * 1024
        ),
        name="reduce",
    )(out_part, hid_part, in_grad, out_grad, vector)


def gelu_tanh(values):
    return (
        0.5 * values * (1.0 + jnp.tanh(GELU_COEF * (values + 0.044715 * values * values * values)))
    )


def turn_tables(positions, width):
    half = ROTARY // 2
    frequency = ROPE_BASE ** (-(jnp.arange(half, dtype=F32) * (2.0 / ROTARY)))
    turned = positions.astype(F32)[:, None] * frequency
    cosine, sine = jnp.cos(turned), jnp.sin(turned)
    rest = jnp.zeros((positions.shape[0], HEAD_DIM - ROTARY), F32)
    none = jnp.zeros_like(sine)
    heads = width // HEAD_DIM
    same = jnp.concatenate([cosine, cosine, rest + 1.0] * heads, axis=1)
    after = jnp.concatenate([-sine, none, rest] * heads, axis=1)
    before = jnp.concatenate([none, sine, rest] * heads, axis=1)
    return same, after, before


def turn(values, tables, back):
    same, after, before = tables
    half = ROTARY // 2
    moved = jnp.roll(values, -half, axis=1) * after + jnp.roll(values, half, axis=1) * before
    return values * same - moved if back else values * same + moved


def on_device(
    tokens, cotangent, block_order, positions, ln_gain, ln_bias, w_qkv, b_qkv, w_dense, b_dense,
    w_fc1, b_fc1, w_fc2, b_fc2,
):
    ctx, fsdp = lax.axis_size("ctx"), lax.axis_size("fsdp")
    c = lax.axis_index("ctx")
    share = ctx // fsdp
    rows, width = tokens.shape[1:]
    seq = rows * ctx
    ff = w_fc1.shape[1]
    own_width, own_ff = width // ctx, ff // ctx
    own_rows = width // fsdp
    tokens = tokens.reshape(rows, width)
    cotangent = cotangent.reshape(rows, width)

    vectors = (ln_gain, ln_bias, b_dense, b_fc2, b_qkv, b_fc1)
    small = jnp.concatenate([vector.reshape(-1, own_rows) for vector in vectors])
    small = jnp.pad(small, ((0, 32 - small.shape[0]), (0, 0)))
    in_rows = jnp.concatenate(
        [
            lax.dynamic_slice_in_dim(w_qkv, part * width + c * own_width, own_width, 1)
            for part in range(3)
        ]
        + [lax.dynamic_slice_in_dim(w_fc1, c * own_ff, own_ff, 1)],
        axis=1,
    )

    def own_piece(weight, amount):
        step = amount // fsdp
        return lax.dynamic_slice_in_dim(weight, (c % share) * amount + (c // share) * step, step, 0)

    out_rows = jnp.concatenate([own_piece(w_dense, own_width), own_piece(w_fc2, own_ff)])
    dense_step, fc2_step = own_width // fsdp, own_ff // fsdp
    pos_rows = jnp.broadcast_to(positions.reshape(1, rows), (16, rows))
    x_all, g_all, pos_all, w_in, w_out, small_all = gather(
        tokens, cotangent, pos_rows, in_rows, out_rows, small, ctx, fsdp
    )
    x_all, g_all = x_all.reshape(seq, width), g_all.reshape(seq, width)
    w_in = w_in.reshape(width, -1)
    w_out = jnp.concatenate(
        [
            w_out[:, :dense_step].reshape(own_width, width),
            w_out[:, dense_step:].reshape(own_ff, width),
        ]
    )
    small_at, at = [], 0
    for vector in vectors:
        count = vector.shape[0] // own_rows
        small_at.append(small_all[:, at : at + count].reshape(-1).astype(F32))
        at += count
    gain, shift, bias_dense, bias_fc2, bias_qkv, bias_fc1 = small_at
    own_bias = jnp.concatenate(
        [
            lax.dynamic_slice_in_dim(bias_qkv, part * width + c * own_width, own_width, 0)
            for part in range(3)
        ]
        + [lax.dynamic_slice_in_dim(bias_fc1, c * own_ff, own_ff, 0)]
    )

    x_f = x_all.astype(F32)
    mean = jnp.mean(x_f, axis=1, keepdims=True)
    centred = x_f - mean
    inverse = lax.rsqrt(jnp.mean(centred * centred, axis=1, keepdims=True) + NORM_EPS)
    hidden = (centred * inverse * gain + shift).astype(BF16)

    cut = 3 * own_width
    projected = jnp.dot(hidden, w_in[:, :cut], preferred_element_type=F32) + own_bias[:cut]
    up_value = jnp.dot(hidden, w_in[:, cut:], preferred_element_type=F32) + own_bias[cut:]
    activated = gelu_tanh(up_value).astype(BF16)
    tables = turn_tables(pos_all[:, 0].reshape(seq), own_width)
    queries = turn(projected[:, :own_width], tables, False).astype(BF16)
    keys = turn(projected[:, own_width : 2 * own_width], tables, False).astype(BF16)
    values = projected[:, 2 * own_width :].astype(BF16)
    d_attended = lax.dot_general(g_all, w_out[:own_width], NT, preferred_element_type=F32)
    d_attended = d_attended.astype(BF16)
    d_act = lax.dot_general(g_all, w_out[own_width:], NT, preferred_element_type=F32)
    d_up = jax.vjp(gelu_tanh, up_value)[1](d_act)[0].astype(BF16)

    blocks = block_order.shape[0]
    where = jnp.argsort(block_order).astype(jnp.int32)
    attended, d_query, d_key, d_value = attention(
        where, seq // blocks, queries, keys, values, d_attended
    )
    d_projected = jnp.concatenate(
        [turn(d_query, tables, True), turn(d_key, tables, True), d_value], axis=1
    ).astype(BF16)

    inner = jnp.concatenate([d_projected, d_up], axis=1)
    outer = jnp.concatenate([attended, activated], axis=1)
    grad_in = lax.dot_general(hidden, inner, TN, preferred_element_type=F32).astype(BF16)
    grad_out = lax.dot_general(outer, g_all, TN, preferred_element_type=F32).astype(BF16)
    grad_out = jnp.concatenate(
        [
            grad_out[:own_width].reshape(fsdp, dense_step, width),
            grad_out[own_width:].reshape(fsdp, fc2_step, width),
        ],
        axis=1,
    )
    branches = jnp.dot(outer, w_out, preferred_element_type=F32).astype(BF16)
    d_hidden = lax.dot_general(inner, w_in, NT, preferred_element_type=F32)
    part_gain = jnp.sum(d_hidden * (centred * inverse), axis=0)
    part_shift = jnp.sum(d_hidden, axis=0)
    columns = jnp.sum(inner.astype(F32), axis=0)
    vector = jnp.concatenate(
        [
            part_gain,
            part_shift,
            jnp.sum(cotangent.astype(F32), axis=0),
            columns,
            jnp.zeros((16 * 1024 - 3 * width - columns.shape[0],), F32),
        ]
    ).reshape(16, 1024)
    branches, d_hidden, in_all, out_all, vector_all = reduce(
        branches.reshape(ctx, rows, width),
        d_hidden.astype(BF16).reshape(ctx, rows, width),
        grad_in.reshape(fsdp, own_rows, -1),
        grad_out,
        vector,
    )

    x_own = tokens.astype(F32)
    result = x_own + branches + bias_dense + bias_fc2
    own_mean = jnp.mean(x_own, axis=1, keepdims=True)
    own_centred = x_own - own_mean
    own_inverse = lax.rsqrt(jnp.mean(own_centred * own_centred, axis=1, keepdims=True) + NORM_EPS)
    normed = own_centred * own_inverse
    scaled = d_hidden * gain
    input_grad = cotangent.astype(F32) + own_inverse * (
        scaled
        - jnp.mean(scaled, axis=1, keepdims=True)
        - normed * jnp.mean(scaled * normed, axis=1, keepdims=True)
    )

    f = lax.axis_index("fsdp")
    vector_all = vector_all.reshape(ctx, -1)
    sums = jnp.sum(vector_all[:, : 3 * width], axis=0).reshape(3, width)
    sums = lax.dynamic_slice_in_dim(sums, f * own_rows, own_rows, 1)
    columns = vector_all[:, 3 * width : 3 * width + cut].reshape(ctx, 3, own_width)
    columns = columns.transpose(1, 0, 2).reshape(3 * width)
    units = vector_all[:, 3 * width + cut : 3 * width + cut + own_ff].reshape(ff)
    d_bias_qkv = lax.dynamic_slice_in_dim(columns, f * (3 * own_rows), 3 * own_rows, 0)
    d_bias_fc1 = lax.dynamic_slice_in_dim(units, f * (ff // fsdp), ff // fsdp, 0)

    def rows_of(pieces, amount):
        pieces = pieces.astype(F32).reshape(fsdp, share, amount // fsdp, width)
        return pieces.transpose(1, 0, 2, 3).reshape(share * amount, width)

    out_fc1 = in_all[:, :, cut:].transpose(1, 0, 2).astype(F32).reshape(own_rows, ff)
    out_qkv = in_all[:, :, :cut].reshape(ctx, own_rows, 3, own_width).transpose(1, 2, 0, 3)
    out_qkv = out_qkv.astype(F32).reshape(own_rows, 3 * width)
    return (
        result.astype(BF16).reshape(1, rows, width),
        input_grad.reshape(1, rows, width),
        sums[0],
        sums[1],
        out_qkv,
        d_bias_qkv,
        rows_of(out_all[:, :dense_step], own_width),
        sums[2],
        out_fc1,
        d_bias_fc1,
        rows_of(out_all[:, dense_step:], own_ff),
        sums[2],
    )


def solution(mesh):
    split = P("fsdp", "ctx", None)
    matrix = P("fsdp", None)
    vector = P("fsdp")
    return jax.shard_map(
        on_device,
        mesh=mesh,
        in_specs=(split, split, P(), P("fsdp", "ctx"), vector, vector)
        + (matrix, vector) * 4,
        out_specs=(split, split, vector, vector) + (matrix, vector) * 4,
        check_vma=False,
    )
```

```python
import functools

import jax
import jax.numpy as jnp
import numpy as np
from jax import lax
from jax.experimental import pallas as pl
from jax.experimental.pallas import tpu as pltpu
from jax.sharding import PartitionSpec as P

HEAD_DIM = 64
ROTARY = 32
NORM_EPS = 1e-05
ROPE_BASE = 10000.0
GELU_COEF = 0.7978845608028654
F32 = jnp.float32
BF16 = jnp.bfloat16
STRIP = 256
NT = (((1,), (1,)), ((), ()))
TN = (((0,), (0,)), ((), ()))
MESH = pl.DeviceIdType.MESH
MIB = 1024 * 1024


def nt_dot(left, right):
    return lax.dot_general(left, right, NT, preferred_element_type=F32)


def tn_dot(left, right):
    return lax.dot_general(left, right, TN, preferred_element_type=F32)


def dot(left, right):
    return jnp.dot(left, right, preferred_element_type=F32)


def turn_rows(positions, width):
    half = ROTARY // 2
    frequency = ROPE_BASE ** (-(jnp.arange(half, dtype=F32) * (2.0 / ROTARY)))
    turned = positions.astype(F32)[:, None] * frequency
    both = jnp.concatenate([jnp.cos(turned), jnp.sin(turned)], axis=1)
    coarse = both.astype(BF16)
    fine = (both - coarse.astype(F32)).astype(BF16)
    rows = positions.shape[0]
    used = 4 * half + 1
    return jnp.concatenate(
        [coarse, fine, jnp.ones((rows, 1), BF16), jnp.zeros((rows, width - used), BF16)], axis=1
    )


def turn_spread(width):
    half = ROTARY // 2
    table = np.zeros((width, 3 * width), np.float32)
    for column in range(width):
        at = column % HEAD_DIM
        if at >= ROTARY:
            table[4 * half, column] = 1.0
            continue
        for part in (0, 2 * half):
            table[part + at % half, column] = 1.0
            if at < half:
                table[part + half + at, width + column] = -1.0
            else:
                table[part + half + at - half, 2 * width + column] = 1.0
    return jnp.asarray(table, BF16)


def turn(values, tables, back):
    width = values.shape[1]
    half = ROTARY // 2
    same, after, before = (tables[:, at * width : (at + 1) * width] for at in range(3))
    moved = pltpu.roll(values, width - half, 1) * after + pltpu.roll(values, half, 1) * before
    return values * same - moved if back else values * same + moved


class Place:
    def __init__(self):
        self.c, self.f = lax.axis_index("ctx"), lax.axis_index("fsdp")
        self.y, self.z, self.core = self.c // 4, (self.c // 2) % 2, self.c % 2
        self.x, self.half = self.f // 2, self.f % 2

    def block(self, dy, flip, other=False):
        core = 1 - self.core if other else self.core
        return ((self.y + dy) % 4) * 4 + (1 - self.z if flip else self.z) * 2 + core

    def shard(self, dx, flip):
        return ((self.x + dx) % 4) * 2 + (1 - self.half if flip else self.half)

    def to_ctx(self, dy, flip, other=False):
        return (self.block(dy, flip, other), self.f)

    def to_fsdp(self, dx, flip):
        return (self.c, self.shard(dx, flip))

    def to_swap(self):
        return (2 * self.f + self.c % 2, self.c // 2)


class Post:
    def __init__(self, place, send, recv):
        self.place, self.send, self.recv, self.started = place, send, recv, []
        self.left = set()

    def copy(self, source, target, device):
        at = len(self.started)
        copy = pltpu.make_async_remote_copy(
            src_ref=source, dst_ref=target, send_sem=self.send.at[at], recv_sem=self.recv.at[at],
            device_id=device, device_id_type=MESH,
        )
        self.started.append(copy)
        copy.start()
        return copy

    def greet(self):
        place = self.place
        barrier = pltpu.get_barrier_semaphore()
        partners = [
            place.to_ctx(1, False), place.to_ctx(-1, False), place.to_ctx(0, True),
            place.to_ctx(0, False, True), place.to_fsdp(1, False), place.to_fsdp(-1, False),
            place.to_fsdp(0, True),
        ]
        for partner in partners:
            pl.semaphore_signal(barrier, inc=1, device_id=partner, device_id_type=MESH)
        swap = place.to_swap()
        same = jnp.logical_and(swap[0] == place.c, swap[1] == place.f)

        @pl.when(jnp.logical_not(same))
        def _():
            pl.semaphore_signal(barrier, inc=1, device_id=swap, device_id_type=MESH)

        pl.semaphore_wait(barrier, len(partners) + jnp.where(same, 0, 1))

    def has_left(self, copy):
        copy.wait_send()
        self.left.add(id(copy))

    def close(self):
        for copy in self.started:
            if id(copy) not in self.left:
                copy.wait_send()


def gather_ctx(post, own, buf, cut):
    place = post.place
    here = post.place.block(0, False)
    crossed = []

    def send(at, *to):
        return post.copy(buf.at[at], buf.at[at], place.to_ctx(*to))

    def cross(at):
        crossed.append(post.copy(buf.at[at], buf.at[at], place.to_ctx(0, False, True)))

    def first(*to):
        return post.copy(own, buf.at[here], place.to_ctx(*to))

    to_pair = first(0, True)
    to_next, to_last = first(1, False), first(-1, False)
    crossed.append(first(0, False, True))
    yield
    to_pair.wait_recv()
    pair = place.block(0, True)
    pair_next, pair_last = send(pair, 1, False), send(pair, -1, False)
    cross(pair)
    yield
    to_next.wait_recv()
    last = place.block(-1, False)
    low = post.copy(
        buf.at[last, pl.ds(0, cut)], buf.at[last, pl.ds(0, cut)], place.to_ctx(1, False)
    )
    cross(last)
    to_last.wait_recv()
    after = place.block(1, False)
    rest = buf.shape[1] - cut
    high = post.copy(
        buf.at[after, pl.ds(cut, rest)], buf.at[after, pl.ds(cut, rest)], place.to_ctx(-1, False)
    )
    cross(after)
    yield
    low.wait_recv()
    high.wait_recv()
    far = place.block(2, False)
    pair_far = send(far, 0, True)
    cross(far)
    yield
    pair_next.wait_recv()
    cross(place.block(-1, True))
    pair_last.wait_recv()
    cross(place.block(1, True))
    yield
    pair_far.wait_recv()
    cross(place.block(2, True))
    yield
    for copy in crossed:
        copy.wait_recv()


def gather_fsdp(post, own, buf, cut):
    place = post.place
    here = place.shard(0, False)
    rest = buf.shape[1] - cut

    def whole(at, dx):
        return post.copy(buf.at[at], buf.at[at], place.to_fsdp(dx, False))

    def lower(at):
        piece = buf.at[at, pl.ds(0, cut)]
        return post.copy(piece, piece, place.to_fsdp(1, False))

    def upper(at):
        piece = buf.at[at, pl.ds(cut, rest)]
        return post.copy(piece, piece, place.to_fsdp(-1, False))

    to_pair = post.copy(own, buf.at[here], place.to_fsdp(0, True))
    to_next = post.copy(own, buf.at[here], place.to_fsdp(1, False))
    to_last = post.copy(own, buf.at[here], place.to_fsdp(-1, False))
    yield
    to_next.wait_recv()
    low = lower(place.shard(-1, False))
    to_last.wait_recv()
    high = upper(place.shard(1, False))
    yield
    to_pair.wait_recv()
    pair = place.shard(0, True)
    pair_next, pair_last = whole(pair, 1), whole(pair, -1)
    yield
    pair_next.wait_recv()
    pair_low = lower(place.shard(-1, True))
    pair_last.wait_recv()
    pair_high = upper(place.shard(1, True))
    yield
    for copy in (low, high, pair_low, pair_high):
        copy.wait_recv()


class Swap:
    def __init__(self, place, source, target, send, recv, local):
        device = place.to_swap()
        self.same = jnp.logical_and(device[0] == place.c, device[1] == place.f)
        self.away = pltpu.make_async_remote_copy(
            src_ref=source, dst_ref=target, send_sem=send, recv_sem=recv, device_id=device,
            device_id_type=MESH,
        )
        self.stay = pltpu.make_async_copy(source, target, local)
        pl.when(jnp.logical_not(self.same))(lambda: self.away.start())
        pl.when(self.same)(lambda: self.stay.start())

    def wait(self):
        pl.when(jnp.logical_not(self.same))(lambda: self.away.wait())
        pl.when(self.same)(lambda: self.stay.wait())


def first_kernel(
    x_in, g_in, turn_in, in_rows, out_rows, small_in, spread,
    x_out, g_out, hid_out, stat, q_out, k_out, v_out, d_att, act, d_up, w_in_out, w_out, turn_out,
    small_out,
    x_all, g_all, hidden, turns, w_in, pieces, piece, small_all, tables, proj, slope, vec, bias,
    send, recv, local, swap_send, swap_recv,
):
    place = Place()
    post = Post(place, send, recv)
    post.greet()
    swap = Swap(place, out_rows, piece, swap_send, swap_recv, local.at[0])
    rows, width = x_in.shape
    own_width = q_out.shape[1]
    cut = 3 * own_width
    here, shard = place.block(0, False), place.shard(0, False)
    keeps = []

    def keep(source, target):
        copy = pltpu.make_async_copy(source, target, local.at[1 + len(keeps)])
        keeps.append(copy)
        copy.start()
        return copy

    own = [
        keep(x_in, x_all.at[here]), keep(in_rows, w_in.at[shard]), keep(turn_in, turns.at[here]),
        keep(small_in, small_all.at[shard]), keep(g_in, g_all.at[here]),
    ]
    x_flow = gather_ctx(post, x_in, x_all, rows // 2)
    in_flow = gather_fsdp(post, in_rows, w_in, in_rows.shape[0] // 2)
    small_flow = gather_fsdp(post, small_in, small_all, 16)
    turn_flow = gather_ctx(post, turn_in, turns, rows // 2)
    next(x_flow)
    next(small_flow)
    next(in_flow)
    next(turn_flow)
    next(x_flow)
    swap.wait()
    keep(piece, pieces.at[shard])
    out_flow = gather_fsdp(post, piece, pieces, 48)
    next(out_flow)
    next(x_flow)
    next(in_flow)
    for _ in small_flow:
        pass
    for copy in own[:4]:
        copy.wait()

    side = small_all.shape[2]
    small_out[...] = small_all[...].astype(F32)
    for at in range(small_all.shape[0]):
        vec[0:2, at * side : (at + 1) * side] = small_out[at, 0:2, :]
    for part in range(3):
        first = part * width + place.c * own_width
        count = 3 * side
        row = small_out[first // count, pl.ds(4 + (first % count) // side, 1), :]
        bias[0:1, part * own_width : (part + 1) * own_width] = jnp.where(
            first % side == 0, row[:, :own_width], row[:, own_width:]
        )
    for part in range(2):
        row = small_out[place.c // 2, pl.ds(7 + 2 * (place.c % 2) + part, 1), :]
        bias[0:1, cut + part * side : cut + (part + 1) * side] = row

    def normalise(block):
        step = 32
        lane = lax.broadcasted_iota(jnp.int32, (step, stat.shape[1]), 1)

        def body(at, carry):
            source = pl.ds(pl.multiple_of(at * step, step), step)
            target = pl.ds(pl.multiple_of(block * rows + at * step, step), step)
            value = x_all[block, source, :].astype(F32)
            mean = jnp.mean(value, axis=1, keepdims=True)
            centred = value - mean
            inverse = lax.rsqrt(jnp.mean(centred * centred, axis=1, keepdims=True) + NORM_EPS)
            hidden[target, :] = (centred * inverse * vec[0:1, :] + vec[1:2, :]).astype(BF16)
            stat[target, :] = jnp.where(lane < HEAD_DIM, mean, inverse)
            return carry

        lax.fori_loop(0, rows // step, body, 0)

    near = [(0, False), (0, True), (1, False), (-1, False)]
    far = [(2, False), (1, True), (-1, True), (2, True)]
    next(x_flow)
    next(in_flow)
    g_flow = gather_ctx(post, g_in, g_all, rows // 2)
    next(g_flow)
    for to in near:
        normalise(place.block(*to))
    next(x_flow)
    next(in_flow)
    next(x_flow)
    for to in far[:2]:
        normalise(place.block(*to))
    next(g_flow)
    for to in far[2:]:
        normalise(place.block(*to))
    next(out_flow)
    for _ in x_flow:
        pass
    keep(x_all, x_out)
    lax.fori_loop(
        0, x_all.shape[0] // 2, lambda at, carry: normalise(2 * at + 1 - place.core) or carry, 0
    )
    keep(hidden, hid_out)
    for _ in in_flow:
        pass
    next(g_flow)
    next(out_flow)
    for _ in turn_flow:
        pass
    keep(w_in, w_in_out)
    keep(turns, turn_out)

    chunk_rows = proj.shape[0]
    step = 64
    group = chunk_rows // rows

    def project(chunk, carry):
        take = pl.ds(pl.multiple_of(chunk * chunk_rows, chunk_rows), chunk_rows)
        weight = w_in[...].reshape(width, proj.shape[1])
        proj[...] = dot(hidden[take, :], weight)
        turned = turns[pl.ds(chunk * group, group)].reshape(chunk_rows, own_width)
        tables[...] = dot(turned, spread[...])

        def body(at, inner):
            source = pl.ds(pl.multiple_of(at * step, step), step)
            target = pl.ds(pl.multiple_of(chunk * chunk_rows + at * step, step), step)
            value = proj[source, :] + bias[0:1, :]
            table = tables[source, :]
            q_out[target, :] = turn(value[:, :own_width], table, False).astype(BF16)
            k_out[target, :] = turn(value[:, own_width : 2 * own_width], table, False).astype(BF16)
            v_out[target, :] = value[:, 2 * own_width : cut].astype(BF16)
            up = value[:, cut:]
            square = up * up
            curve = jnp.tanh(GELU_COEF * up * (1.0 + 0.044715 * square))
            act[target, :] = (0.5 * up * (1.0 + curve)).astype(BF16)
            slope[target, :] = 0.5 * (1.0 + curve) + 0.5 * up * (1.0 - curve * curve) * (
                GELU_COEF * (1.0 + 3.0 * 0.044715 * square)
            )
            return inner

        lax.fori_loop(0, chunk_rows // step, body, 0)
        return carry

    chunks = hidden.shape[0] // chunk_rows
    lax.fori_loop(0, chunks // 2, project, 0)
    next(g_flow)
    next(out_flow)
    next(g_flow)
    lax.fori_loop(chunks // 2, chunks, project, 0)
    next(g_flow)
    for _ in out_flow:
        pass
    keeps[5].wait()
    dense_step = own_width // pieces.shape[0]
    fc2_step = pieces.shape[1] - dense_step
    for at in range(pieces.shape[0]):
        w_out[at * dense_step : (at + 1) * dense_step, :] = pieces[at, :dense_step, :]
        first = own_width + at * fc2_step
        w_out[first : first + fc2_step, :] = pieces[at, dense_step:, :]
    for _ in g_flow:
        pass
    own[4].wait()
    keep(g_all, g_out)

    def back(chunk, carry):
        grads = g_all[pl.ds(chunk * group, group)].reshape(chunk_rows, width)
        proj[:, : w_out.shape[0]] = nt_dot(grads, w_out[...])

        def body(at, inner):
            source = pl.ds(pl.multiple_of(at * step, step), step)
            target = pl.ds(pl.multiple_of(chunk * chunk_rows + at * step, step), step)
            d_att[target, :] = proj[source, :own_width].astype(BF16)
            d_act = proj[source, own_width : w_out.shape[0]]
            d_up[target, :] = (d_act * slope[target, :]).astype(BF16)
            return inner

        lax.fori_loop(0, chunk_rows // step, body, 0)
        return carry

    lax.fori_loop(0, chunks, back, 0)
    for copy in keeps[6:]:
        copy.wait()
    post.close()


def first(tokens, cotangent, turns, in_rows, out_rows, small, spread, ctx, fsdp):
    rows, width = tokens.shape
    seq = ctx * rows
    own_width = turns.shape[1]
    columns = in_rows.shape[1]
    own_ff = columns - 3 * own_width
    out_total = fsdp * out_rows.shape[0]
    many = 3 * 16 + 3 * 9
    any_, vmem = pl.BlockSpec(memory_space=pl.ANY), pl.BlockSpec(memory_space=pltpu.VMEM)

    def low(*shape):
        return jax.ShapeDtypeStruct(shape, BF16)

    outs = [
        (low(ctx, rows, width), any_), (low(ctx, rows, width), any_), (low(seq, width), any_),
        (jax.ShapeDtypeStruct((seq, 128), F32), vmem),
        (low(seq, own_width), vmem), (low(seq, own_width), vmem), (low(seq, own_width), vmem),
        (low(seq, own_width), vmem), (low(seq, own_ff), vmem), (low(seq, own_ff), vmem),
        (low(fsdp, in_rows.shape[0], columns), any_), (low(out_total, width), vmem),
        (low(ctx, rows, own_width), any_),
        (jax.ShapeDtypeStruct((fsdp,) + small.shape, F32), vmem),
    ]
    chunk_rows = 4 * rows
    return pl.pallas_call(
        first_kernel,
        out_shape=tuple(out[0] for out in outs),
        in_specs=[any_] * 6 + [vmem],
        out_specs=tuple(out[1] for out in outs),
        scratch_shapes=[
            pltpu.VMEM((ctx, rows, width), BF16),
            pltpu.VMEM((ctx, rows, width), BF16),
            pltpu.VMEM((seq, width), BF16),
            pltpu.VMEM((ctx, rows, own_width), BF16),
            pltpu.VMEM((fsdp,) + in_rows.shape, BF16),
            pltpu.VMEM((fsdp,) + out_rows.shape, BF16),
            pltpu.VMEM(out_rows.shape, BF16),
            pltpu.VMEM((fsdp,) + small.shape, BF16),
            pltpu.VMEM((chunk_rows, 3 * own_width), F32),
            pltpu.VMEM((chunk_rows, columns), F32),
            pltpu.VMEM((seq, own_ff), F32),
            pltpu.VMEM((8, width), F32),
            pltpu.VMEM((8, columns), F32),
            pltpu.SemaphoreType.DMA((many,)),
            pltpu.SemaphoreType.DMA((many,)),
            pltpu.SemaphoreType.DMA((12,)),
            pltpu.SemaphoreType.DMA,
            pltpu.SemaphoreType.DMA,
        ],
        compiler_params=pltpu.CompilerParams(
            collective_id=0, has_side_effects=True, vmem_limit_bytes=60 * MIB
        ),
        name="first",
    )(tokens, cotangent, turns, in_rows, out_rows, small, spread)


def attention_kernel(
    block, order, where, q_in, k_in, v_in, g_in, turns, spread, o_out, d_out,
    qs, ks, vs, gs, os, dqs, dks, dvs, score, weight,
):
    rows, width = q_in.shape
    blocks = rows // block

    def collect(at, carry):
        src = pl.ds(pl.multiple_of(where[at] * block, block), block)
        dst = pl.ds(pl.multiple_of(at * block, block), block)
        qs[dst, :] = q_in[src, :]
        ks[dst, :] = k_in[src, :]
        vs[dst, :] = v_in[src, :]
        gs[dst, :] = g_in[src, :]
        return carry

    lax.fori_loop(0, blocks, collect, 0)
    dks[...] = jnp.zeros_like(dks)
    dvs[...] = jnp.zeros_like(dvs)
    heads = width // HEAD_DIM
    scale = HEAD_DIM ** (-0.5)
    q_pos = lax.broadcasted_iota(jnp.int32, (STRIP, STRIP), 0)
    k_pos = lax.broadcasted_iota(jnp.int32, (STRIP, STRIP), 1)
    diagonal = k_pos <= q_pos
    for strip in range(rows // STRIP):
        here = slice(strip * STRIP, (strip + 1) * STRIP)
        for head in range(heads):
            cols = slice(head * HEAD_DIM, (head + 1) * HEAD_DIM)
            query = qs[here, cols] * jnp.asarray(scale, BF16)
            grad = gs[here, cols].astype(F32)
            peak = jnp.full((STRIP, 128), -1e30, F32)
            for chunk in range(strip + 1):
                there = slice(chunk * STRIP, (chunk + 1) * STRIP)
                part = nt_dot(query, ks[there, cols])
                if chunk == strip:
                    part = jnp.where(diagonal, part, -1e30)
                score[chunk] = part
                for lane in range(0, STRIP, 128):
                    peak = jnp.maximum(peak, part[:, lane : lane + 128])
            peak = jnp.max(peak, axis=1, keepdims=True)
            mass = jnp.zeros((STRIP, 128), F32)
            mixed = jnp.zeros((STRIP, HEAD_DIM), F32)
            for chunk in range(strip + 1):
                there = slice(chunk * STRIP, (chunk + 1) * STRIP)
                part = jnp.exp(score[chunk] - peak)
                score[chunk] = part
                for lane in range(0, STRIP, 128):
                    mass = mass + part[:, lane : lane + 128]
                low = part.astype(BF16)
                weight[chunk] = low
                mixed = mixed + dot(low, vs[there, cols])
            inverse = 1.0 / jnp.sum(mass, axis=1, keepdims=True)
            mixed = mixed * inverse
            os[here, cols] = mixed.astype(BF16)
            grad = (grad * inverse).astype(BF16)
            centre = jnp.sum(grad.astype(F32) * mixed, axis=1, keepdims=True)
            d_query = jnp.zeros((STRIP, HEAD_DIM), F32)
            for chunk in range(strip + 1):
                there = slice(chunk * STRIP, (chunk + 1) * STRIP)
                part = nt_dot(grad, vs[there, cols])
                d_score = (score[chunk] * (part - centre)).astype(BF16)
                d_query = d_query + dot(d_score, ks[there, cols])
                dks[there, cols] += tn_dot(d_score, query)
                dvs[there, cols] += tn_dot(weight[chunk], grad)
            dqs[here, cols] = d_query * scale

    def give(at, carry):
        src = pl.ds(pl.multiple_of(order[at] * block, block), block)
        dst = pl.ds(pl.multiple_of(at * block, block), block)
        tables = dot(turns[dst, :], spread[...])
        o_out[dst, :] = os[src, :]
        d_out[dst, :width] = turn(dqs[src, :], tables, True).astype(BF16)
        d_out[dst, width : 2 * width] = turn(dks[src, :], tables, True).astype(BF16)
        d_out[dst, 2 * width :] = dvs[src, :].astype(BF16)
        return carry

    lax.fori_loop(0, blocks, give, 0)


def attention(order, where, block, queries, keys, values, grads, turns, spread):
    rows, width = queries.shape
    vmem = pl.BlockSpec(memory_space=pltpu.VMEM)
    smem = pl.BlockSpec(memory_space=pltpu.SMEM)
    chunks = rows // STRIP
    return pl.pallas_call(
        functools.partial(attention_kernel, block),
        out_shape=(
            jax.ShapeDtypeStruct((rows, width), BF16),
            jax.ShapeDtypeStruct((rows, 3 * width), BF16),
        ),
        in_specs=[smem, smem] + [vmem] * 6,
        out_specs=(vmem, vmem),
        scratch_shapes=[pltpu.VMEM((rows, width), BF16)] * 5
        + [pltpu.VMEM((rows, width), F32)] * 3
        + [pltpu.VMEM((chunks, STRIP, STRIP), F32), pltpu.VMEM((chunks, STRIP, STRIP), BF16)],
        compiler_params=pltpu.CompilerParams(vmem_limit_bytes=48 * MIB),
        cost_estimate=pl.CostEstimate(
            flops=6 * rows * rows * width,
            bytes_accessed=rows * width * 22,
            transcendentals=rows * rows * width // HEAD_DIM // 2,
        ),
        name="attention",
    )(order, where, queries, keys, values, grads, turns, spread)


ORDER = [(2, True), (1, True), (-1, True), (2, False), (0, True), (1, False), (-1, False), (0, False)]
SHARDS = [(2, True), (2, False), (1, True), (-1, True), (1, False), (-1, False), (0, True), (0, False)]


def add_into(target, *parts):
    step = 16

    def body(at, carry):
        take = pl.ds(pl.multiple_of(at * step, step), step)
        total = parts[0][take, :].astype(F32)
        for part in parts[1:]:
            total = total + part[take, :].astype(F32)
        target[take, :] = total.astype(target.dtype)
        return carry

    lax.fori_loop(0, target.shape[0] // step, body, 0)


def reduce_ctx(post, own, core, crossed, pair_in, half_in, ring_in, cross_in, last_in, total):
    place = post.place
    cut = half_in.shape[1]
    up, down, pair = place.to_ctx(1, False), place.to_ctx(-1, False), place.to_ctx(0, True)

    def meet(at, *more):
        crossed[at].wait_recv()
        add_into(core.at[at], own.at[at], core.at[at], *more)

    meet(0)
    far = post.copy(core.at[0], pair_in, pair)
    yield
    meet(1)
    cross_next = post.copy(core.at[1], cross_in.at[0], up)
    meet(2)
    cross_last = post.copy(core.at[2], cross_in.at[1], down)
    yield
    far.wait_recv()
    meet(3, pair_in)
    low = post.copy(core.at[3, pl.ds(0, cut)], half_in.at[0], up)
    high = post.copy(core.at[3, pl.ds(cut, cut)], half_in.at[1], down)
    yield
    cross_next.wait_recv()
    cross_last.wait_recv()
    meet(4, cross_in.at[0], cross_in.at[1])
    last = post.copy(core.at[4], last_in, pair)
    yield
    meet(5)
    low.wait_recv()
    lower = core.at[5, pl.ds(0, cut)]
    add_into(lower, lower, half_in.at[0])
    ring_next = post.copy(core.at[5], ring_in.at[0], up)
    meet(6)
    high.wait_recv()
    upper = core.at[6, pl.ds(cut, cut)]
    add_into(upper, upper, half_in.at[1])
    ring_last = post.copy(core.at[6], ring_in.at[1], down)
    yield
    crossed[7].wait_recv()
    last.wait_recv()
    ring_next.wait_recv()
    ring_last.wait_recv()
    add_into(total, own.at[7], core.at[7], ring_in.at[0], ring_in.at[1], last_in)


def reduce_fsdp(post, part, low_in, high_in, ring_in, pair_in, total):
    place = post.place
    cut, rest = low_in.shape[1], high_in.shape[1]
    lower, upper = pl.ds(0, cut), pl.ds(cut, rest)
    up, down, pair = place.to_fsdp(1, False), place.to_fsdp(-1, False), place.to_fsdp(0, True)
    halves = [
        (
            post.copy(part.at[side, lower], low_in.at[side], up),
            post.copy(part.at[side, upper], high_in.at[side], down),
        )
        for side in range(2)
    ]
    yield
    rings = []
    for side in range(2):
        low, high = halves[side]
        after, before = part.at[2 + 2 * side], part.at[3 + 2 * side]
        low.wait_recv()
        add_into(after.at[lower], after.at[lower], low_in.at[side])
        to_next = post.copy(after, ring_in.at[side, 0], up)
        high.wait_recv()
        add_into(before.at[upper], before.at[upper], high_in.at[side])
        to_last = post.copy(before, ring_in.at[side, 1], down)
        rings.append((to_next, to_last))
        yield
    for copy in rings[0]:
        copy.wait_recv()
    add_into(part.at[6], part.at[6], ring_in.at[0, 0], ring_in.at[0, 1])
    across = post.copy(part.at[6], pair_in, pair)
    yield
    for copy in rings[1]:
        copy.wait_recv()
    across.wait_recv()
    add_into(total, part.at[7], ring_in.at[1, 0], ring_in.at[1, 1], pair_in)


def run(*flows):
    flows = list(flows)
    while flows:
        flows = [flow for flow in flows if next(flow, flows) is not flows]


def second_kernel(
    att, act, d_proj, d_up, w_in, w_out, stat, small, x_own, g_own, x_all, g_all, hidden,
    result, input_grad, in_all, out_all, vector_all,
    own_a, own_b, core_a, core_b, slot_a, slot_b,
    pair_a, half_a, ring_a, cross_a, last_a, pair_b, half_b, ring_b, cross_b, last_b,
    in_part, in_low, in_high, in_ring, in_pair, in_sum,
    out_part, out_low, out_high, out_ring, out_pair, out_sum, out_piece,
    column, x_block, total_a, total_b, vec, gain_sum, shift_sum,
    vector, vector_shards, vector_sum,
    send, recv, local, loads, swap_send, swap_recv,
):
    place = Place()
    post = Post(place, send, recv)
    post.greet()
    rows, width = x_own.shape
    own_width = att.shape[1]
    cut = d_proj.shape[1]
    side = small.shape[2]
    here, shard = place.block(0, False), place.shard(0, False)
    keeps, numbers = [], iter(range(4))

    def keep(source, target):
        copy = pltpu.make_async_copy(source, target, local.at[next(numbers)])
        keeps.append(copy)
        copy.start()
        return copy

    for at in range(small.shape[0]):
        vec[0:4, at * side : (at + 1) * side] = small[at, 0:4, :]
    gain_sum[...] = jnp.zeros_like(gain_sum)
    shift_sum[...] = jnp.zeros_like(shift_sum)

    def load_x(at):
        dy, flip = ORDER[at]
        block = place.block(dy, flip) // 2
        copy = pltpu.make_async_copy(
            x_all.at[pl.ds(2 * block, 2)], x_block.at[at % 2], loads.at[at % 2]
        )
        copy.start()
        return copy

    def load_hidden(at):
        first = pl.multiple_of(place.shard(*SHARDS[at]) * side, side)
        copy = pltpu.make_async_copy(
            hidden.at[:, pl.ds(first, side)], column.at[at % 2], loads.at[2 + at % 2]
        )
        copy.start()
        return copy

    def load_grads(at):
        copy = pltpu.make_async_copy(
            g_all.at[:, pl.ds(at * side, side)], column.at[at % 2], loads.at[4 + at % 2]
        )
        copy.start()
        return copy

    pending_x = [load_x(0)]
    pending_column = [load_hidden(0)]
    crossed_a, crossed_b, slots = {}, {}, {}
    partner = place.to_ctx(0, False, True)
    depth = slot_a.shape[0]

    def produce(at):
        dy, flip = ORDER[at]
        block = place.block(dy, flip) // 2
        pending_x.pop().wait()
        if at + 1 < len(ORDER):
            pending_x.append(load_x(at + 1))
        slot = at % depth
        if at >= depth:
            for copy in slots[at - depth]:
                post.has_left(copy)
        other_rows = pl.ds(pl.multiple_of(block * (2 * rows) + (1 - place.core) * rows, rows), rows)
        own_rows = pl.ds(pl.multiple_of(block * (2 * rows) + place.core * rows, rows), rows)

        def both(ref):
            return jnp.concatenate([ref[other_rows, :], ref[own_rows, :]], axis=0)

        left, right = both(att), both(act)
        span = width // 2
        for first in range(0, width, span):
            take = slice(first, first + span)
            value = dot(left, w_out[:own_width, take]) + dot(right, w_out[own_width:, take])
            slot_a[slot, :, take] = value[:rows].astype(BF16)
            own_a[at, :, take] = value[rows:].astype(BF16)
        left, right, stats = both(d_proj), both(d_up), both(stat)
        mean, inverse = stats[:, 0:1], stats[:, HEAD_DIM : HEAD_DIM + 1]
        span = width // 4
        for first in range(0, width, span):
            take = slice(first, first + span)
            value = nt_dot(left, w_in[take, :cut]) + nt_dot(right, w_in[take, cut:])
            slot_b[slot, :, take] = value[:rows].astype(BF16)
            own_b[at, :, take] = value[rows:].astype(BF16)
            tokens = jnp.concatenate(
                [x_block[at % 2, 1 - place.core, :, take], x_block[at % 2, place.core, :, take]],
                axis=0,
            )
            normed = (tokens.astype(F32) - mean) * inverse
            parts = (2 * rows // 8, 8, span)
            gain_sum[:, take] += jnp.sum((value * normed).reshape(parts), axis=0)
            shift_sum[:, take] += jnp.sum(value.reshape(parts), axis=0)
        crossed_a[at] = post.copy(slot_a.at[slot], core_a.at[at], partner)
        crossed_b[at] = post.copy(slot_b.at[slot], core_b.at[at], partner)
        slots[at] = (crossed_a[at], crossed_b[at])

    def grad_in(at):
        pending_column.pop().wait()
        pending_column.append(load_hidden(at + 1) if at + 1 < len(SHARDS) else load_grads(0))
        rows_of = column[at % 2]
        in_part[at, :, :cut] = tn_dot(rows_of, d_proj[...]).astype(BF16)
        in_part[at, :, cut:] = tn_dot(rows_of, d_up[...]).astype(BF16)

    def grad_out(at):
        pending_column.pop().wait()
        if at + 1 < width // side:
            pending_column.append(load_grads(at + 1))
        columns = column[at % 2]
        take = slice(at * side, (at + 1) * side)
        dense = tn_dot(att[...], columns).astype(BF16)
        fc2 = tn_dot(act[...], columns).astype(BF16)
        dense_step, fc2_step = dense.shape[0] // len(SHARDS), fc2.shape[0] // len(SHARDS)
        for to in range(len(SHARDS)):
            out_part[to, :dense_step, take] = dense[to * dense_step : (to + 1) * dense_step]
            out_part[to, dense_step:, take] = fc2[to * fc2_step : (to + 1) * fc2_step]

    class ByShard:
        @property
        def at(self):
            return self

        def __getitem__(self, index):
            if isinstance(index, tuple):
                return out_part.at[(place.shard(*SHARDS[index[0]]),) + index[1:]]
            return out_part.at[place.shard(*SHARDS[index])]

    def in_flow():
        yield from reduce_fsdp(post, in_part, in_low, in_high, in_ring, in_pair, in_sum)
        keep(in_sum, in_all.at[here])
        yield from gather_ctx(post, in_sum, in_all, in_sum.shape[0] // 2)

    def out_flow():
        yield from reduce_fsdp(post, ByShard(), out_low, out_high, out_ring, out_pair, out_sum)
        swap = Swap(place, out_sum, out_piece, swap_send, swap_recv, local.at[4])
        yield
        swap.wait()
        keep(out_piece, out_all.at[here])
        yield from gather_ctx(post, out_piece, out_all, 48)

    def vector_flow():
        mine = keep(vector, vector_shards.at[shard])
        yield from gather_fsdp(post, vector, vector_shards, 8)
        mine.wait()
        keeps[:] = [kept for kept in keeps if kept is not mine]
        total = vector_shards[0]
        for at in range(1, vector_shards.shape[0]):
            total = total + vector_shards[at]
        vector_sum[...] = total
        keep(vector_sum, vector_all.at[here])
        yield from gather_ctx(post, vector_sum, vector_all, 8)

    ins, outs = in_flow(), out_flow()
    a = reduce_ctx(
        post, own_a, core_a, crossed_a, pair_a, half_a, ring_a, cross_a, last_a, total_a
    )
    b = reduce_ctx(
        post, own_b, core_b, crossed_b, pair_b, half_b, ring_b, cross_b, last_b, total_b
    )
    grad_in(0)
    grad_in(1)
    next(ins)
    produce(0)
    next(a)
    next(b)
    produce(1)
    produce(2)
    next(a)
    next(b)
    grad_in(2)
    grad_in(3)
    produce(3)
    next(ins)
    next(a)
    next(b)
    produce(4)
    grad_in(4)
    grad_in(5)
    next(a)
    next(b)
    next(ins)
    produce(5)
    produce(6)
    next(a)
    next(b)
    grad_in(6)
    grad_in(7)
    next(ins)
    for at in range(width // side):
        grad_out(at)
        if at == 3:
            next(ins)
    next(outs)
    produce(7)

    half = vector.shape[1]
    ones = jnp.ones((16, att.shape[0]), BF16)
    columns = jnp.concatenate([dot(ones, d_proj[...])[:1], dot(ones, d_up[...])[:1]], axis=1)
    vector[...] = jnp.zeros_like(vector)
    sums = [
        jnp.sum(gain_sum[...], axis=0, keepdims=True),
        jnp.sum(shift_sum[...], axis=0, keepdims=True),
        dot(ones[:, :rows], g_own[...])[:1],
    ]
    for at, row in enumerate(sums):
        vector[2 * at : 2 * at + 1, :] = row[:, :half]
        vector[2 * at + 1 : 2 * at + 2, :] = row[:, half:]
    vector[6:7, : columns.shape[1]] = columns
    vectors = vector_flow()
    next(vectors)
    run(ins, outs, a, b, vectors)

    def finish(at, carry):
        step = 16
        take = pl.ds(pl.multiple_of(at * step, step), step)
        stats = stat[pl.ds(pl.multiple_of(here * rows + at * step, step), step), :]
        mean, inverse = stats[:, 0:1], stats[:, HEAD_DIM : HEAD_DIM + 1]
        token = x_own[take, :].astype(F32)
        result[take, :] = (token + total_a[take, :] + vec[2:3, :] + vec[3:4, :]).astype(BF16)
        normed = (token - mean) * inverse
        scaled = total_b[take, :] * vec[0:1, :]
        input_grad[take, :] = g_own[take, :].astype(F32) + inverse * (
            scaled
            - jnp.mean(scaled, axis=1, keepdims=True)
            - normed * jnp.mean(scaled * normed, axis=1, keepdims=True)
        )
        return carry

    lax.fori_loop(0, rows // 16, finish, 0)
    for kept in keeps:
        kept.wait()
    post.close()


def second(att, act, d_proj, d_up, w_in, w_out, stat, small, tokens, cotangent, x_all, g_all, hidden, fsdp):
    rows, width = tokens.shape
    ctx = x_all.shape[0]
    side = width // fsdp
    in_columns, out_rows = w_in.shape[1], w_out.shape[0] // fsdp
    any_, vmem = pl.BlockSpec(memory_space=pl.ANY), pl.BlockSpec(memory_space=pltpu.VMEM)

    def low(*shape):
        return pltpu.VMEM(shape, BF16)

    def wide(*shape):
        return pltpu.VMEM(shape, F32)

    def ctx_slots():
        return [
            low(rows, width), low(2, rows // 2, width), low(2, rows, width), low(2, rows, width),
            low(rows, width),
        ]

    def fsdp_slots(depth, columns, cut):
        return [
            low(fsdp, depth, columns), low(2, cut, columns), low(2, depth - cut, columns),
            low(2, 2, depth, columns), low(depth, columns), low(depth, columns),
        ]

    vector = (16, width // 2)
    many = 2 * 16 + 2 * 9 + 2 * 16 + 9 + 16
    return pl.pallas_call(
        second_kernel,
        out_shape=(
            jax.ShapeDtypeStruct((rows, width), BF16),
            jax.ShapeDtypeStruct((rows, width), F32),
            jax.ShapeDtypeStruct((ctx, side, in_columns), BF16),
            jax.ShapeDtypeStruct((ctx, out_rows, width), BF16),
            jax.ShapeDtypeStruct((ctx,) + vector, F32),
        ),
        in_specs=[vmem] * 10 + [any_] * 3,
        out_specs=(vmem, vmem, any_, any_, any_),
        scratch_shapes=[low(ctx // 2, rows, width)] * 4
        + [low(2, rows, width)] * 2
        + ctx_slots()
        + ctx_slots()
        + fsdp_slots(side, in_columns, side // 2)
        + fsdp_slots(out_rows, width, 48)
        + [low(out_rows, width)]
        + [
            low(2, ctx * rows, side), low(2, 2, rows, width), wide(rows, width), wide(rows, width),
            wide(8, width), wide(8, width), wide(8, width),
            wide(*vector), wide(fsdp, *vector), wide(*vector),
            pltpu.SemaphoreType.DMA((many,)),
            pltpu.SemaphoreType.DMA((many,)),
            pltpu.SemaphoreType.DMA((5,)),
            pltpu.SemaphoreType.DMA((6,)),
            pltpu.SemaphoreType.DMA,
            pltpu.SemaphoreType.DMA,
        ],
        compiler_params=pltpu.CompilerParams(
            collective_id=1, has_side_effects=True, vmem_limit_bytes=63 * MIB
        ),
        name="second",
    )(att, act, d_proj, d_up, w_in, w_out, stat, small, tokens, cotangent, x_all,
      g_all.reshape(ctx * rows, width), hidden)


def widen_kernel(in_all, out_all, qkv, fc1, dense, fc2, in_low, out_low, in_wide, out_wide, loads, stores):
    count = in_all.shape[0]
    fsdp = count // 2
    slots = in_low.shape[0]
    own = qkv.shape[1] // 3 // count
    units = fc1.shape[1] // count
    dense_step, fc2_step = dense.shape[0] // count, fc2.shape[0] // count

    def load(at):
        slot = at % slots
        copies = [
            pltpu.make_async_copy(in_all.at[at], in_low.at[slot], loads.at[slot, 0]),
            pltpu.make_async_copy(out_all.at[at], out_low.at[slot], loads.at[slot, 1]),
        ]
        for copy in copies:
            copy.start()
        return copies

    ahead = [load(at) for at in range(slots - 1)]
    stored = []
    for at in range(count):
        slot = at % slots
        for copy in ahead[at]:
            copy.wait()
        if at + slots - 1 < count:
            ahead.append(load(at + slots - 1))
        if at >= slots:
            for copy in stored[at - slots]:
                copy.wait()
        add_into(in_wide.at[slot], in_low.at[slot])
        add_into(out_wide.at[slot], out_low.at[slot])
        shard, part = at // 2, at % 2
        targets = [
            (in_wide.at[slot, :, pl.ds(0, own)], qkv.at[:, pl.ds(at * own, own)]),
            (in_wide.at[slot, :, pl.ds(own, own)], qkv.at[:, pl.ds((count + at) * own, own)]),
            (in_wide.at[slot, :, pl.ds(2 * own, own)], qkv.at[:, pl.ds((2 * count + at) * own, own)]),
            (in_wide.at[slot, :, pl.ds(3 * own, units)], fc1.at[:, pl.ds(at * units, units)]),
            (
                out_wide.at[slot, pl.ds(0, dense_step)],
                dense.at[pl.ds((part * fsdp + shard) * dense_step, dense_step)],
            ),
            (
                out_wide.at[slot, pl.ds(dense_step, fc2_step)],
                fc2.at[pl.ds((part * fsdp + shard) * fc2_step, fc2_step)],
            ),
        ]
        copies = [
            pltpu.make_async_copy(source, target, stores.at[slot, number])
            for number, (source, target) in enumerate(targets)
        ]
        for copy in copies:
            copy.start()
        stored.append(copies)
    for copies in stored[-slots:]:
        for copy in copies:
            copy.wait()


def widen(in_all, out_all, width, ff, fsdp):
    any_ = pl.BlockSpec(memory_space=pl.ANY)
    slots = 4
    side = width // fsdp
    shapes = [(side, 3 * width), (side, ff), (side, width), (ff // fsdp, width)]
    return pl.pallas_call(
        widen_kernel,
        out_shape=tuple(jax.ShapeDtypeStruct(shape, F32) for shape in shapes),
        in_specs=[any_] * 2,
        out_specs=(any_,) * 4,
        scratch_shapes=[
            pltpu.VMEM((slots,) + in_all.shape[1:], BF16),
            pltpu.VMEM((slots,) + out_all.shape[1:], BF16),
            pltpu.VMEM((slots,) + in_all.shape[1:], F32),
            pltpu.VMEM((slots,) + out_all.shape[1:], F32),
            pltpu.SemaphoreType.DMA((slots, 2)),
            pltpu.SemaphoreType.DMA((slots, 6)),
        ],
        compiler_params=pltpu.CompilerParams(vmem_limit_bytes=32 * MIB),
        name="widen",
    )(in_all, out_all)


def on_device(
    tokens, cotangent, block_order, positions, ln_gain, ln_bias, w_qkv, b_qkv, w_dense, b_dense,
    w_fc1, b_fc1, w_fc2, b_fc2,
):
    ctx, fsdp = lax.axis_size("ctx"), lax.axis_size("fsdp")
    c, f = lax.axis_index("ctx"), lax.axis_index("fsdp")
    share = ctx // fsdp
    rows, width = tokens.shape[1:]
    seq = rows * ctx
    ff = w_fc1.shape[1]
    own_width, own_ff = width // ctx, ff // ctx
    own_rows = width // fsdp
    cut = 3 * own_width
    tokens = tokens.reshape(rows, width)
    cotangent = cotangent.reshape(rows, width)

    vectors = (ln_gain, ln_bias, b_dense, b_fc2, b_qkv, b_fc1)
    small = jnp.concatenate([vector.reshape(-1, own_rows) for vector in vectors])
    small = jnp.pad(small, ((0, 32 - small.shape[0]), (0, 0)))
    in_rows = jnp.concatenate(
        [
            lax.dynamic_slice_in_dim(w_qkv, part * width + c * own_width, own_width, 1)
            for part in range(3)
        ]
        + [lax.dynamic_slice_in_dim(w_fc1, c * own_ff, own_ff, 1)],
        axis=1,
    )

    def own_piece(weight, amount):
        step = amount // fsdp
        return lax.dynamic_slice_in_dim(weight, (c % share) * amount + (c // share) * step, step, 0)

    out_rows = jnp.concatenate([own_piece(w_dense, own_width), own_piece(w_fc2, own_ff)])
    spread = turn_spread(own_width)
    (
        x_all, g_all, hidden, stat, queries, keys, values, d_att, act, d_up, w_in, w_out, turns, small,
    ) = first(
        tokens, cotangent, turn_rows(positions.reshape(rows), own_width), in_rows, out_rows, small,
        spread, ctx, fsdp,
    )
    where = jnp.argsort(block_order).astype(jnp.int32)
    att, d_proj = attention(
        block_order, where, seq // block_order.shape[0], queries, keys, values, d_att,
        turns.reshape(seq, own_width), spread,
    )
    result, input_grad, in_all, out_all, vector = second(
        att, act, d_proj, d_up, w_in.reshape(width, -1), w_out, stat, small, tokens, cotangent, x_all,
        g_all, hidden, fsdp,
    )
    grad_qkv, grad_fc1, grad_dense, grad_fc2 = widen(in_all, out_all, width, ff, fsdp)

    vector = vector.reshape(ctx, -1)
    sums = jnp.sum(vector[:, : 3 * width], axis=0).reshape(3, width)
    sums = lax.dynamic_slice_in_dim(sums, f * own_rows, own_rows, 1)
    columns = vector[:, 3 * width : 3 * width + cut].reshape(ctx, 3, own_width)
    columns = columns.transpose(1, 0, 2).reshape(3 * width)
    units = vector[:, 3 * width + cut : 3 * width + cut + own_ff].reshape(ff)
    return (
        result.reshape(1, rows, width),
        input_grad.reshape(1, rows, width),
        sums[0],
        sums[1],
        grad_qkv,
        lax.dynamic_slice_in_dim(columns, f * (3 * own_rows), 3 * own_rows, 0),
        grad_dense,
        sums[2],
        grad_fc1,
        lax.dynamic_slice_in_dim(units, f * (ff // fsdp), ff // fsdp, 0),
        grad_fc2,
        sums[2],
    )


def solution(mesh):
    split = P("fsdp", "ctx", None)
    matrix = P("fsdp", None)
    vector = P("fsdp")
    return jax.shard_map(
        on_device,
        mesh=mesh,
        in_specs=(split, split, P(), P("fsdp", "ctx"), vector, vector)
        + (matrix, vector) * 4,
        out_specs=(split, split, vector, vector) + (matrix, vector) * 4,
        check_vma=False,
    )
```

```python
import functools

import jax
import jax.numpy as jnp
import numpy as np
from jax import lax
from jax.experimental import pallas as pl
from jax.experimental.pallas import tpu as pltpu
from jax.sharding import PartitionSpec as P

HEAD_DIM = 64
ROTARY = 32
NORM_EPS = 1e-05
ROPE_BASE = 10000.0
GELU_COEF = 0.7978845608028654
F32 = jnp.float32
BF16 = jnp.bfloat16
STRIP = 256
NT = (((1,), (1,)), ((), ()))
TN = (((0,), (0,)), ((), ()))
MESH = pl.DeviceIdType.MESH
MIB = 1024 * 1024


def nt_dot(left, right):
    return lax.dot_general(left, right, NT, preferred_element_type=F32)


def tn_dot(left, right):
    return lax.dot_general(left, right, TN, preferred_element_type=F32)


def dot(left, right):
    return jnp.dot(left, right, preferred_element_type=F32)


def turn_rows(positions, width):
    half = ROTARY // 2
    frequency = ROPE_BASE ** (-(jnp.arange(half, dtype=F32) * (2.0 / ROTARY)))
    turned = positions.astype(F32)[:, None] * frequency
    both = jnp.concatenate([jnp.cos(turned), jnp.sin(turned)], axis=1)
    coarse = both.astype(BF16)
    fine = (both - coarse.astype(F32)).astype(BF16)
    rows = positions.shape[0]
    used = 4 * half + 1
    return jnp.concatenate(
        [coarse, fine, jnp.ones((rows, 1), BF16), jnp.zeros((rows, width - used), BF16)], axis=1
    )


def turn_spread(width):
    half = ROTARY // 2
    table = np.zeros((width, 3 * width), np.float32)
    for column in range(width):
        at = column % HEAD_DIM
        if at >= ROTARY:
            table[4 * half, column] = 1.0
            continue
        for part in (0, 2 * half):
            table[part + at % half, column] = 1.0
            if at < half:
                table[part + half + at, width + column] = -1.0
            else:
                table[part + half + at - half, 2 * width + column] = 1.0
    return jnp.asarray(table, BF16)


def turn(values, tables, back):
    width = values.shape[1]
    half = ROTARY // 2
    same, after, before = (tables[:, at * width : (at + 1) * width] for at in range(3))
    moved = pltpu.roll(values, width - half, 1) * after + pltpu.roll(values, half, 1) * before
    return values * same - moved if back else values * same + moved


AWAY = [(dx, flip) for dx in range(4) for flip in (False, True) if dx or flip]


class Place:
    def __init__(self):
        self.c, self.f = lax.axis_index("ctx"), lax.axis_index("fsdp")
        self.y, self.z, self.core = self.c // 4, (self.c // 2) % 2, self.c % 2
        self.x, self.half = self.f // 2, self.f % 2

    def block(self, dy, flip, other=False):
        core = 1 - self.core if other else self.core
        return ((self.y + dy) % 4) * 4 + (1 - self.z if flip else self.z) * 2 + core

    def shard(self, dx, flip):
        return ((self.x + dx) % 4) * 2 + (1 - self.half if flip else self.half)

    def to_ctx(self, dy, flip, other=False):
        return (self.block(dy, flip, other), self.f)

    def to_fsdp(self, dx, flip):
        return (self.c, self.shard(dx, flip))

    def to_swap(self):
        return (2 * self.f + self.c % 2, self.c // 2)


class Post:
    def __init__(self, place, send, recv):
        self.place, self.send, self.recv, self.started = place, send, recv, []
        self.left = set()

    def copy(self, source, target, device):
        at = len(self.started)
        copy = pltpu.make_async_remote_copy(
            src_ref=source, dst_ref=target, send_sem=self.send.at[at], recv_sem=self.recv.at[at],
            device_id=device, device_id_type=MESH,
        )
        self.started.append(copy)
        copy.start()
        return copy

    def greet(self):
        place = self.place
        barrier = pltpu.get_barrier_semaphore()
        partners = [
            place.to_ctx(1, False), place.to_ctx(-1, False), place.to_ctx(0, True),
            place.to_ctx(0, False, True),
        ] + [place.to_fsdp(*to) for to in AWAY]
        for partner in partners:
            pl.semaphore_signal(barrier, inc=1, device_id=partner, device_id_type=MESH)
        swap = place.to_swap()
        same = jnp.logical_and(swap[0] == place.c, swap[1] == place.f)

        @pl.when(jnp.logical_not(same))
        def _():
            pl.semaphore_signal(barrier, inc=1, device_id=swap, device_id_type=MESH)

        pl.semaphore_wait(barrier, len(partners) + jnp.where(same, 0, 1))

    def has_left(self, copy):
        copy.wait_send()
        self.left.add(id(copy))

    def close(self):
        for copy in self.started:
            if id(copy) not in self.left:
                copy.wait_send()


def gather_ctx(post, own, buf, cut):
    place = post.place
    here = post.place.block(0, False)
    crossed = []

    def send(at, *to):
        return post.copy(buf.at[at], buf.at[at], place.to_ctx(*to))

    def cross(at):
        crossed.append(post.copy(buf.at[at], buf.at[at], place.to_ctx(0, False, True)))

    def first(*to):
        return post.copy(own, buf.at[here], place.to_ctx(*to))

    to_next, to_last, to_pair = first(1, False), first(-1, False), first(0, True)
    crossed.append(first(0, False, True))
    yield
    last, after = place.block(-1, False), place.block(1, False)
    lower, upper = pl.ds(0, cut), pl.ds(cut, buf.shape[1] - cut)
    to_next.wait_recv()
    low = post.copy(buf.at[last, lower], buf.at[last, lower], place.to_ctx(1, False))
    to_last.wait_recv()
    high = post.copy(buf.at[after, upper], buf.at[after, upper], place.to_ctx(-1, False))
    cross(last)
    cross(after)
    yield
    to_pair.wait_recv()
    pair = place.block(0, True)
    pair_next, pair_last = send(pair, 1, False), send(pair, -1, False)
    cross(pair)
    yield
    low.wait_recv()
    high.wait_recv()
    far = place.block(2, False)
    pair_far = send(far, 0, True)
    cross(far)
    yield
    pair_next.wait_recv()
    cross(place.block(-1, True))
    pair_last.wait_recv()
    cross(place.block(1, True))
    yield
    pair_far.wait_recv()
    cross(place.block(2, True))
    yield
    for copy in crossed:
        copy.wait_recv()


def gather_fsdp(post, own, buf, cut):
    place = post.place
    here = place.shard(0, False)
    rest = buf.shape[1] - cut

    def whole(at, dx):
        return post.copy(buf.at[at], buf.at[at], place.to_fsdp(dx, False))

    def lower(at):
        piece = buf.at[at, pl.ds(0, cut)]
        return post.copy(piece, piece, place.to_fsdp(1, False))

    def upper(at):
        piece = buf.at[at, pl.ds(cut, rest)]
        return post.copy(piece, piece, place.to_fsdp(-1, False))

    to_pair = post.copy(own, buf.at[here], place.to_fsdp(0, True))
    to_next = post.copy(own, buf.at[here], place.to_fsdp(1, False))
    to_last = post.copy(own, buf.at[here], place.to_fsdp(-1, False))
    yield
    to_next.wait_recv()
    low = lower(place.shard(-1, False))
    to_last.wait_recv()
    high = upper(place.shard(1, False))
    yield
    to_pair.wait_recv()
    pair = place.shard(0, True)
    pair_next, pair_last = whole(pair, 1), whole(pair, -1)
    yield
    pair_next.wait_recv()
    pair_low = lower(place.shard(-1, True))
    pair_last.wait_recv()
    pair_high = upper(place.shard(1, True))
    yield
    for copy in (low, high, pair_low, pair_high):
        copy.wait_recv()


def gather_direct(post, own, buf):
    place = post.place
    here = place.shard(0, False)
    copies = [post.copy(own, buf.at[here], place.to_fsdp(*to)) for to in AWAY]
    yield
    for copy in copies:
        copy.wait_recv()


class Swap:
    def __init__(self, place, source, target, send, recv, local):
        device = place.to_swap()
        self.same = jnp.logical_and(device[0] == place.c, device[1] == place.f)
        self.away = pltpu.make_async_remote_copy(
            src_ref=source, dst_ref=target, send_sem=send, recv_sem=recv, device_id=device,
            device_id_type=MESH,
        )
        self.stay = pltpu.make_async_copy(source, target, local)
        pl.when(jnp.logical_not(self.same))(lambda: self.away.start())
        pl.when(self.same)(lambda: self.stay.start())

    def wait(self):
        pl.when(jnp.logical_not(self.same))(lambda: self.away.wait())
        pl.when(self.same)(lambda: self.stay.wait())


def first_kernel(
    x_in, g_in, turn_in, w_qkv, w_fc1, w_dense, w_fc2, small_in, spread,
    x_to, g_to, hidden_to, stat_to, q_to, k_to, v_to, d_att_to, act_to, d_up_to, w_in_to, w_out_to,
    turns_to, small_to,
    x_all, g_all, hidden, stat, q_out, k_out, v_out, d_att, act, d_up, w_in, w_out, turns, small_out,
    in_rows, out_rows, pieces, piece, small_all, tables, proj, slope, vec, bias,
    send, recv, local, reads, swap_send, swap_recv,
):
    place = Place()
    post = Post(place, send, recv)
    rows, width = x_in.shape
    own_width = q_out.shape[1]
    own_ff = act.shape[1]
    cut = 3 * own_width
    here, shard = place.block(0, False), place.shard(0, False)

    def columns(first, count):
        return pl.ds(pl.multiple_of(first, 128), count)

    def rows_at(weight, amount, count):
        first = (place.c % 2) * amount + (place.c // 2) * count
        return weight.at[pl.ds(pl.multiple_of(first, 16), count)]

    dense_step = own_width // pieces.shape[0]
    fc2_step = own_ff // pieces.shape[0]
    sources = [
        (rows_at(w_dense, own_width, dense_step), out_rows.at[pl.ds(0, dense_step)]),
        (rows_at(w_fc2, own_ff, fc2_step), out_rows.at[pl.ds(dense_step, fc2_step)]),
        (w_fc1.at[:, columns(place.c * own_ff, own_ff)], in_rows.at[:, pl.ds(cut, own_ff)]),
    ] + [
        (
            w_qkv.at[:, columns(part * width + place.c * own_width, own_width)],
            in_rows.at[:, pl.ds(part * own_width, own_width)],
        )
        for part in range(3)
    ]
    ready = [
        pltpu.make_async_copy(source, target, reads.at[at])
        for at, (source, target) in enumerate(sources)
    ]
    for copy in ready:
        copy.start()
    post.greet()
    for copy in ready:
        copy.wait()
    swap = Swap(place, out_rows, piece, swap_send, swap_recv, local.at[0])
    keeps = []

    def keep(source, target):
        copy = pltpu.make_async_copy(source, target, local.at[1 + len(keeps)])
        keeps.append(copy)
        copy.start()
        return copy

    own = [
        keep(x_in, x_all.at[here]), keep(in_rows, w_in.at[shard]), keep(turn_in, turns.at[here]),
        keep(small_in, small_all.at[shard]), keep(g_in, g_all.at[here]),
    ]
    x_flow = gather_ctx(post, x_in, x_all, rows // 2)
    in_flow = gather_fsdp(post, in_rows, w_in, in_rows.shape[0] // 2)
    small_flow = gather_direct(post, small_in, small_all)
    turn_flow = gather_ctx(post, turn_in, turns, rows // 2)
    def advance(*flows):
        for flow in flows:
            next(flow, None)

    advance(x_flow, in_flow, small_flow, turn_flow)
    advance(x_flow, in_flow)
    g_flow = gather_ctx(post, g_in, g_all, rows // 2)
    advance(g_flow)
    swap.wait()
    keep(piece, pieces.at[shard])
    out_flow = gather_fsdp(post, piece, pieces, 48)
    advance(out_flow)
    advance(x_flow, in_flow, g_flow, turn_flow, out_flow)
    for _ in small_flow:
        pass
    for copy in own[:4]:
        copy.wait()

    side = small_all.shape[2]
    small_out[...] = small_all[...].astype(F32)
    for at in range(small_all.shape[0]):
        vec[0:2, at * side : (at + 1) * side] = small_out[at, 0:2, :]
    for part in range(3):
        first = part * width + place.c * own_width
        count = 3 * side
        row = small_out[first // count, pl.ds(4 + (first % count) // side, 1), :]
        bias[0:1, part * own_width : (part + 1) * own_width] = jnp.where(
            first % side == 0, row[:, :own_width], row[:, own_width:]
        )
    for part in range(2):
        row = small_out[place.c // 2, pl.ds(7 + 2 * (place.c % 2) + part, 1), :]
        bias[0:1, cut + part * side : cut + (part + 1) * side] = row

    def normalise(block):
        lane = lax.broadcasted_iota(jnp.int32, (rows, stat.shape[1]), 1)
        target = pl.ds(pl.multiple_of(block * rows, rows), rows)
        value = x_all[block].astype(F32)
        mean = jnp.mean(value, axis=1, keepdims=True)
        centred = value - mean
        inverse = lax.rsqrt(jnp.mean(centred * centred, axis=1, keepdims=True) + NORM_EPS)
        hidden[target, :] = (centred * inverse * vec[0:1, :] + vec[1:2, :]).astype(BF16)
        stat[target, :] = jnp.where(lane < HEAD_DIM, mean, inverse)

    def normalise_each(targets):
        order = [place.block(*to) for to in targets]

        def body(at, carry):
            block = order[0]
            for number, other in enumerate(order[1:]):
                block = jnp.where(at == number + 1, other, block)
            normalise(block)
            return carry

        lax.fori_loop(0, len(order), body, 0)

    normalise_each([(0, False), (1, False), (-1, False)])
    advance(x_flow, in_flow, g_flow, turn_flow, out_flow)
    normalise_each([(0, True)])
    advance(x_flow, in_flow, g_flow, turn_flow, out_flow)
    keep(w_in, w_in_to)
    normalise_each([(2, False), (1, True), (-1, True)])
    advance(x_flow, g_flow, turn_flow, out_flow)
    normalise_each([(2, True)])
    advance(x_flow, turn_flow)
    keep(x_all, x_to)
    normalise_each([(dy, flip, True) for dy in range(4) for flip in (False, True)])
    keep(hidden, hidden_to)
    keep(stat, stat_to)
    keep(small_out, small_to)
    advance(turn_flow)
    keep(turns, turns_to)

    chunk_rows = proj.shape[0]
    step = 64
    group = chunk_rows // rows

    def project(chunk, carry):
        take = pl.ds(pl.multiple_of(chunk * chunk_rows, chunk_rows), chunk_rows)
        weight = w_in[...].reshape(width, proj.shape[1])
        proj[...] = dot(hidden[take, :], weight)
        turned = turns[pl.ds(chunk * group, group)].reshape(chunk_rows, own_width)
        tables[...] = dot(turned, spread[...])

        def body(at, inner):
            source = pl.ds(pl.multiple_of(at * step, step), step)
            target = pl.ds(pl.multiple_of(chunk * chunk_rows + at * step, step), step)
            value = proj[source, :] + bias[0:1, :]
            table = tables[source, :]
            q_out[target, :] = turn(value[:, :own_width], table, False).astype(BF16)
            k_out[target, :] = turn(value[:, own_width : 2 * own_width], table, False).astype(BF16)
            v_out[target, :] = value[:, 2 * own_width : cut].astype(BF16)
            up = value[:, cut:]
            square = up * up
            curve = jnp.tanh(GELU_COEF * up * (1.0 + 0.044715 * square))
            act[target, :] = (0.5 * up * (1.0 + curve)).astype(BF16)
            slope[target, :] = 0.5 * (1.0 + curve) + 0.5 * up * (1.0 - curve * curve) * (
                GELU_COEF * (1.0 + 3.0 * 0.044715 * square)
            )
            return inner

        lax.fori_loop(0, chunk_rows // step, body, 0)
        return carry

    chunks = hidden.shape[0] // chunk_rows
    project(0, 0)
    project(1, 0)
    advance(g_flow)
    project(2, 0)
    project(3, 0)
    for target, source in ((q_to, q_out), (k_to, k_out), (v_to, v_out), (act_to, act)):
        keep(source, target)
    for _ in out_flow:
        pass
    keeps[5].wait()
    for at in range(pieces.shape[0]):
        w_out[at * dense_step : (at + 1) * dense_step, :] = pieces[at, :dense_step, :]
        first = own_width + at * fc2_step
        w_out[first : first + fc2_step, :] = pieces[at, dense_step:, :]
    keep(w_out, w_out_to)
    advance(g_flow)
    own[4].wait()
    keep(g_all, g_to)

    def back(chunk, carry):
        grads = g_all[pl.ds(chunk * group, group)].reshape(chunk_rows, width)
        proj[:, : w_out.shape[0]] = nt_dot(grads, w_out[...])

        def body(at, inner):
            source = pl.ds(pl.multiple_of(at * step, step), step)
            target = pl.ds(pl.multiple_of(chunk * chunk_rows + at * step, step), step)
            d_att[target, :] = proj[source, :own_width].astype(BF16)
            d_act = proj[source, own_width : w_out.shape[0]]
            d_up[target, :] = (d_act * slope[target, :]).astype(BF16)
            return inner

        lax.fori_loop(0, chunk_rows // step, body, 0)
        return carry

    lax.fori_loop(0, chunks, back, 0)
    keep(d_att, d_att_to)
    keep(d_up, d_up_to)
    for copy in keeps[6:]:
        copy.wait()
    post.close()


def first(tokens, cotangent, turns, w_qkv, w_fc1, w_dense, w_fc2, small, spread, ctx, fsdp):
    rows, width = tokens.shape
    seq = ctx * rows
    own_width, own_ff = turns.shape[1], w_fc1.shape[1] // ctx
    columns = 3 * own_width + own_ff
    out_total = own_width + own_ff
    in_rows = pltpu.VMEM((width // fsdp, columns), BF16)
    out_rows = pltpu.VMEM((out_total // fsdp, width), BF16)
    many = 3 * 16 + 2 * 9 + fsdp - 1
    any_, vmem = pl.BlockSpec(memory_space=pl.ANY), pl.BlockSpec(memory_space=pltpu.VMEM)

    def low(*shape):
        return jax.ShapeDtypeStruct(shape, BF16)

    def wide(*shape):
        return jax.ShapeDtypeStruct(shape, F32)

    outs = [
        low(ctx, rows, width), low(ctx, rows, width), low(seq, width), wide(seq, 128),
        low(seq, own_width), low(seq, own_width), low(seq, own_width), low(seq, own_width),
        low(seq, own_ff), low(seq, own_ff), low(fsdp, width // fsdp, columns),
        low(out_total, width), low(ctx, rows, own_width), wide(*((fsdp,) + small.shape)),
    ]
    chunk_rows = 4 * rows
    return pl.pallas_call(
        first_kernel,
        out_shape=tuple(outs),
        in_specs=[any_] * 8 + [vmem],
        out_specs=(any_,) * len(outs),
        scratch_shapes=[pltpu.VMEM(out.shape, out.dtype) for out in outs]
        + [
            in_rows,
            out_rows,
            pltpu.VMEM((fsdp, out_total // fsdp, width), BF16),
            out_rows,
            pltpu.VMEM((fsdp,) + small.shape, BF16),
            pltpu.VMEM((chunk_rows, 3 * own_width), F32),
            pltpu.VMEM((chunk_rows, columns), F32),
            pltpu.VMEM((seq, own_ff), F32),
            pltpu.VMEM((8, width), F32),
            pltpu.VMEM((8, columns), F32),
            pltpu.SemaphoreType.DMA((many,)),
            pltpu.SemaphoreType.DMA((many,)),
            pltpu.SemaphoreType.DMA((24,)),
            pltpu.SemaphoreType.DMA((6,)),
            pltpu.SemaphoreType.DMA,
            pltpu.SemaphoreType.DMA,
        ],
        compiler_params=pltpu.CompilerParams(
            collective_id=0, has_side_effects=True, vmem_limit_bytes=60 * MIB
        ),
        name="first",
    )(tokens, cotangent, turns, w_qkv, w_fc1, w_dense, w_fc2, small, spread)


def attention_kernel(
    block, order, q_hbm, k_hbm, v_hbm, g_hbm, turns_hbm, spread, o_to, d_to,
    q_in, k_in, v_in, g_in, turns, o_out, d_out, loads, qs, ks, vs, gs, os, dqs, dks, dvs, kt, vt, table,
):
    rows, width = q_in.shape
    blocks = rows // block
    reads = [
        pltpu.make_async_copy(source, target, loads.at[at])
        for at, (source, target) in enumerate(
            [(q_hbm, q_in), (k_hbm, k_in), (v_hbm, v_in), (g_hbm, g_in), (turns_hbm, turns)]
        )
    ]
    for copy in reads:
        copy.start()
    for copy in reads:
        copy.wait()

    def collect(at, carry):
        src = pl.ds(pl.multiple_of(at * block, block), block)
        dst = pl.ds(pl.multiple_of(order[at] * block, block), block)
        qs[dst, :] = q_in[src, :]
        ks[dst, :] = k_in[src, :]
        vs[dst, :] = v_in[src, :]
        gs[dst, :] = g_in[src, :]
        return carry

    lax.fori_loop(0, blocks, collect, 0, unroll=4)
    dks[...] = jnp.zeros_like(dks)
    dvs[...] = jnp.zeros_like(dvs)
    heads = width // HEAD_DIM
    scale = HEAD_DIM ** (-0.5)
    q_pos = lax.broadcasted_iota(jnp.int32, (STRIP, STRIP), 0)
    k_pos = lax.broadcasted_iota(jnp.int32, (STRIP, STRIP), 1)
    diagonal = q_pos <= k_pos
    table[...] = dot(turns[...], spread[...])
    kt[...] = ks[...].T
    vt[...] = vs[...].T
    sides = [slice(head * HEAD_DIM, (head + 1) * HEAD_DIM) for head in range(heads)]
    strips = rows // STRIP

    def begin(strip):
        here = slice(strip * STRIP, (strip + 1) * STRIP)
        count = (strip + 1) * STRIP
        query = [qs[here, cols] * jnp.asarray(scale, BF16) for cols in sides]
        part = [nt_dot(ks[:count, cols], query[h]) for h, cols in enumerate(sides)]
        return query, part

    ready = begin(0)
    for strip in range(strips):
        here = slice(strip * STRIP, (strip + 1) * STRIP)
        count = (strip + 1) * STRIP
        query, part = ready
        edge = [jnp.where(diagonal, p[count - STRIP :, :], -1e30) for p in part]
        part = [jnp.concatenate([p[: count - STRIP, :], e], axis=0) if strip else e for p, e in zip(part, edge)]
        part = [jnp.exp(p - jnp.max(p, axis=0, keepdims=True)) for p in part]
        inverse = [1.0 / jnp.sum(p, axis=0, keepdims=True) for p in part]
        low = [p.astype(BF16) for p in part]
        mixed = [dot(vt[cols, :count], low[h]) * inverse[h] for h, cols in enumerate(sides)]
        grad = [gs[here, cols].astype(F32).T * inverse[h] for h, cols in enumerate(sides)]
        centre = [jnp.sum(g * m, axis=0, keepdims=True) for g, m in zip(grad, mixed)]
        os[here, :] = jnp.concatenate(mixed, axis=0).T.astype(BF16)
        grad = [g.astype(BF16) for g in grad]
        if strip + 1 < strips:
            ready = begin(strip + 1)
        d_score = [(part[h] * (dot(vs[:count, cols], grad[h]) - centre[h])).astype(BF16) for h, cols in enumerate(sides)]
        dqs[here, :] = jnp.concatenate([dot(kt[cols, :count], d_score[h]) for h, cols in enumerate(sides)], axis=0).T * scale
        dks[:count, :] += jnp.concatenate([dot(d_score[h], query[h]) for h in range(heads)], axis=1)
        dvs[:count, :] += jnp.concatenate([nt_dot(low[h], grad[h]) for h in range(heads)], axis=1)

    def give(at, carry):
        src = pl.ds(pl.multiple_of(order[at] * block, block), block)
        dst = pl.ds(pl.multiple_of(at * block, block), block)
        tables = table[dst, :]
        o_out[dst, :] = os[src, :]
        d_out[dst, :width] = turn(dqs[src, :], tables, True).astype(BF16)
        d_out[dst, width : 2 * width] = turn(dks[src, :], tables, True).astype(BF16)
        d_out[dst, 2 * width :] = dvs[src, :].astype(BF16)
        return carry

    lax.fori_loop(0, blocks, give, 0, unroll=4)
    writes = [
        pltpu.make_async_copy(o_out, o_to, loads.at[0]),
        pltpu.make_async_copy(d_out, d_to, loads.at[1]),
    ]
    for copy in writes:
        copy.start()
    for copy in writes:
        copy.wait()


def attention(order, block, queries, keys, values, grads, turns, spread):
    rows, width = queries.shape
    vmem = pl.BlockSpec(memory_space=pltpu.VMEM)
    smem = pl.BlockSpec(memory_space=pltpu.SMEM)
    any_ = pl.BlockSpec(memory_space=pl.ANY)
    return pl.pallas_call(
        functools.partial(attention_kernel, block),
        out_shape=(
            jax.ShapeDtypeStruct((rows, width), BF16),
            jax.ShapeDtypeStruct((rows, 3 * width), BF16),
        ),
        in_specs=[smem] + [any_] * 5 + [vmem],
        out_specs=(any_, any_),
        scratch_shapes=[pltpu.VMEM((rows, width), BF16)] * 6
        + [pltpu.VMEM((rows, 3 * width), BF16), pltpu.SemaphoreType.DMA((5,))]
        + [pltpu.VMEM((rows, width), BF16)] * 5
        + [pltpu.VMEM((rows, width), F32)] * 3
        + [pltpu.VMEM((width, rows), BF16), pltpu.VMEM((width, rows), BF16)]
        + [pltpu.VMEM((rows, 3 * width), F32)],
        compiler_params=pltpu.CompilerParams(vmem_limit_bytes=60 * MIB),
        cost_estimate=pl.CostEstimate(
            flops=6 * rows * rows * width,
            bytes_accessed=rows * width * 22,
            transcendentals=rows * rows * width // HEAD_DIM // 2,
        ),
        name="attention",
    )(order, queries, keys, values, grads, turns, spread)


ORDER = [(2, True), (1, True), (-1, True), (2, False), (0, True), (1, False), (-1, False), (0, False)]
SHARDS = [(2, True), (2, False), (1, True), (-1, True), (1, False), (-1, False), (0, True), (0, False)]


def add_into(target, *parts):
    step = 64 if target.shape[0] % 64 == 0 else 16
    plain = len(parts) == 2 and target.dtype == BF16

    def body(at, carry):
        take = pl.ds(pl.multiple_of(at * step, step), step)
        if plain:
            target[take, :] = parts[0][take, :] + parts[1][take, :]
            return carry
        total = parts[0][take, :].astype(F32)
        for part in parts[1:]:
            total = total + part[take, :].astype(F32)
        target[take, :] = total.astype(target.dtype)
        return carry

    lax.fori_loop(0, target.shape[0] // step, body, 0)


def reduce_ctx(post, own, core, crossed, pair_in, half_in, ring_in, cross_in, last_in, total):
    place = post.place
    cut = half_in.shape[1]
    up, down, pair = place.to_ctx(1, False), place.to_ctx(-1, False), place.to_ctx(0, True)

    def meet(at, *more):
        crossed[at].wait_recv()
        add_into(core.at[at], own.at[at], core.at[at], *more)

    meet(0)
    far = post.copy(core.at[0], pair_in, pair)
    yield
    meet(1)
    cross_next = post.copy(core.at[1], cross_in.at[0], up)
    meet(2)
    cross_last = post.copy(core.at[2], cross_in.at[1], down)
    yield
    far.wait_recv()
    meet(3, pair_in)
    low = post.copy(core.at[3, pl.ds(0, cut)], half_in.at[0], up)
    high = post.copy(core.at[3, pl.ds(cut, cut)], half_in.at[1], down)
    yield
    cross_next.wait_recv()
    cross_last.wait_recv()
    meet(4, cross_in.at[0], cross_in.at[1])
    last = post.copy(core.at[4], last_in, pair)
    yield
    meet(5)
    low.wait_recv()
    lower = core.at[5, pl.ds(0, cut)]
    add_into(lower, lower, half_in.at[0])
    ring_next = post.copy(core.at[5], ring_in.at[0], up)
    meet(6)
    high.wait_recv()
    upper = core.at[6, pl.ds(cut, cut)]
    add_into(upper, upper, half_in.at[1])
    ring_last = post.copy(core.at[6], ring_in.at[1], down)
    yield
    crossed[7].wait_recv()
    last.wait_recv()
    ring_next.wait_recv()
    ring_last.wait_recv()
    add_into(total, own.at[7], core.at[7], ring_in.at[0], ring_in.at[1], last_in)


def reduce_fsdp(post, part, low_in, high_in, ring_in, pair_in, total):
    place = post.place
    cut, rest = low_in.shape[1], high_in.shape[1]
    lower, upper = pl.ds(0, cut), pl.ds(cut, rest)
    up, down, pair = place.to_fsdp(1, False), place.to_fsdp(-1, False), place.to_fsdp(0, True)
    halves = [
        (
            post.copy(part.at[side, lower], low_in.at[side], up),
            post.copy(part.at[side, upper], high_in.at[side], down),
        )
        for side in range(2)
    ]
    yield
    rings = []
    for side in range(2):
        low, high = halves[side]
        after, before = part.at[2 + 2 * side], part.at[3 + 2 * side]
        low.wait_recv()
        add_into(after.at[lower], after.at[lower], low_in.at[side])
        to_next = post.copy(after, ring_in.at[side, 0], up)
        high.wait_recv()
        add_into(before.at[upper], before.at[upper], high_in.at[side])
        to_last = post.copy(before, ring_in.at[side, 1], down)
        rings.append((to_next, to_last))
        yield
    for copy in rings[0]:
        copy.wait_recv()
    add_into(part.at[6], part.at[6], ring_in.at[0, 0], ring_in.at[0, 1])
    across = post.copy(part.at[6], pair_in, pair)
    yield
    for copy in rings[1]:
        copy.wait_recv()
    across.wait_recv()
    add_into(total, part.at[7], ring_in.at[1, 0], ring_in.at[1, 1], pair_in)


def run(*flows):
    flows = list(flows)
    while flows:
        flows = [flow for flow in flows if next(flow, flows) is not flows]


def second_kernel(
    att_in, act_in, d_proj_in, d_up_in, w_in_in, w_out_in, stat_in, g_own_in, x_all, g_all, hidden,
    out_total, hid_total, in_all, out_all, vector_all,
    att, act, d_proj, d_up, w_in, w_out, stat, g_own,
    own_a, own_b, core_a, core_b, slot_a, slot_b,
    pair_a, half_a, ring_a, cross_a, last_a, pair_b, half_b, ring_b, cross_b, last_b,
    in_part, in_low, in_high, in_ring, in_pair, in_sum,
    out_part, out_low, out_high, out_ring, out_pair, out_sum, out_piece,
    column, x_block, total_a, total_b, gain_sum, shift_sum,
    vector, vector_shards, vector_sum,
    send, recv, local, loads, reads, swap_send, swap_recv,
):
    place = Place()
    post = Post(place, send, recv)
    rows, width = g_own.shape
    own_width = att.shape[1]
    cut = d_proj.shape[1]
    side = in_part.shape[1]
    here, shard = place.block(0, False), place.shard(0, False)
    keeps, numbers = [], iter(range(6))

    def keep(source, target):
        copy = pltpu.make_async_copy(source, target, local.at[next(numbers)])
        keeps.append(copy)
        copy.start()
        return copy

    operands = [
        pltpu.make_async_copy(source, target, reads.at[at])
        for at, (source, target) in enumerate(
            [
                (d_proj_in, d_proj), (d_up_in, d_up), (att_in, att), (act_in, act), (w_out_in, w_out),
                (w_in_in, w_in), (stat_in, stat), (g_own_in, g_own),
            ]
        )
    ]

    def load_x(at):
        dy, flip = ORDER[at]
        block = place.block(dy, flip) // 2
        copy = pltpu.make_async_copy(
            x_all.at[pl.ds(2 * block, 2)], x_block.at[at % 2], loads.at[at % 2]
        )
        copy.start()
        return copy

    ahead = column.shape[0]

    def load_column(at):
        if at < len(SHARDS):
            first = pl.multiple_of(place.shard(*SHARDS[at]) * side, side)
            source = hidden.at[:, pl.ds(first, side)]
        else:
            source = g_all.at[:, pl.ds((at - len(SHARDS)) * side, side)]
        copy = pltpu.make_async_copy(source, column.at[at % ahead], loads.at[2 + at % ahead])
        copy.start()
        return copy

    for copy in operands[:2]:
        copy.start()
    pending_column = [load_column(at) for at in range(ahead - 1)]
    pending_x = [load_x(0)]
    for copy in operands[2:]:
        copy.start()
    post.greet()
    gain_sum[...] = jnp.zeros_like(gain_sum)
    shift_sum[...] = jnp.zeros_like(shift_sum)
    crossed_a, crossed_b, slots = {}, {}, {}
    partner = place.to_ctx(0, False, True)
    depth = slot_a.shape[0]

    def produce(at):
        dy, flip = ORDER[at]
        block = place.block(dy, flip) // 2
        pending_x.pop().wait()
        if at + 1 < len(ORDER):
            pending_x.append(load_x(at + 1))
        slot = at % depth
        if at >= depth:
            for copy in slots[at - depth]:
                post.has_left(copy)
        other_rows = pl.ds(pl.multiple_of(block * (2 * rows) + (1 - place.core) * rows, rows), rows)
        own_rows = pl.ds(pl.multiple_of(block * (2 * rows) + place.core * rows, rows), rows)

        def both(ref):
            return jnp.concatenate([ref[other_rows, :], ref[own_rows, :]], axis=0)

        left, right = both(att), both(act)
        span = width // 2
        for first in range(0, width, span):
            take = slice(first, first + span)
            value = dot(left, w_out[:own_width, take]) + dot(right, w_out[own_width:, take])
            slot_a[slot, :, take] = value[:rows].astype(BF16)
            own_a[at, :, take] = value[rows:].astype(BF16)
        left, right, stats = both(d_proj), both(d_up), both(stat)
        mean, inverse = stats[:, 0:1], stats[:, HEAD_DIM : HEAD_DIM + 1]
        span = width // 4
        for first in range(0, width, span):
            take = slice(first, first + span)
            value = nt_dot(left, w_in[take, :cut]) + nt_dot(right, w_in[take, cut:])
            slot_b[slot, :, take] = value[:rows].astype(BF16)
            own_b[at, :, take] = value[rows:].astype(BF16)
            tokens = jnp.concatenate(
                [x_block[at % 2, 1 - place.core, :, take], x_block[at % 2, place.core, :, take]],
                axis=0,
            )
            normed = (tokens.astype(F32) - mean) * inverse
            parts = (2 * rows // 8, 8, span)
            gain_sum[:, take] += jnp.sum((value * normed).reshape(parts), axis=0)
            shift_sum[:, take] += jnp.sum(value.reshape(parts), axis=0)
        crossed_a[at] = post.copy(slot_a.at[slot], core_a.at[at], partner)
        crossed_b[at] = post.copy(slot_b.at[slot], core_b.at[at], partner)
        slots[at] = (crossed_a[at], crossed_b[at])

    def next_column(at):
        pending_column.pop(0).wait()
        if at + ahead - 1 < 2 * len(SHARDS):
            pending_column.append(load_column(at + ahead - 1))
        return column[at % ahead]

    def grad_in(at):
        rows_of = next_column(at)
        in_part[at, :, :cut] = tn_dot(rows_of, d_proj[...]).astype(BF16)
        in_part[at, :, cut:] = tn_dot(rows_of, d_up[...]).astype(BF16)

    def grad_out(at):
        columns = next_column(len(SHARDS) + at)
        take = slice(at * side, (at + 1) * side)
        dense = tn_dot(att[...], columns).astype(BF16)
        fc2 = tn_dot(act[...], columns).astype(BF16)
        dense_step, fc2_step = dense.shape[0] // len(SHARDS), fc2.shape[0] // len(SHARDS)
        for to in range(len(SHARDS)):
            out_part[to, :dense_step, take] = dense[to * dense_step : (to + 1) * dense_step]
            out_part[to, dense_step:, take] = fc2[to * fc2_step : (to + 1) * fc2_step]

    class ByShard:
        @property
        def at(self):
            return self

        def __getitem__(self, index):
            if isinstance(index, tuple):
                return out_part.at[(place.shard(*SHARDS[index[0]]),) + index[1:]]
            return out_part.at[place.shard(*SHARDS[index])]

    def in_flow():
        yield from reduce_fsdp(post, in_part, in_low, in_high, in_ring, in_pair, in_sum)
        keep(in_sum, in_all.at[here])
        yield from gather_ctx(post, in_sum, in_all, in_sum.shape[0] // 2)

    def out_flow():
        yield from reduce_fsdp(post, ByShard(), out_low, out_high, out_ring, out_pair, out_sum)
        swap = Swap(place, out_sum, out_piece, swap_send, swap_recv, local.at[6])
        yield
        swap.wait()
        keep(out_piece, out_all.at[here])
        yield from gather_ctx(post, out_piece, out_all, 48)

    def vector_flow():
        mine = keep(vector, vector_shards.at[shard])
        yield from gather_fsdp(post, vector, vector_shards, 8)
        mine.wait()
        keeps[:] = [kept for kept in keeps if kept is not mine]
        total = vector_shards[0]
        for at in range(1, vector_shards.shape[0]):
            total = total + vector_shards[at]
        vector_sum[...] = total
        keep(vector_sum, vector_all.at[here])
        yield from gather_ctx(post, vector_sum, vector_all, 8)

    def rows_flow(own, core, crossed, pair, half, ring, cross, last, total, target):
        yield from reduce_ctx(post, own, core, crossed, pair, half, ring, cross, last, total)
        keep(total, target)

    ins, outs = in_flow(), out_flow()
    a = rows_flow(
        own_a, core_a, crossed_a, pair_a, half_a, ring_a, cross_a, last_a, total_a, out_total
    )
    b = rows_flow(
        own_b, core_b, crossed_b, pair_b, half_b, ring_b, cross_b, last_b, total_b, hid_total
    )

    def both_next():
        next(a)
        next(b)

    for copy in operands[:2]:
        copy.wait()
    grad_in(0)
    grad_in(1)
    next(ins)
    for copy in operands[2:]:
        copy.wait()
    produce(0)
    produce(1)
    both_next()
    produce(2)
    both_next()
    for at in range(2, 8):
        grad_in(at)
    produce(3)
    for at in range(8):
        grad_out(at)
    next(outs)
    both_next()
    next(ins)
    produce(4)
    next(ins)
    both_next()
    produce(5)
    produce(6)
    next(outs)
    both_next()
    next(outs)
    produce(7)
    next(ins)

    half = vector.shape[1]
    ones = jnp.ones((16, att.shape[0]), BF16)
    columns = jnp.concatenate([dot(ones, d_proj[...])[:1], dot(ones, d_up[...])[:1]], axis=1)
    vector[...] = jnp.zeros_like(vector)
    sums = [
        jnp.sum(gain_sum[...], axis=0, keepdims=True),
        jnp.sum(shift_sum[...], axis=0, keepdims=True),
        dot(ones[:, :rows], g_own[...])[:1],
    ]
    for at, row in enumerate(sums):
        vector[2 * at : 2 * at + 1, :] = row[:, :half]
        vector[2 * at + 1 : 2 * at + 2, :] = row[:, half:]
    vector[6:7, : columns.shape[1]] = columns
    vectors = vector_flow()
    next(vectors)
    run(ins, outs, a, b, vectors)

    for kept in keeps:
        kept.wait()
    post.close()


def second(att, act, d_proj, d_up, w_in, w_out, stat, cotangent, x_all, g_all, hidden, fsdp):
    rows, width = cotangent.shape
    ctx = x_all.shape[0]
    side = width // fsdp
    in_columns, out_rows = w_in.shape[1], w_out.shape[0] // fsdp
    any_ = pl.BlockSpec(memory_space=pl.ANY)

    def low(*shape):
        return pltpu.VMEM(shape, BF16)

    def wide(*shape):
        return pltpu.VMEM(shape, F32)

    def ctx_slots():
        return [
            low(rows, width), low(2, rows // 2, width), low(2, rows, width), low(2, rows, width),
            low(rows, width),
        ]

    def fsdp_slots(depth, columns, cut):
        return [
            low(fsdp, depth, columns), low(2, cut, columns), low(2, depth - cut, columns),
            low(2, 2, depth, columns), low(depth, columns), low(depth, columns),
        ]

    vector = (16, width // 2)
    many = 2 * 16 + 2 * 9 + 2 * 16 + 9 + 16
    ahead = 4
    operands = (att, act, d_proj, d_up, w_in, w_out, stat, cotangent)
    return pl.pallas_call(
        second_kernel,
        out_shape=(
            jax.ShapeDtypeStruct((rows, width), F32),
            jax.ShapeDtypeStruct((rows, width), F32),
            jax.ShapeDtypeStruct((ctx, side, in_columns), BF16),
            jax.ShapeDtypeStruct((ctx, out_rows, width), BF16),
            jax.ShapeDtypeStruct((ctx,) + vector, F32),
        ),
        in_specs=[any_] * 11,
        out_specs=(any_,) * 5,
        scratch_shapes=[pltpu.VMEM(operand.shape, operand.dtype) for operand in operands]
        + [low(ctx // 2, rows, width)] * 4
        + [low(2, rows, width)] * 2
        + ctx_slots()
        + ctx_slots()
        + fsdp_slots(side, in_columns, side // 2)
        + fsdp_slots(out_rows, width, 48)
        + [low(out_rows, width)]
        + [
            low(ahead, ctx * rows, side), low(2, 2, rows, width), wide(rows, width),
            wide(rows, width), wide(8, width), wide(8, width),
            wide(*vector), wide(fsdp, *vector), wide(*vector),
            pltpu.SemaphoreType.DMA((many,)),
            pltpu.SemaphoreType.DMA((many,)),
            pltpu.SemaphoreType.DMA((7,)),
            pltpu.SemaphoreType.DMA((2 + ahead,)),
            pltpu.SemaphoreType.DMA((len(operands),)),
            pltpu.SemaphoreType.DMA,
            pltpu.SemaphoreType.DMA,
        ],
        compiler_params=pltpu.CompilerParams(
            collective_id=1, has_side_effects=True, vmem_limit_bytes=63 * MIB
        ),
        name="second",
    )(*operands, x_all, g_all.reshape(ctx * rows, width), hidden)


def widen_kernel(
    in_all, out_all, branches_in, d_hidden_in, x_in, g_in, small_in,
    qkv, fc1, dense, fc2, result_to, input_grad_to,
    in_low, out_low, in_wide, out_wide, vec, branches, d_hidden, x_own, g_own, small, result,
    input_grad, loads, stores, reads,
):
    count = in_all.shape[0]
    fsdp = count // 2
    slots = in_low.shape[0]
    own = qkv.shape[1] // 3 // count
    units = fc1.shape[1] // count
    dense_step, fc2_step = dense.shape[0] // count, fc2.shape[0] // count

    def load(at):
        slot = at % slots
        copies = [
            pltpu.make_async_copy(in_all.at[at], in_low.at[slot], loads.at[slot, 0]),
            pltpu.make_async_copy(out_all.at[at], out_low.at[slot], loads.at[slot, 1]),
        ]
        for copy in copies:
            copy.start()
        return copies

    ahead = [load(at) for at in range(slots - 1)]
    stored = []
    own_rows = [
        pltpu.make_async_copy(source, target, reads.at[at])
        for at, (source, target) in enumerate(
            [
                (branches_in, branches), (d_hidden_in, d_hidden), (x_in, x_own), (g_in, g_own),
                (small_in, small),
            ]
        )
    ]
    for copy in own_rows:
        copy.start()

    side = small.shape[2]

    def finish():
        take = slice(None)
        token = x_own[take, :].astype(F32)
        result[take, :] = (token + branches[take, :] + vec[2:3, :] + vec[3:4, :]).astype(BF16)
        centred = token - jnp.mean(token, axis=1, keepdims=True)
        inverse = lax.rsqrt(jnp.mean(centred * centred, axis=1, keepdims=True) + NORM_EPS)
        normed = centred * inverse
        scaled = d_hidden[take, :] * vec[0:1, :]
        input_grad[take, :] = g_own[take, :].astype(F32) + inverse * (
            scaled
            - jnp.mean(scaled, axis=1, keepdims=True)
            - normed * jnp.mean(scaled * normed, axis=1, keepdims=True)
        )

    for at in range(count):
        slot = at % slots
        for copy in ahead[at]:
            copy.wait()
        if at + slots - 1 < count:
            ahead.append(load(at + slots - 1))
        if at >= slots:
            for copy in stored[at - slots]:
                copy.wait()
        add_into(in_wide.at[slot], in_low.at[slot])
        add_into(out_wide.at[slot], out_low.at[slot])
        shard, part = at // 2, at % 2
        targets = [
            (in_wide.at[slot, :, pl.ds(0, own)], qkv.at[:, pl.ds(at * own, own)]),
            (in_wide.at[slot, :, pl.ds(own, own)], qkv.at[:, pl.ds((count + at) * own, own)]),
            (in_wide.at[slot, :, pl.ds(2 * own, own)], qkv.at[:, pl.ds((2 * count + at) * own, own)]),
            (in_wide.at[slot, :, pl.ds(3 * own, units)], fc1.at[:, pl.ds(at * units, units)]),
            (
                out_wide.at[slot, pl.ds(0, dense_step)],
                dense.at[pl.ds((part * fsdp + shard) * dense_step, dense_step)],
            ),
            (
                out_wide.at[slot, pl.ds(dense_step, fc2_step)],
                fc2.at[pl.ds((part * fsdp + shard) * fc2_step, fc2_step)],
            ),
        ]
        copies = [
            pltpu.make_async_copy(source, target, stores.at[slot, number])
            for number, (source, target) in enumerate(targets)
        ]
        for copy in copies:
            copy.start()
        stored.append(copies)
        if at == 4:
            for copy in own_rows:
                copy.wait()
            for shard in range(small.shape[0]):
                vec[0:4, shard * side : (shard + 1) * side] = small[shard, 0:4, :]
            finish()
    writes = [
        pltpu.make_async_copy(result, result_to, reads.at[0]),
        pltpu.make_async_copy(input_grad, input_grad_to, reads.at[1]),
    ]
    for copy in writes:
        copy.start()
    for copies in stored[-slots:]:
        for copy in copies:
            copy.wait()
    for copy in writes:
        copy.wait()


def widen(in_all, out_all, branches, d_hidden, tokens, cotangent, small, ff):
    any_ = pl.BlockSpec(memory_space=pl.ANY)
    rows, width = tokens.shape
    fsdp = small.shape[0]
    slots = 4
    side = width // fsdp
    shapes = [(side, 3 * width), (side, ff), (side, width), (ff // fsdp, width)]
    return pl.pallas_call(
        widen_kernel,
        out_shape=tuple(jax.ShapeDtypeStruct(shape, F32) for shape in shapes)
        + (jax.ShapeDtypeStruct((rows, width), BF16), jax.ShapeDtypeStruct((rows, width), F32)),
        in_specs=[any_] * 7,
        out_specs=(any_,) * 6,
        scratch_shapes=[
            pltpu.VMEM((slots,) + in_all.shape[1:], BF16),
            pltpu.VMEM((slots,) + out_all.shape[1:], BF16),
            pltpu.VMEM((slots,) + in_all.shape[1:], F32),
            pltpu.VMEM((slots,) + out_all.shape[1:], F32),
            pltpu.VMEM((8, width), F32),
            pltpu.VMEM((rows, width), F32),
            pltpu.VMEM((rows, width), F32),
            pltpu.VMEM((rows, width), BF16),
            pltpu.VMEM((rows, width), BF16),
            pltpu.VMEM(small.shape, F32),
            pltpu.VMEM((rows, width), BF16),
            pltpu.VMEM((rows, width), F32),
            pltpu.SemaphoreType.DMA((slots, 2)),
            pltpu.SemaphoreType.DMA((slots, 6)),
            pltpu.SemaphoreType.DMA((5,)),
        ],
        compiler_params=pltpu.CompilerParams(vmem_limit_bytes=62 * MIB),
        name="widen",
    )(in_all, out_all, branches, d_hidden, tokens, cotangent, small)


def on_device(
    tokens, cotangent, block_order, positions, ln_gain, ln_bias, w_qkv, b_qkv, w_dense, b_dense,
    w_fc1, b_fc1, w_fc2, b_fc2,
):
    ctx, fsdp = lax.axis_size("ctx"), lax.axis_size("fsdp")
    f = lax.axis_index("fsdp")
    rows, width = tokens.shape[1:]
    seq = rows * ctx
    ff = w_fc1.shape[1]
    own_width, own_ff = width // ctx, ff // ctx
    own_rows = width // fsdp
    cut = 3 * own_width
    tokens = tokens.reshape(rows, width)
    cotangent = cotangent.reshape(rows, width)

    vectors = (ln_gain, ln_bias, b_dense, b_fc2, b_qkv, b_fc1)
    used = sum(vector.shape[0] for vector in vectors)
    small = jnp.concatenate(vectors + (jnp.zeros((32 * own_rows - used,), BF16),))
    small = small.reshape(32, own_rows)
    spread = turn_spread(own_width)
    (
        x_all, g_all, hidden, stat, queries, keys, values, d_att, act, d_up, w_in, w_out, turns, small,
    ) = first(
        tokens, cotangent, turn_rows(positions.reshape(rows), own_width), w_qkv, w_fc1, w_dense, w_fc2,
        small, spread, ctx, fsdp,
    )
    att, d_proj = attention(
        block_order, seq // block_order.shape[0], queries, keys, values, d_att,
        turns.reshape(seq, own_width), spread,
    )
    branches, d_hidden, in_all, out_all, vector = second(
        att, act, d_proj, d_up, w_in.reshape(width, -1), w_out, stat, cotangent, x_all, g_all, hidden,
        fsdp,
    )
    grad_qkv, grad_fc1, grad_dense, grad_fc2, result, input_grad = widen(
        in_all, out_all, branches, d_hidden, tokens, cotangent, small, ff
    )

    vector = vector.reshape(ctx, -1)
    sums = jnp.sum(vector[:, : 3 * width], axis=0).reshape(3, width)
    sums = lax.dynamic_slice_in_dim(sums, f * own_rows, own_rows, 1)
    columns = vector[:, 3 * width : 3 * width + cut].reshape(ctx, 3, own_width)
    columns = columns.transpose(1, 0, 2).reshape(3 * width)
    units = vector[:, 3 * width + cut : 3 * width + cut + own_ff].reshape(ff)
    return (
        result.reshape(1, rows, width),
        input_grad.reshape(1, rows, width),
        sums[0],
        sums[1],
        grad_qkv,
        lax.dynamic_slice_in_dim(columns, f * (3 * own_rows), 3 * own_rows, 0),
        grad_dense,
        sums[2],
        grad_fc1,
        lax.dynamic_slice_in_dim(units, f * (ff // fsdp), ff // fsdp, 0),
        grad_fc2,
        sums[2],
    )


def solution(mesh):
    split = P("fsdp", "ctx", None)
    matrix = P("fsdp", None)
    vector = P("fsdp")
    return jax.shard_map(
        on_device,
        mesh=mesh,
        in_specs=(split, split, P(), P("fsdp", "ctx"), vector, vector)
        + (matrix, vector) * 4,
        out_specs=(split, split, vector, vector) + (matrix, vector) * 4,
        check_vma=False,
    )
```

```python
import functools

import jax
import jax.numpy as jnp
import numpy as np
from jax import lax
from jax.experimental import pallas as pl
from jax.experimental.pallas import tpu as pltpu
from jax.sharding import PartitionSpec as P

HEAD_DIM = 64
ROTARY = 32
NORM_EPS = 1e-05
ROPE_BASE = 10000.0
GELU_COEF = 0.7978845608028654
F32 = jnp.float32
BF16 = jnp.bfloat16
STRIP = 256
NT = (((1,), (1,)), ((), ()))
TN = (((0,), (0,)), ((), ()))
MESH = pl.DeviceIdType.MESH
MIB = 1024 * 1024


def nt_dot(left, right):
    return lax.dot_general(left, right, NT, preferred_element_type=F32)


def tn_dot(left, right):
    return lax.dot_general(left, right, TN, preferred_element_type=F32)


def dot(left, right):
    return jnp.dot(left, right, preferred_element_type=F32)


def turn_rows(positions, width):
    half = ROTARY // 2
    frequency = ROPE_BASE ** (-(jnp.arange(half, dtype=F32) * (2.0 / ROTARY)))
    turned = positions.astype(F32)[:, None] * frequency
    both = jnp.concatenate([jnp.cos(turned), jnp.sin(turned)], axis=1)
    coarse = both.astype(BF16)
    fine = (both - coarse.astype(F32)).astype(BF16)
    rows = positions.shape[0]
    used = 4 * half + 1
    return jnp.concatenate(
        [coarse, fine, jnp.ones((rows, 1), BF16), jnp.zeros((rows, width - used), BF16)], axis=1
    )


def turn_spread(width):
    half = ROTARY // 2
    table = np.zeros((width, 3 * width), np.float32)
    for column in range(width):
        at = column % HEAD_DIM
        if at >= ROTARY:
            table[4 * half, column] = 1.0
            continue
        for part in (0, 2 * half):
            table[part + at % half, column] = 1.0
            if at < half:
                table[part + half + at, width + column] = -1.0
            else:
                table[part + half + at - half, 2 * width + column] = 1.0
    return jnp.asarray(table, BF16)


def turn(values, tables, back):
    width = values.shape[1]
    half = ROTARY // 2
    same, after, before = (tables[:, at * width : (at + 1) * width] for at in range(3))
    moved = pltpu.roll(values, width - half, 1) * after + pltpu.roll(values, half, 1) * before
    return values * same - moved if back else values * same + moved


AWAY = [(dx, flip) for dx in range(4) for flip in (False, True) if dx or flip]


def fold(left, right, first):
    lane = lax.broadcasted_iota(jnp.int32, left.shape, 1)
    half = left.shape[1] // 2
    return jnp.where(
        lane < half,
        jnp.where(first, left, pltpu.roll(left, half, 1)),
        jnp.where(first, pltpu.roll(right, half, 1), right),
    )


class Place:
    def __init__(self):
        self.c, self.f = lax.axis_index("ctx"), lax.axis_index("fsdp")
        self.y, self.z, self.core = self.c // 4, (self.c // 2) % 2, self.c % 2
        self.x, self.half = self.f // 2, self.f % 2

    def block(self, dy, flip, other=False):
        core = 1 - self.core if other else self.core
        return ((self.y + dy) % 4) * 4 + (1 - self.z if flip else self.z) * 2 + core

    def shard(self, dx, flip):
        return ((self.x + dx) % 4) * 2 + (1 - self.half if flip else self.half)

    def to_ctx(self, dy, flip, other=False):
        return (self.block(dy, flip, other), self.f)

    def to_fsdp(self, dx, flip):
        return (self.c, self.shard(dx, flip))

    def to_swap(self):
        return (2 * self.f + self.c % 2, self.c // 2)


class Post:
    def __init__(self, place, send, recv):
        self.place, self.send, self.recv, self.started = place, send, recv, []
        self.left = set()

    def copy(self, source, target, device):
        at = len(self.started)
        copy = pltpu.make_async_remote_copy(
            src_ref=source, dst_ref=target, send_sem=self.send.at[at], recv_sem=self.recv.at[at],
            device_id=device, device_id_type=MESH,
        )
        self.started.append(copy)
        copy.start()
        return copy

    def greet(self):
        place = self.place
        barrier = pltpu.get_barrier_semaphore()
        partners = [
            place.to_ctx(1, False), place.to_ctx(-1, False), place.to_ctx(0, True),
            place.to_ctx(0, False, True),
        ] + [place.to_fsdp(*to) for to in AWAY]
        for partner in partners:
            pl.semaphore_signal(barrier, inc=1, device_id=partner, device_id_type=MESH)
        swap = place.to_swap()
        same = jnp.logical_and(swap[0] == place.c, swap[1] == place.f)

        @pl.when(jnp.logical_not(same))
        def _():
            pl.semaphore_signal(barrier, inc=1, device_id=swap, device_id_type=MESH)

        pl.semaphore_wait(barrier, len(partners) + jnp.where(same, 0, 1))

    def has_left(self, copy):
        copy.wait_send()
        self.left.add(id(copy))

    def close(self):
        for copy in self.started:
            if id(copy) not in self.left:
                copy.wait_send()


def gather_ctx(post, own, buf, cut):
    place = post.place
    here = post.place.block(0, False)
    crossed = []

    def send(at, *to):
        return post.copy(buf.at[at], buf.at[at], place.to_ctx(*to))

    def cross(at):
        crossed.append(post.copy(buf.at[at], buf.at[at], place.to_ctx(0, False, True)))

    def first(*to):
        return post.copy(own, buf.at[here], place.to_ctx(*to))

    to_next, to_last, to_pair = first(1, False), first(-1, False), first(0, True)
    crossed.append(first(0, False, True))
    yield
    last, after = place.block(-1, False), place.block(1, False)
    rest = buf.shape[1] - cut
    lower, upper = pl.ds(0, cut), pl.ds(cut, rest)
    to_next.wait_recv()
    halves = [post.copy(buf.at[last, lower], buf.at[last, lower], place.to_ctx(1, False))]
    to_last.wait_recv()
    if rest:
        piece = buf.at[after, upper]
        halves.append(post.copy(piece, piece, place.to_ctx(-1, False)))
    cross(last)
    cross(after)
    yield
    to_pair.wait_recv()
    pair = place.block(0, True)
    pair_next, pair_last = send(pair, 1, False), send(pair, -1, False)
    cross(pair)
    yield
    for copy in halves:
        copy.wait_recv()
    far = place.block(2, False)
    pair_far = send(far, 0, True)
    cross(far)
    yield
    pair_next.wait_recv()
    cross(place.block(-1, True))
    pair_last.wait_recv()
    cross(place.block(1, True))
    yield
    pair_far.wait_recv()
    cross(place.block(2, True))
    yield
    for copy in crossed:
        copy.wait_recv()


def gather_fsdp(post, own, buf, cut):
    place = post.place
    here = place.shard(0, False)
    rest = buf.shape[1] - cut

    def whole(at, dx):
        return post.copy(buf.at[at], buf.at[at], place.to_fsdp(dx, False))

    def lower(at):
        piece = buf.at[at, pl.ds(0, cut)]
        return post.copy(piece, piece, place.to_fsdp(1, False))

    def upper(at):
        piece = buf.at[at, pl.ds(cut, rest)]
        return post.copy(piece, piece, place.to_fsdp(-1, False))

    to_pair = post.copy(own, buf.at[here], place.to_fsdp(0, True))
    to_next = post.copy(own, buf.at[here], place.to_fsdp(1, False))
    to_last = post.copy(own, buf.at[here], place.to_fsdp(-1, False))
    yield
    to_next.wait_recv()
    halves = [lower(place.shard(-1, False))]
    to_last.wait_recv()
    if rest:
        halves.append(upper(place.shard(1, False)))
    yield
    to_pair.wait_recv()
    pair = place.shard(0, True)
    pair_next, pair_last = whole(pair, 1), whole(pair, -1)
    yield
    pair_next.wait_recv()
    halves.append(lower(place.shard(-1, True)))
    pair_last.wait_recv()
    if rest:
        halves.append(upper(place.shard(1, True)))
    yield
    for copy in halves:
        copy.wait_recv()


def gather_direct(post, own, buf):
    place = post.place
    here = place.shard(0, False)
    copies = [post.copy(own, buf.at[here], place.to_fsdp(*to)) for to in AWAY]
    yield
    for copy in copies:
        copy.wait_recv()


class Swap:
    def __init__(self, place, source, target, send, recv, local):
        device = place.to_swap()
        self.same = jnp.logical_and(device[0] == place.c, device[1] == place.f)
        self.away = pltpu.make_async_remote_copy(
            src_ref=source, dst_ref=target, send_sem=send, recv_sem=recv, device_id=device,
            device_id_type=MESH,
        )
        self.stay = pltpu.make_async_copy(source, target, local)
        pl.when(jnp.logical_not(self.same))(lambda: self.away.start())
        pl.when(self.same)(lambda: self.stay.start())

    def wait(self):
        pl.when(jnp.logical_not(self.same))(lambda: self.away.wait())
        pl.when(self.same)(lambda: self.stay.wait())


def first_kernel(
    x_in, g_in, turn_in, w_qkv, w_fc1, w_dense, w_fc2, small_in, spread,
    x_to, g_to, hidden_to, stat_to, q_to, k_to, v_to, d_att_to, act_to, d_up_to, w_in_to, fc2_to,
    dense_to,
    turns_to, small_to,
    x_all, g_all, hidden, stat, q_out, k_out, v_out, d_att, act, d_up, w_in, fc2, dense,
    turns, small_out,
    wide_rows, in_rows, fc2_rows, dense_rows, piece, small_all, tables, proj, slope, vec, bias,
    send, recv, local, reads, swap_send, swap_recv,
):
    place = Place()
    post = Post(place, send, recv)
    rows, width = x_in.shape
    own_width = q_out.shape[1]
    own_ff = act.shape[1]
    cut = 3 * own_width
    here, shard = place.block(0, False), place.shard(0, False)

    def columns(first, count):
        return pl.ds(pl.multiple_of(first, 128), count)

    fsdp, fc2_step = fc2.shape[:2]
    dense_step = dense.shape[1]
    units = w_fc1.shape[1] // fsdp
    first_dense = (place.c % 2) * own_width + (place.c // 2) * dense_step
    first_fc2 = place.c * fc2_step
    sources = [
        (w_dense.at[pl.ds(pl.multiple_of(first_dense, 16), dense_step)], dense_rows),
        (w_fc2.at[pl.ds(pl.multiple_of(first_fc2, 16), fc2_step)], fc2_rows),
    ]
    for part in range(3):
        take = columns(part * width + place.c * own_width, own_width)
        sources.append((w_qkv.at[:, take], in_rows.at[:, pl.ds(part * own_width, own_width)]))
    for part in range(fsdp):
        take = columns(part * units + place.c // 2 * 128, 128)
        sources.append((w_fc1.at[:, take], wide_rows.at[:, pl.ds(part * 128, 128)]))
    ready = [
        pltpu.make_async_copy(source, target, reads.at[at])
        for at, (source, target) in enumerate(sources)
    ]
    for copy in ready:
        copy.start()
    post.greet()
    for copy in ready:
        copy.wait()
    swap = Swap(place, dense_rows, piece, swap_send, swap_recv, local.at[0])
    for part in range(fsdp // 2):
        left, right = (
            wide_rows[:, at * 128 : (at + 1) * 128].astype(F32) for at in (2 * part, 2 * part + 1)
        )
        in_rows[:, cut + part * 128 : cut + (part + 1) * 128] = fold(
            left, right, place.core == 0
        ).astype(BF16)
    keeps = []

    def keep(source, target):
        copy = pltpu.make_async_copy(source, target, local.at[1 + len(keeps)])
        keeps.append(copy)
        copy.start()
        return copy

    own = [
        keep(x_in, x_all.at[here]), keep(in_rows, w_in.at[shard]), keep(turn_in, turns.at[here]),
        keep(small_in, small_all.at[shard]), keep(g_in, g_all.at[here]),
        keep(fc2_rows, fc2.at[shard]),
    ]
    x_flow = gather_ctx(post, x_in, x_all, rows // 2)
    in_flow = gather_fsdp(post, in_rows, w_in, in_rows.shape[0] // 2)
    small_flow = gather_direct(post, small_in, small_all)
    turn_flow = gather_ctx(post, turn_in, turns, rows // 2)
    def advance(*flows):
        for flow in flows:
            next(flow, None)

    advance(x_flow, in_flow, small_flow, turn_flow)
    advance(x_flow, in_flow)
    g_flow = gather_ctx(post, g_in, g_all, rows // 2)
    fc2_flow = gather_fsdp(post, fc2_rows, fc2, fc2_step // 2)
    advance(g_flow, fc2_flow)
    swap.wait()
    keep(piece, dense.at[shard])
    dense_flow = gather_fsdp(post, piece, dense, dense_step)
    advance(dense_flow)
    advance(x_flow, in_flow, g_flow, turn_flow, fc2_flow, dense_flow)
    for _ in small_flow:
        pass
    for copy in own[:4]:
        copy.wait()

    side = small_all.shape[2]
    small_out[...] = small_all[...].astype(F32)
    for at in range(small_all.shape[0]):
        vec[0:2, at * side : (at + 1) * side] = small_out[at, 0:2, :]
    for part in range(3):
        first = part * width + place.c * own_width
        count = 3 * side
        row = small_out[first // count, pl.ds(4 + (first % count) // side, 1), :]
        bias[0:1, part * own_width : (part + 1) * own_width] = jnp.where(
            first % side == 0, row[:, :own_width], row[:, own_width:]
        )
    quarter = place.c % 4
    pieces = []
    for part in range(fsdp):
        row = small_out[part, pl.ds(7 + place.c // 4, 1), :]
        row = jnp.where(quarter >= 2, row[:, 128:], row[:, :128])
        pieces.append(jnp.broadcast_to(row, (8, 128)))
    for part in range(fsdp // 2):
        row = fold(pieces[2 * part], pieces[2 * part + 1], quarter % 2 == 0)
        bias[0:1, cut + part * 128 : cut + (part + 1) * 128] = row[0:1, :]

    def normalise(block):
        lane = lax.broadcasted_iota(jnp.int32, (rows, stat.shape[1]), 1)
        target = pl.ds(pl.multiple_of(block * rows, rows), rows)
        value = x_all[block].astype(F32)
        mean = jnp.mean(value, axis=1, keepdims=True)
        centred = value - mean
        inverse = lax.rsqrt(jnp.mean(centred * centred, axis=1, keepdims=True) + NORM_EPS)
        hidden[target, :] = (centred * inverse * vec[0:1, :] + vec[1:2, :]).astype(BF16)
        stat[target, :] = jnp.where(lane < HEAD_DIM, mean, inverse)

    def normalise_each(targets):
        order = [place.block(*to) for to in targets]

        def body(at, carry):
            block = order[0]
            for number, other in enumerate(order[1:]):
                block = jnp.where(at == number + 1, other, block)
            normalise(block)
            return carry

        lax.fori_loop(0, len(order), body, 0)

    normalise_each([(0, False), (1, False), (-1, False)])
    advance(x_flow, in_flow, g_flow, turn_flow, fc2_flow, dense_flow)
    normalise_each([(0, True)])
    advance(x_flow, in_flow, g_flow, turn_flow, fc2_flow, dense_flow)
    keep(w_in, w_in_to)
    normalise_each([(2, False), (1, True), (-1, True)])
    advance(x_flow, g_flow, turn_flow, fc2_flow, dense_flow)
    normalise_each([(2, True)])
    advance(x_flow, turn_flow)
    keep(x_all, x_to)
    normalise_each([(dy, flip, True) for dy in range(4) for flip in (False, True)])
    keep(hidden, hidden_to)
    keep(stat, stat_to)
    keep(small_out, small_to)
    advance(turn_flow)
    keep(turns, turns_to)

    chunk_rows = proj.shape[0]
    step = 64
    group = chunk_rows // rows

    def project(chunk, carry):
        take = pl.ds(pl.multiple_of(chunk * chunk_rows, chunk_rows), chunk_rows)
        weight = w_in[...].reshape(width, proj.shape[1])
        proj[...] = dot(hidden[take, :], weight)
        turned = turns[pl.ds(chunk * group, group)].reshape(chunk_rows, own_width)
        tables[...] = dot(turned, spread[...])

        def body(at, inner):
            source = pl.ds(pl.multiple_of(at * step, step), step)
            target = pl.ds(pl.multiple_of(chunk * chunk_rows + at * step, step), step)
            value = proj[source, :] + bias[0:1, :]
            table = tables[source, :]
            q_out[target, :] = turn(value[:, :own_width], table, False).astype(BF16)
            k_out[target, :] = turn(value[:, own_width : 2 * own_width], table, False).astype(BF16)
            v_out[target, :] = value[:, 2 * own_width : cut].astype(BF16)
            up = value[:, cut:]
            square = up * up
            curve = jnp.tanh(GELU_COEF * up * (1.0 + 0.044715 * square))
            act[target, :] = (0.5 * up * (1.0 + curve)).astype(BF16)
            slope[target, :] = 0.5 * (1.0 + curve) + 0.5 * up * (1.0 - curve * curve) * (
                GELU_COEF * (1.0 + 3.0 * 0.044715 * square)
            )
            return inner

        lax.fori_loop(0, chunk_rows // step, body, 0)
        return carry

    chunks = hidden.shape[0] // chunk_rows
    project(0, 0)
    project(1, 0)
    advance(g_flow)
    project(2, 0)
    project(3, 0)
    for target, source in ((q_to, q_out), (k_to, k_out), (v_to, v_out), (act_to, act)):
        keep(source, target)
    advance(fc2_flow, dense_flow)
    own[5].wait()
    keeps[6].wait()
    keep(fc2, fc2_to)
    keep(dense, dense_to)
    advance(g_flow)
    own[4].wait()
    keep(g_all, g_to)

    def back(chunk, carry):
        grads = g_all[pl.ds(chunk * group, group)].reshape(chunk_rows, width)
        proj[:, :own_width] = nt_dot(grads, dense[...].reshape(own_width, width))
        proj[:, own_width : own_width + own_ff] = nt_dot(grads, fc2[...].reshape(own_ff, width))

        def body(at, inner):
            source = pl.ds(pl.multiple_of(at * step, step), step)
            target = pl.ds(pl.multiple_of(chunk * chunk_rows + at * step, step), step)
            d_att[target, :] = proj[source, :own_width].astype(BF16)
            d_act = proj[source, own_width : own_width + own_ff]
            d_up[target, :] = (d_act * slope[target, :]).astype(BF16)
            return inner

        lax.fori_loop(0, chunk_rows // step, body, 0)
        return carry

    lax.fori_loop(0, chunks, back, 0)
    keep(d_att, d_att_to)
    keep(d_up, d_up_to)
    for copy in keeps[7:]:
        copy.wait()
    post.close()


def first(tokens, cotangent, turns, w_qkv, w_fc1, w_dense, w_fc2, small, spread, ctx, fsdp):
    rows, width = tokens.shape
    seq = ctx * rows
    own_width, own_ff = turns.shape[1], w_fc1.shape[1] // ctx
    columns = 3 * own_width + own_ff
    side = width // fsdp
    many = 3 * 16 + 3 * 9 + fsdp - 1
    any_, vmem = pl.BlockSpec(memory_space=pl.ANY), pl.BlockSpec(memory_space=pltpu.VMEM)

    def low(*shape):
        return jax.ShapeDtypeStruct(shape, BF16)

    def wide(*shape):
        return jax.ShapeDtypeStruct(shape, F32)

    outs = [
        low(ctx, rows, width), low(ctx, rows, width), low(seq, width), wide(seq, 128),
        low(seq, own_width), low(seq, own_width), low(seq, own_width), low(seq, own_width),
        low(seq, own_ff), low(seq, own_ff), low(fsdp, side, columns),
        low(fsdp, own_ff // fsdp, width), low(fsdp, own_width // fsdp, width),
        low(ctx, rows, own_width), wide(*((fsdp,) + small.shape)),
    ]
    chunk_rows = 4 * rows
    return pl.pallas_call(
        first_kernel,
        out_shape=tuple(outs),
        in_specs=[any_] * 8 + [vmem],
        out_specs=(any_,) * len(outs),
        scratch_shapes=[pltpu.VMEM(out.shape, out.dtype) for out in outs]
        + [
            pltpu.VMEM((side, fsdp * 128), BF16),
            pltpu.VMEM((side, columns), BF16),
            pltpu.VMEM((own_ff // fsdp, width), BF16),
            pltpu.VMEM((own_width // fsdp, width), BF16),
            pltpu.VMEM((own_width // fsdp, width), BF16),
            pltpu.VMEM((fsdp,) + small.shape, BF16),
            pltpu.VMEM((chunk_rows, 3 * own_width), F32),
            pltpu.VMEM((chunk_rows, columns), F32),
            pltpu.VMEM((seq, own_ff), F32),
            pltpu.VMEM((8, width), F32),
            pltpu.VMEM((8, columns), F32),
            pltpu.SemaphoreType.DMA((many,)),
            pltpu.SemaphoreType.DMA((many,)),
            pltpu.SemaphoreType.DMA((24,)),
            pltpu.SemaphoreType.DMA((5 + fsdp,)),
            pltpu.SemaphoreType.DMA,
            pltpu.SemaphoreType.DMA,
        ],
        compiler_params=pltpu.CompilerParams(
            collective_id=0, has_side_effects=True, vmem_limit_bytes=60 * MIB
        ),
        name="first",
    )(tokens, cotangent, turns, w_qkv, w_fc1, w_dense, w_fc2, small, spread)


def attention_kernel(
    block, order, q_hbm, k_hbm, v_hbm, g_hbm, turns_hbm, spread, o_to, d_to,
    q_in, k_in, v_in, g_in, turns, o_out, d_out, loads, qs, ks, vs, gs, os, dqs, dks, dvs, kt, vt, table,
):
    rows, width = q_in.shape
    blocks = rows // block
    reads = [
        pltpu.make_async_copy(source, target, loads.at[at])
        for at, (source, target) in enumerate(
            [(q_hbm, q_in), (k_hbm, k_in), (v_hbm, v_in), (g_hbm, g_in), (turns_hbm, turns)]
        )
    ]
    for copy in reads:
        copy.start()
    for copy in reads[:4]:
        copy.wait()

    def collect(at, carry):
        src = pl.ds(pl.multiple_of(at * block, block), block)
        dst = pl.ds(pl.multiple_of(order[at] * block, block), block)
        qs[dst, :] = q_in[src, :]
        ks[dst, :] = k_in[src, :]
        vs[dst, :] = v_in[src, :]
        gs[dst, :] = g_in[src, :]
        return carry

    lax.fori_loop(0, blocks, collect, 0, unroll=4)
    dks[...] = jnp.zeros_like(dks)
    dvs[...] = jnp.zeros_like(dvs)
    heads = width // HEAD_DIM
    scale = HEAD_DIM ** (-0.5)
    q_pos = lax.broadcasted_iota(jnp.int32, (STRIP, STRIP), 0)
    k_pos = lax.broadcasted_iota(jnp.int32, (STRIP, STRIP), 1)
    diagonal = q_pos <= k_pos
    reads[4].wait()
    table[...] = dot(turns[...], spread[...])
    kt[...] = ks[...].T
    vt[...] = vs[...].T
    sides = [slice(head * HEAD_DIM, (head + 1) * HEAD_DIM) for head in range(heads)]
    strips = rows // STRIP

    def begin(strip):
        here = slice(strip * STRIP, (strip + 1) * STRIP)
        count = (strip + 1) * STRIP
        query = [qs[here, cols] * jnp.asarray(scale, BF16) for cols in sides]
        part = [nt_dot(ks[:count, cols], query[h]) for h, cols in enumerate(sides)]
        return query, part

    ready = begin(0)
    for strip in range(strips):
        here = slice(strip * STRIP, (strip + 1) * STRIP)
        count = (strip + 1) * STRIP
        query, part = ready
        edge = [jnp.where(diagonal, p[count - STRIP :, :], -1e30) for p in part]
        part = [jnp.concatenate([p[: count - STRIP, :], e], axis=0) if strip else e for p, e in zip(part, edge)]
        part = [jnp.exp(p - jnp.max(p, axis=0, keepdims=True)) for p in part]
        inverse = [1.0 / jnp.sum(p, axis=0, keepdims=True) for p in part]
        low = [p.astype(BF16) for p in part]
        mixed = [dot(vt[cols, :count], low[h]) * inverse[h] for h, cols in enumerate(sides)]
        grad = [gs[here, cols].astype(F32).T * inverse[h] for h, cols in enumerate(sides)]
        centre = [jnp.sum(g * m, axis=0, keepdims=True) for g, m in zip(grad, mixed)]
        os[here, :] = jnp.concatenate(mixed, axis=0).T.astype(BF16)
        grad = [g.astype(BF16) for g in grad]
        if strip + 1 < strips:
            ready = begin(strip + 1)
        d_score = [(part[h] * (dot(vs[:count, cols], grad[h]) - centre[h])).astype(BF16) for h, cols in enumerate(sides)]
        dqs[here, :] = jnp.concatenate([dot(kt[cols, :count], d_score[h]) for h, cols in enumerate(sides)], axis=0).T * scale
        dks[:count, :] += jnp.concatenate([dot(d_score[h], query[h]) for h in range(heads)], axis=1)
        dvs[:count, :] += jnp.concatenate([nt_dot(low[h], grad[h]) for h in range(heads)], axis=1)

    def give(at, carry):
        src = pl.ds(pl.multiple_of(order[at] * block, block), block)
        dst = pl.ds(pl.multiple_of(at * block, block), block)
        tables = table[dst, :]
        o_out[dst, :] = os[src, :]
        d_out[dst, :width] = turn(dqs[src, :], tables, True).astype(BF16)
        d_out[dst, width : 2 * width] = turn(dks[src, :], tables, True).astype(BF16)
        d_out[dst, 2 * width :] = dvs[src, :].astype(BF16)
        return carry

    writes = []
    parts = 4
    for part in range(parts):
        lax.fori_loop(part * blocks // parts, (part + 1) * blocks // parts, give, 0, unroll=4)
        take = pl.ds(part * rows // parts, rows // parts)
        for number, (source, target) in enumerate(((o_out, o_to), (d_out, d_to))):
            copy = pltpu.make_async_copy(
                source.at[take], target.at[take], loads.at[5 + 2 * part + number]
            )
            copy.start()
            writes.append(copy)
    for copy in writes:
        copy.wait()


def attention(order, block, queries, keys, values, grads, turns, spread):
    rows, width = queries.shape
    vmem = pl.BlockSpec(memory_space=pltpu.VMEM)
    smem = pl.BlockSpec(memory_space=pltpu.SMEM)
    any_ = pl.BlockSpec(memory_space=pl.ANY)
    return pl.pallas_call(
        functools.partial(attention_kernel, block),
        out_shape=(
            jax.ShapeDtypeStruct((rows, width), BF16),
            jax.ShapeDtypeStruct((rows, 3 * width), BF16),
        ),
        in_specs=[smem] + [any_] * 5 + [vmem],
        out_specs=(any_, any_),
        scratch_shapes=[pltpu.VMEM((rows, width), BF16)] * 6
        + [pltpu.VMEM((rows, 3 * width), BF16), pltpu.SemaphoreType.DMA((13,))]
        + [pltpu.VMEM((rows, width), BF16)] * 5
        + [pltpu.VMEM((rows, width), F32)] * 3
        + [pltpu.VMEM((width, rows), BF16), pltpu.VMEM((width, rows), BF16)]
        + [pltpu.VMEM((rows, 3 * width), F32)],
        compiler_params=pltpu.CompilerParams(vmem_limit_bytes=60 * MIB),
        cost_estimate=pl.CostEstimate(
            flops=6 * rows * rows * width,
            bytes_accessed=rows * width * 22,
            transcendentals=rows * rows * width // HEAD_DIM // 2,
        ),
        name="attention",
    )(order, queries, keys, values, grads, turns, spread)


ORDER = [(2, True), (1, True), (-1, True), (2, False), (0, True), (1, False), (-1, False), (0, False)]
SHARDS = [(2, True), (2, False), (1, True), (-1, True), (1, False), (-1, False), (0, True), (0, False)]


def add_into(target, *parts):
    step = 64 if target.shape[0] % 64 == 0 else 16
    plain = len(parts) == 2 and target.dtype == BF16

    def body(at, carry):
        take = pl.ds(pl.multiple_of(at * step, step), step)
        if plain:
            target[take, :] = parts[0][take, :] + parts[1][take, :]
            return carry
        total = parts[0][take, :].astype(F32)
        for part in parts[1:]:
            total = total + part[take, :].astype(F32)
        target[take, :] = total.astype(target.dtype)
        return carry

    lax.fori_loop(0, target.shape[0] // step, body, 0)


def reduce_ctx(post, own, core, crossed, pair_in, half_in, ring_in, cross_in, last_in, total):
    place = post.place
    cut = half_in.shape[1]
    up, down, pair = place.to_ctx(1, False), place.to_ctx(-1, False), place.to_ctx(0, True)

    def meet(at, *more):
        crossed[at].wait_recv()
        add_into(core.at[at], own.at[at], core.at[at], *more)

    meet(0)
    far = post.copy(core.at[0], pair_in, pair)
    yield
    meet(1)
    cross_next = post.copy(core.at[1], cross_in.at[0], up)
    meet(2)
    cross_last = post.copy(core.at[2], cross_in.at[1], down)
    yield
    far.wait_recv()
    meet(3, pair_in)
    low = post.copy(core.at[3, pl.ds(0, cut)], half_in.at[0], up)
    high = post.copy(core.at[3, pl.ds(cut, cut)], half_in.at[1], down)
    yield
    cross_next.wait_recv()
    cross_last.wait_recv()
    meet(4, cross_in.at[0], cross_in.at[1])
    last = post.copy(core.at[4], last_in, pair)
    yield
    meet(5)
    low.wait_recv()
    lower = core.at[5, pl.ds(0, cut)]
    add_into(lower, lower, half_in.at[0])
    ring_next = post.copy(core.at[5], ring_in.at[0], up)
    meet(6)
    high.wait_recv()
    upper = core.at[6, pl.ds(cut, cut)]
    add_into(upper, upper, half_in.at[1])
    ring_last = post.copy(core.at[6], ring_in.at[1], down)
    yield
    crossed[7].wait_recv()
    last.wait_recv()
    ring_next.wait_recv()
    ring_last.wait_recv()
    add_into(total, own.at[7], core.at[7], ring_in.at[0], ring_in.at[1], last_in)


def reduce_fsdp(post, part, low_in, high_in, ring_in, pair_in, total):
    place = post.place
    cut, rest = low_in.shape[1], high_in.shape[1]
    lower, upper = pl.ds(0, cut), pl.ds(cut, rest)
    up, down, pair = place.to_fsdp(1, False), place.to_fsdp(-1, False), place.to_fsdp(0, True)
    halves = [
        (
            post.copy(part.at[side, lower], low_in.at[side], up),
            post.copy(part.at[side, upper], high_in.at[side], down),
        )
        for side in range(2)
    ]
    yield
    rings = []
    for side in range(2):
        low, high = halves[side]
        after, before = part.at[2 + 2 * side], part.at[3 + 2 * side]
        low.wait_recv()
        add_into(after.at[lower], after.at[lower], low_in.at[side])
        to_next = post.copy(after, ring_in.at[side, 0], up)
        high.wait_recv()
        add_into(before.at[upper], before.at[upper], high_in.at[side])
        to_last = post.copy(before, ring_in.at[side, 1], down)
        rings.append((to_next, to_last))
        yield
    for copy in rings[0]:
        copy.wait_recv()
    add_into(part.at[6], part.at[6], ring_in.at[0, 0], ring_in.at[0, 1])
    across = post.copy(part.at[6], pair_in, pair)
    yield
    for copy in rings[1]:
        copy.wait_recv()
    across.wait_recv()
    add_into(total, part.at[7], ring_in.at[1, 0], ring_in.at[1, 1], pair_in)


def run(*flows):
    flows = list(flows)
    while flows:
        flows = [flow for flow in flows if next(flow, flows) is not flows]


def second_kernel(
    att_in, act_in, d_proj_in, d_up_in, w_in_in, w_fc2_in, w_dense_in, stat_in, g_own_in, x_all, g_all, hidden,
    out_total, hid_total, in_all, fc2_all, dense_all, vector_all,
    att, act, d_proj, d_up, w_in, w_fc2, w_dense, stat, g_own,
    own_a, own_b, core_a, core_b, slot_a, slot_b,
    pair_a, half_a, ring_a, cross_a, last_a, pair_b, half_b, ring_b, cross_b, last_b,
    in_part, in_low, in_high, in_ring, in_pair, in_sum,
    out_part, out_low, out_high, out_ring, out_pair, out_sum, out_piece,
    column, x_block, total_a, total_b, gain_sum, shift_sum,
    vector, vector_shards, vector_sum,
    send, recv, local, loads, reads, swap_send, swap_recv,
):
    place = Place()
    post = Post(place, send, recv)
    rows, width = g_own.shape
    cut = d_proj.shape[1]
    side = in_part.shape[1]
    here, shard = place.block(0, False), place.shard(0, False)
    keeps, numbers = [], iter(range(7))

    def keep(source, target):
        copy = pltpu.make_async_copy(source, target, local.at[next(numbers)])
        keeps.append(copy)
        copy.start()
        return copy

    operands = [
        pltpu.make_async_copy(source, target, reads.at[at])
        for at, (source, target) in enumerate(
            [
                (d_proj_in, d_proj), (d_up_in, d_up), (att_in, att), (act_in, act), (w_fc2_in, w_fc2),
                (w_dense_in, w_dense),
                (w_in_in, w_in), (stat_in, stat), (g_own_in, g_own),
            ]
        )
    ]

    def load_x(at):
        dy, flip = ORDER[at]
        block = place.block(dy, flip) // 2
        copy = pltpu.make_async_copy(
            x_all.at[pl.ds(2 * block, 2)], x_block.at[at % 2], loads.at[at % 2]
        )
        copy.start()
        return copy

    ahead = column.shape[0]

    def load_column(at):
        if at < len(SHARDS):
            first = pl.multiple_of(place.shard(*SHARDS[at]) * side, side)
            source = hidden.at[:, pl.ds(first, side)]
        else:
            source = g_all.at[:, pl.ds((at - len(SHARDS)) * side, side)]
        copy = pltpu.make_async_copy(source, column.at[at % ahead], loads.at[2 + at % ahead])
        copy.start()
        return copy

    for copy in operands[:2]:
        copy.start()
    pending_column = [load_column(at) for at in range(ahead - 1)]
    pending_x = [load_x(0)]
    for copy in operands[2:]:
        copy.start()
    post.greet()
    gain_sum[...] = jnp.zeros_like(gain_sum)
    shift_sum[...] = jnp.zeros_like(shift_sum)
    crossed_a, crossed_b, slots = {}, {}, {}
    partner = place.to_ctx(0, False, True)
    depth = slot_a.shape[0]

    def produce(at):
        dy, flip = ORDER[at]
        block = place.block(dy, flip) // 2
        pending_x.pop().wait()
        if at + 1 < len(ORDER):
            pending_x.append(load_x(at + 1))
        slot = at % depth
        if at >= depth:
            for copy in slots[at - depth]:
                post.has_left(copy)
        other_rows = pl.ds(pl.multiple_of(block * (2 * rows) + (1 - place.core) * rows, rows), rows)
        own_rows = pl.ds(pl.multiple_of(block * (2 * rows) + place.core * rows, rows), rows)

        def both(ref):
            return jnp.concatenate([ref[other_rows, :], ref[own_rows, :]], axis=0)

        left, right = both(att), both(act)
        span = width // 2
        for first in range(0, width, span):
            take = slice(first, first + span)
            value = dot(left, w_dense[:, take]) + dot(right, w_fc2[:, take])
            slot_a[slot, :, take] = value[:rows].astype(BF16)
            own_a[at, :, take] = value[rows:].astype(BF16)
        left, right, stats = both(d_proj), both(d_up), both(stat)
        mean, inverse = stats[:, 0:1], stats[:, HEAD_DIM : HEAD_DIM + 1]
        span = width // 4
        for first in range(0, width, span):
            take = slice(first, first + span)
            value = nt_dot(left, w_in[take, :cut]) + nt_dot(right, w_in[take, cut:])
            slot_b[slot, :, take] = value[:rows].astype(BF16)
            own_b[at, :, take] = value[rows:].astype(BF16)
            tokens = jnp.concatenate(
                [x_block[at % 2, 1 - place.core, :, take], x_block[at % 2, place.core, :, take]],
                axis=0,
            )
            normed = (tokens.astype(F32) - mean) * inverse
            parts = (2 * rows // 8, 8, span)
            gain_sum[:, take] += jnp.sum((value * normed).reshape(parts), axis=0)
            shift_sum[:, take] += jnp.sum(value.reshape(parts), axis=0)
        crossed_a[at] = post.copy(slot_a.at[slot], core_a.at[at], partner)
        crossed_b[at] = post.copy(slot_b.at[slot], core_b.at[at], partner)
        slots[at] = (crossed_a[at], crossed_b[at])

    def next_column(at):
        pending_column.pop(0).wait()
        if at + ahead - 1 < 2 * len(SHARDS):
            pending_column.append(load_column(at + ahead - 1))
        return column[at % ahead]

    def grad_in(at):
        rows_of = next_column(at)
        in_part[at, :, :cut] = tn_dot(rows_of, d_proj[...]).astype(BF16)
        in_part[at, :, cut:] = tn_dot(rows_of, d_up[...]).astype(BF16)

    def grad_out(at):
        columns = next_column(len(SHARDS) + at)
        take = slice(at * side, (at + 1) * side)
        dense = tn_dot(att[...], columns).astype(BF16)
        fc2 = tn_dot(act[...], columns).astype(BF16)
        dense_step, fc2_step = dense.shape[0] // len(SHARDS), fc2.shape[0] // len(SHARDS)
        for to in range(len(SHARDS)):
            out_part[to, :dense_step, take] = dense[to * dense_step : (to + 1) * dense_step]
            out_part[to, dense_step:, take] = fc2[to * fc2_step : (to + 1) * fc2_step]

    class ByShard:
        @property
        def at(self):
            return self

        def __getitem__(self, index):
            if isinstance(index, tuple):
                return out_part.at[(place.shard(*SHARDS[index[0]]),) + index[1:]]
            return out_part.at[place.shard(*SHARDS[index])]

    def in_flow():
        yield from reduce_fsdp(post, in_part, in_low, in_high, in_ring, in_pair, in_sum)
        keep(in_sum, in_all.at[here])
        yield from gather_ctx(post, in_sum, in_all, in_sum.shape[0] // 2)

    def out_flow():
        yield from reduce_fsdp(post, ByShard(), out_low, out_high, out_ring, out_pair, out_sum)
        first, count = dense_all.shape[1], fc2_all.shape[1]
        swap = Swap(
            place, out_sum.at[pl.ds(0, first)], out_piece, swap_send, swap_recv, local.at[7]
        )
        fc2_own = out_sum.at[pl.ds(first, count)]
        keep(fc2_own, fc2_all.at[here])
        flows = [gather_ctx(post, fc2_own, fc2_all, count // 2)]
        next(flows[0])
        yield
        next(flows[0])
        swap.wait()
        keep(out_piece, dense_all.at[here])
        flows.append(gather_ctx(post, out_piece, dense_all, first))
        while flows:
            flows = [flow for flow in flows if next(flow, flows) is not flows]
            yield

    def vector_flow():
        mine = keep(vector, vector_shards.at[shard])
        yield from gather_fsdp(post, vector, vector_shards, 8)
        mine.wait()
        keeps[:] = [kept for kept in keeps if kept is not mine]
        total = vector_shards[0]
        for at in range(1, vector_shards.shape[0]):
            total = total + vector_shards[at]
        vector_sum[...] = total
        keep(vector_sum, vector_all.at[here])
        yield from gather_ctx(post, vector_sum, vector_all, 8)

    def rows_flow(own, core, crossed, pair, half, ring, cross, last, total, target):
        yield from reduce_ctx(post, own, core, crossed, pair, half, ring, cross, last, total)
        keep(total, target)

    ins, outs = in_flow(), out_flow()
    a = rows_flow(
        own_a, core_a, crossed_a, pair_a, half_a, ring_a, cross_a, last_a, total_a, out_total
    )
    b = rows_flow(
        own_b, core_b, crossed_b, pair_b, half_b, ring_b, cross_b, last_b, total_b, hid_total
    )

    def both_next():
        next(a)
        next(b)

    for copy in operands[:2]:
        copy.wait()
    grad_in(0)
    grad_in(1)
    next(ins)
    for copy in operands[2:]:
        copy.wait()
    produce(0)
    produce(1)
    both_next()
    produce(2)
    both_next()
    for at in range(2, 8):
        grad_in(at)
    produce(3)
    next(ins)
    next(ins)
    for at in range(8):
        grad_out(at)
    next(outs)
    both_next()
    produce(4)
    next(ins)
    produce(5)
    both_next()
    produce(6)
    next(ins)
    next(outs)
    both_next()
    next(outs)
    produce(7)

    half = vector.shape[1]
    ones = jnp.ones((16, att.shape[0]), BF16)
    columns = jnp.concatenate([dot(ones, d_proj[...])[:1], dot(ones, d_up[...])[:1]], axis=1)
    vector[...] = jnp.zeros_like(vector)
    sums = [
        jnp.sum(gain_sum[...], axis=0, keepdims=True),
        jnp.sum(shift_sum[...], axis=0, keepdims=True),
        dot(ones[:, :rows], g_own[...])[:1],
    ]
    for at, row in enumerate(sums):
        vector[2 * at : 2 * at + 1, :] = row[:, :half]
        vector[2 * at + 1 : 2 * at + 2, :] = row[:, half:]
    vector[6:7, : columns.shape[1]] = columns
    vectors = vector_flow()
    next(vectors)
    run(ins, outs, a, b, vectors)

    for kept in keeps:
        kept.wait()
    post.close()


def second(att, act, d_proj, d_up, w_in, w_fc2, w_dense, stat, cotangent, x_all, g_all, hidden, fsdp):
    rows, width = cotangent.shape
    ctx = x_all.shape[0]
    side = width // fsdp
    in_columns = w_in.shape[1]
    fc2_rows, dense_rows = w_fc2.shape[0] // fsdp, w_dense.shape[0] // fsdp
    out_rows = fc2_rows + dense_rows
    any_ = pl.BlockSpec(memory_space=pl.ANY)

    def low(*shape):
        return pltpu.VMEM(shape, BF16)

    def wide(*shape):
        return pltpu.VMEM(shape, F32)

    def ctx_slots():
        return [
            low(rows, width), low(2, rows // 2, width), low(2, rows, width), low(2, rows, width),
            low(rows, width),
        ]

    def fsdp_slots(depth, columns, cut):
        return [
            low(fsdp, depth, columns), low(2, cut, columns), low(2, depth - cut, columns),
            low(2, 2, depth, columns), low(depth, columns), low(depth, columns),
        ]

    vector = (16, width // 2)
    many = 2 * 16 + 2 * 9 + 3 * 16 + 9 + 16
    ahead = 4
    operands = (att, act, d_proj, d_up, w_in, w_fc2, w_dense, stat, cotangent)
    return pl.pallas_call(
        second_kernel,
        out_shape=(
            jax.ShapeDtypeStruct((rows, width), F32),
            jax.ShapeDtypeStruct((rows, width), F32),
            jax.ShapeDtypeStruct((ctx, side, in_columns), BF16),
            jax.ShapeDtypeStruct((ctx, fc2_rows, width), BF16),
            jax.ShapeDtypeStruct((ctx, dense_rows, width), BF16),
            jax.ShapeDtypeStruct((ctx,) + vector, F32),
        ),
        in_specs=[any_] * 12,
        out_specs=(any_,) * 6,
        scratch_shapes=[pltpu.VMEM(operand.shape, operand.dtype) for operand in operands]
        + [low(ctx // 2, rows, width)] * 4
        + [low(2, rows, width)] * 2
        + ctx_slots()
        + ctx_slots()
        + fsdp_slots(side, in_columns, side // 2)
        + fsdp_slots(out_rows, width, 48)
        + [low(dense_rows, width)]
        + [
            low(ahead, ctx * rows, side), low(2, 2, rows, width), wide(rows, width),
            wide(rows, width), wide(8, width), wide(8, width),
            wide(*vector), wide(fsdp, *vector), wide(*vector),
            pltpu.SemaphoreType.DMA((many,)),
            pltpu.SemaphoreType.DMA((many,)),
            pltpu.SemaphoreType.DMA((8,)),
            pltpu.SemaphoreType.DMA((2 + ahead,)),
            pltpu.SemaphoreType.DMA((len(operands),)),
            pltpu.SemaphoreType.DMA,
            pltpu.SemaphoreType.DMA,
        ],
        compiler_params=pltpu.CompilerParams(
            collective_id=1, has_side_effects=True, vmem_limit_bytes=63 * MIB
        ),
        name="second",
    )(*operands, x_all, g_all.reshape(ctx * rows, width), hidden)


def widen_kernel(
    in_all, fc2_all, dense_all, branches_in, d_hidden_in, x_in, g_in, small_in,
    qkv, fc1, dense, fc2, result_to, input_grad_to,
    in_low, fc2_low, dense_low, qkv_wide, fc1_wide, fc2_wide, dense_wide,
    vec, branches, d_hidden, x_own, g_own, small, result, input_grad, loads, stores, reads,
):
    count = in_all.shape[0] // 2
    slots = in_low.shape[0]
    own = qkv.shape[1] // 3 // count
    units = fc1.shape[1] // count
    fc2_step, dense_step = fc2.shape[0] // count, dense.shape[0] // count // 2
    cut = 3 * own // 2

    def load(at):
        slot = at % slots
        copies = [
            pltpu.make_async_copy(source.at[pl.ds(2 * at, 2)], target.at[slot], loads.at[slot, number])
            for number, (source, target) in enumerate(
                [(in_all, in_low), (fc2_all, fc2_low), (dense_all, dense_low)]
            )
        ]
        for copy in copies:
            copy.start()
        return copies

    ahead = [load(at) for at in range(slots - 1)]
    stored = []
    own_rows = [
        pltpu.make_async_copy(source, target, reads.at[at])
        for at, (source, target) in enumerate(
            [
                (branches_in, branches), (d_hidden_in, d_hidden), (x_in, x_own), (g_in, g_own),
                (small_in, small),
            ]
        )
    ]
    for copy in own_rows:
        copy.start()

    side = small.shape[2]

    def finish():
        take = slice(None)
        token = x_own[take, :].astype(F32)
        result[take, :] = (token + branches[take, :] + vec[2:3, :] + vec[3:4, :]).astype(BF16)
        centred = token - jnp.mean(token, axis=1, keepdims=True)
        inverse = lax.rsqrt(jnp.mean(centred * centred, axis=1, keepdims=True) + NORM_EPS)
        normed = centred * inverse
        scaled = d_hidden[take, :] * vec[0:1, :]
        input_grad[take, :] = g_own[take, :].astype(F32) + inverse * (
            scaled
            - jnp.mean(scaled, axis=1, keepdims=True)
            - normed * jnp.mean(scaled * normed, axis=1, keepdims=True)
        )

    for at in range(count):
        slot = at % slots
        for copy in ahead[at]:
            copy.wait()
        if at + slots - 1 < count:
            ahead.append(load(at + slots - 1))
        if at >= slots:
            for copy in stored[at - slots]:
                copy.wait()
        half = own // 2
        for core in range(2):
            for part in range(3):
                first = part * own + core * half
                qkv_wide[slot, :, first : first + half] = in_low[
                    slot, core, :, part * half : (part + 1) * half
                ].astype(F32)
            fc2_wide[slot, core * (fc2_step // 2) : (core + 1) * (fc2_step // 2), :] = fc2_low[
                slot, core
            ].astype(F32)
            dense_wide[slot, core] = dense_low[slot, core].astype(F32)
        for part in range(count // 2):
            first = cut + part * 128
            left = in_low[slot, 0, :, first : first + 128].astype(F32)
            right = in_low[slot, 1, :, first : first + 128].astype(F32)
            fc1_wide[slot, :, 2 * part * 128 : (2 * part + 1) * 128] = fold(left, right, True)
            fc1_wide[slot, :, (2 * part + 1) * 128 : (2 * part + 2) * 128] = fold(left, right, False)
        targets = [
            (
                qkv_wide.at[slot, :, pl.ds(part * own, own)],
                qkv.at[:, pl.ds((part * count + at) * own, own)],
            )
            for part in range(3)
        ] + [
            (
                fc1_wide.at[slot, :, pl.ds(part * 128, 128)],
                fc1.at[:, pl.ds(part * units + at * 128, 128)],
            )
            for part in range(count)
        ] + [
            (fc2_wide.at[slot], fc2.at[pl.ds(at * fc2_step, fc2_step)]),
        ] + [
            (
                dense_wide.at[slot, core],
                dense.at[pl.ds((core * count + at) * dense_step, dense_step)],
            )
            for core in range(2)
        ]
        copies = [
            pltpu.make_async_copy(source, target, stores.at[slot, number])
            for number, (source, target) in enumerate(targets)
        ]
        for copy in copies:
            copy.start()
        stored.append(copies)
        if at == 2:
            for copy in own_rows:
                copy.wait()
            for shard in range(small.shape[0]):
                vec[0:4, shard * side : (shard + 1) * side] = small[shard, 0:4, :]
            finish()
    writes = [
        pltpu.make_async_copy(result, result_to, reads.at[0]),
        pltpu.make_async_copy(input_grad, input_grad_to, reads.at[1]),
    ]
    for copy in writes:
        copy.start()
    for copies in stored[-slots:]:
        for copy in copies:
            copy.wait()
    for copy in writes:
        copy.wait()


def widen(in_all, fc2_all, dense_all, branches, d_hidden, tokens, cotangent, small, ff):
    any_ = pl.BlockSpec(memory_space=pl.ANY)
    rows, width = tokens.shape
    fsdp = small.shape[0]
    slots = 3
    side = width // fsdp
    shapes = [(side, 3 * width), (side, ff), (side, width), (ff // fsdp, width)]
    return pl.pallas_call(
        widen_kernel,
        out_shape=tuple(jax.ShapeDtypeStruct(shape, F32) for shape in shapes)
        + (jax.ShapeDtypeStruct((rows, width), BF16), jax.ShapeDtypeStruct((rows, width), F32)),
        in_specs=[any_] * 8,
        out_specs=(any_,) * 6,
        scratch_shapes=[
            pltpu.VMEM((slots, 2) + in_all.shape[1:], BF16),
            pltpu.VMEM((slots, 2) + fc2_all.shape[1:], BF16),
            pltpu.VMEM((slots, 2) + dense_all.shape[1:], BF16),
            pltpu.VMEM((slots, side, 3 * width // fsdp), F32),
            pltpu.VMEM((slots, side, ff // fsdp), F32),
            pltpu.VMEM((slots, ff // fsdp // fsdp, width), F32),
            pltpu.VMEM((slots, 2) + dense_all.shape[1:], F32),
            pltpu.VMEM((8, width), F32),
            pltpu.VMEM((rows, width), F32),
            pltpu.VMEM((rows, width), F32),
            pltpu.VMEM((rows, width), BF16),
            pltpu.VMEM((rows, width), BF16),
            pltpu.VMEM(small.shape, F32),
            pltpu.VMEM((rows, width), BF16),
            pltpu.VMEM((rows, width), F32),
            pltpu.SemaphoreType.DMA((slots, 3)),
            pltpu.SemaphoreType.DMA((slots, 14)),
            pltpu.SemaphoreType.DMA((5,)),
        ],
        compiler_params=pltpu.CompilerParams(vmem_limit_bytes=62 * MIB),
        name="widen",
    )(in_all, fc2_all, dense_all, branches, d_hidden, tokens, cotangent, small)


def on_device(
    tokens, cotangent, block_order, positions, ln_gain, ln_bias, w_qkv, b_qkv, w_dense, b_dense,
    w_fc1, b_fc1, w_fc2, b_fc2,
):
    ctx, fsdp = lax.axis_size("ctx"), lax.axis_size("fsdp")
    f = lax.axis_index("fsdp")
    rows, width = tokens.shape[1:]
    seq = rows * ctx
    ff = w_fc1.shape[1]
    own_width, own_ff = width // ctx, ff // ctx
    own_rows = width // fsdp
    cut = 3 * own_width
    tokens = tokens.reshape(rows, width)
    cotangent = cotangent.reshape(rows, width)

    vectors = (ln_gain, ln_bias, b_dense, b_fc2, b_qkv, b_fc1)
    small, used = jnp.zeros((32 * own_rows,), BF16), 0
    for vector in vectors:
        left = small.shape[0] - used - vector.shape[0]
        small = small + jnp.pad(vector, (used, left))
        used += vector.shape[0]
    small = small.reshape(32, own_rows)
    spread = turn_spread(own_width)
    (
        x_all, g_all, hidden, stat, queries, keys, values, d_att, act, d_up, w_in, fc2, dense, turns,
        small,
    ) = first(
        tokens, cotangent, turn_rows(positions.reshape(rows), own_width), w_qkv, w_fc1, w_dense, w_fc2,
        small, spread, ctx, fsdp,
    )
    att, d_proj = attention(
        block_order, seq // block_order.shape[0], queries, keys, values, d_att,
        turns.reshape(seq, own_width), spread,
    )
    branches, d_hidden, in_all, fc2_all, dense_all, vector = second(
        att, act, d_proj, d_up, w_in.reshape(width, -1), fc2.reshape(own_ff, width),
        dense.reshape(own_width, width), stat, cotangent, x_all, g_all, hidden, fsdp,
    )
    grad_qkv, grad_fc1, grad_dense, grad_fc2, result, input_grad = widen(
        in_all, fc2_all, dense_all, branches, d_hidden, tokens, cotangent, small, ff
    )

    vector = vector.reshape(ctx, -1)
    sums = jnp.sum(vector[:, : 3 * width], axis=0).reshape(3, width)
    sums = lax.dynamic_slice_in_dim(sums, f * own_rows, own_rows, 1)
    columns = vector[:, 3 * width : 3 * width + cut].reshape(ctx, 3, own_width)
    columns = columns.transpose(1, 0, 2).reshape(3 * width)
    units = vector[:, 3 * width + cut : 3 * width + cut + own_ff].reshape(ctx, fsdp, -1)
    units = lax.dynamic_slice_in_dim(units, f, 1, 1).reshape(ff // fsdp)
    return (
        result.reshape(1, rows, width),
        input_grad.reshape(1, rows, width),
        sums[0],
        sums[1],
        grad_qkv,
        lax.dynamic_slice_in_dim(columns, f * (3 * own_rows), 3 * own_rows, 0),
        grad_dense,
        sums[2],
        grad_fc1,
        units,
        grad_fc2,
        sums[2],
    )


def solution(mesh):
    split = P("fsdp", "ctx", None)
    matrix = P("fsdp", None)
    vector = P("fsdp")
    return jax.shard_map(
        on_device,
        mesh=mesh,
        in_specs=(split, split, P(), P("fsdp", "ctx"), vector, vector)
        + (matrix, vector) * 4,
        out_specs=(split, split, vector, vector) + (matrix, vector) * 4,
        check_vma=False,
    )
```

```python
import functools

import jax
import jax.numpy as jnp
import numpy as np
from jax import lax
from jax.experimental import pallas as pl
from jax.experimental.pallas import tpu as pltpu
from jax.sharding import PartitionSpec as P

HEAD_DIM = 64
ROTARY = 32
NORM_EPS = 1e-05
ROPE_BASE = 10000.0
GELU_COEF = 0.7978845608028654
F32 = jnp.float32
BF16 = jnp.bfloat16
STRIP = 256
NT = (((1,), (1,)), ((), ()))
TN = (((0,), (0,)), ((), ()))
MESH = pl.DeviceIdType.MESH
MIB = 1024 * 1024


def nt_dot(left, right):
    return lax.dot_general(left, right, NT, preferred_element_type=F32)


def tn_dot(left, right):
    return lax.dot_general(left, right, TN, preferred_element_type=F32)


def dot(left, right):
    return jnp.dot(left, right, preferred_element_type=F32)


def turn_rows(positions, width):
    half = ROTARY // 2
    frequency = ROPE_BASE ** (-(jnp.arange(half, dtype=F32) * (2.0 / ROTARY)))
    turned = positions.astype(F32)[:, None] * frequency
    both = jnp.concatenate([jnp.cos(turned), jnp.sin(turned)], axis=1)
    coarse = both.astype(BF16)
    fine = (both - coarse.astype(F32)).astype(BF16)
    rows = positions.shape[0]
    used = 4 * half + 1
    return jnp.concatenate(
        [coarse, fine, jnp.ones((rows, 1), BF16), jnp.zeros((rows, width - used), BF16)], axis=1
    )


def turn_spread(width):
    half = ROTARY // 2
    table = np.zeros((width, 3 * width), np.float32)
    for column in range(width):
        at = column % HEAD_DIM
        if at >= ROTARY:
            table[4 * half, column] = 1.0
            continue
        for part in (0, 2 * half):
            table[part + at % half, column] = 1.0
            if at < half:
                table[part + half + at, width + column] = -1.0
            else:
                table[part + half + at - half, 2 * width + column] = 1.0
    return jnp.asarray(table, BF16)


def turn(values, tables, back):
    width = values.shape[1]
    half = ROTARY // 2
    same, after, before = (tables[:, at * width : (at + 1) * width] for at in range(3))
    moved = pltpu.roll(values, width - half, 1) * after + pltpu.roll(values, half, 1) * before
    return values * same - moved if back else values * same + moved


AWAY = [(dx, flip) for dx in range(4) for flip in (False, True) if dx or flip]


def fold(left, right, first):
    lane = lax.broadcasted_iota(jnp.int32, left.shape, 1)
    half = left.shape[1] // 2
    return jnp.where(
        lane < half,
        jnp.where(first, left, pltpu.roll(left, half, 1)),
        jnp.where(first, pltpu.roll(right, half, 1), right),
    )


class Place:
    def __init__(self):
        self.c, self.f = lax.axis_index("ctx"), lax.axis_index("fsdp")
        self.y, self.z, self.core = self.c // 4, (self.c // 2) % 2, self.c % 2
        self.x, self.half = self.f // 2, self.f % 2

    def block(self, dy, flip, other=False):
        core = 1 - self.core if other else self.core
        return ((self.y + dy) % 4) * 4 + (1 - self.z if flip else self.z) * 2 + core

    def shard(self, dx, flip):
        return ((self.x + dx) % 4) * 2 + (1 - self.half if flip else self.half)

    def to_ctx(self, dy, flip, other=False):
        return (self.block(dy, flip, other), self.f)

    def to_fsdp(self, dx, flip):
        return (self.c, self.shard(dx, flip))

    def to_swap(self):
        return (2 * self.f + self.c % 2, self.c // 2)


class Post:
    def __init__(self, place, send, recv):
        self.place, self.send, self.recv, self.started = place, send, recv, []
        self.left = set()

    def copy(self, source, target, device):
        at = len(self.started)
        copy = pltpu.make_async_remote_copy(
            src_ref=source, dst_ref=target, send_sem=self.send.at[at], recv_sem=self.recv.at[at],
            device_id=device, device_id_type=MESH,
        )
        self.started.append(copy)
        copy.start()
        return copy

    def greet(self):
        place = self.place
        barrier = pltpu.get_barrier_semaphore()
        partners = [
            place.to_ctx(1, False), place.to_ctx(-1, False), place.to_ctx(0, True),
            place.to_ctx(0, False, True),
        ] + [place.to_fsdp(*to) for to in AWAY]
        for partner in partners:
            pl.semaphore_signal(barrier, inc=1, device_id=partner, device_id_type=MESH)
        swap = place.to_swap()
        same = jnp.logical_and(swap[0] == place.c, swap[1] == place.f)

        @pl.when(jnp.logical_not(same))
        def _():
            pl.semaphore_signal(barrier, inc=1, device_id=swap, device_id_type=MESH)

        pl.semaphore_wait(barrier, len(partners) + jnp.where(same, 0, 1))

    def has_left(self, copy):
        copy.wait_send()
        self.left.add(id(copy))

    def close(self):
        for copy in self.started:
            if id(copy) not in self.left:
                copy.wait_send()


def gather_ctx(post, own, buf, cut):
    place = post.place
    here = post.place.block(0, False)
    crossed = []

    def send(at, *to):
        return post.copy(buf.at[at], buf.at[at], place.to_ctx(*to))

    def cross(at):
        crossed.append(post.copy(buf.at[at], buf.at[at], place.to_ctx(0, False, True)))

    def first(*to):
        return post.copy(own, buf.at[here], place.to_ctx(*to))

    to_next, to_last, to_pair = first(1, False), first(-1, False), first(0, True)
    crossed.append(first(0, False, True))
    yield
    last, after = place.block(-1, False), place.block(1, False)
    rest = buf.shape[1] - cut
    lower, upper = pl.ds(0, cut), pl.ds(cut, rest)
    to_next.wait_recv()
    halves = [post.copy(buf.at[last, lower], buf.at[last, lower], place.to_ctx(1, False))]
    to_last.wait_recv()
    if rest:
        piece = buf.at[after, upper]
        halves.append(post.copy(piece, piece, place.to_ctx(-1, False)))
    cross(last)
    cross(after)
    yield
    to_pair.wait_recv()
    pair = place.block(0, True)
    pair_next, pair_last = send(pair, 1, False), send(pair, -1, False)
    cross(pair)
    yield
    for copy in halves:
        copy.wait_recv()
    far = place.block(2, False)
    pair_far = send(far, 0, True)
    cross(far)
    yield
    pair_next.wait_recv()
    cross(place.block(-1, True))
    pair_last.wait_recv()
    cross(place.block(1, True))
    yield
    pair_far.wait_recv()
    cross(place.block(2, True))
    yield
    for copy in crossed:
        copy.wait_recv()


def gather_fsdp(post, own, buf, cut):
    place = post.place
    here = place.shard(0, False)
    rest = buf.shape[1] - cut

    def whole(at, dx):
        return post.copy(buf.at[at], buf.at[at], place.to_fsdp(dx, False))

    def lower(at):
        piece = buf.at[at, pl.ds(0, cut)]
        return post.copy(piece, piece, place.to_fsdp(1, False))

    def upper(at):
        piece = buf.at[at, pl.ds(cut, rest)]
        return post.copy(piece, piece, place.to_fsdp(-1, False))

    to_pair = post.copy(own, buf.at[here], place.to_fsdp(0, True))
    to_next = post.copy(own, buf.at[here], place.to_fsdp(1, False))
    to_last = post.copy(own, buf.at[here], place.to_fsdp(-1, False))
    yield
    to_next.wait_recv()
    halves = [lower(place.shard(-1, False))]
    to_last.wait_recv()
    if rest:
        halves.append(upper(place.shard(1, False)))
    yield
    to_pair.wait_recv()
    pair = place.shard(0, True)
    pair_next, pair_last = whole(pair, 1), whole(pair, -1)
    yield
    pair_next.wait_recv()
    halves.append(lower(place.shard(-1, True)))
    pair_last.wait_recv()
    if rest:
        halves.append(upper(place.shard(1, True)))
    yield
    for copy in halves:
        copy.wait_recv()


def gather_direct(post, own, buf):
    place = post.place
    here = place.shard(0, False)
    copies = [post.copy(own, buf.at[here], place.to_fsdp(*to)) for to in AWAY]
    yield
    for copy in copies:
        copy.wait_recv()


class Swap:
    def __init__(self, place, source, target, send, recv, local):
        device = place.to_swap()
        self.same = jnp.logical_and(device[0] == place.c, device[1] == place.f)
        self.away = pltpu.make_async_remote_copy(
            src_ref=source, dst_ref=target, send_sem=send, recv_sem=recv, device_id=device,
            device_id_type=MESH,
        )
        self.stay = pltpu.make_async_copy(source, target, local)
        pl.when(jnp.logical_not(self.same))(lambda: self.away.start())
        pl.when(self.same)(lambda: self.stay.start())

    def wait(self):
        pl.when(jnp.logical_not(self.same))(lambda: self.away.wait())
        pl.when(self.same)(lambda: self.stay.wait())


def first_kernel(
    x_in, g_in, turn_in, w_qkv, w_fc1, w_dense, w_fc2, small_in, spread,
    x_to, g_to, hidden_to, stat_to, q_to, k_to, v_to, d_att_to, act_to, d_up_to, w_in_to, fc2_to,
    dense_to,
    turns_to, small_to,
    x_all, g_all, hidden, stat, q_out, k_out, v_out, d_att, act, d_up, w_in, fc2, dense,
    turns, small_out,
    wide_rows, in_rows, fc2_rows, dense_rows, piece, small_all, tables, proj, slope, vec, bias,
    send, recv, local, reads, swap_send, swap_recv,
):
    place = Place()
    post = Post(place, send, recv)
    rows, width = x_in.shape
    own_width = q_out.shape[1]
    own_ff = act.shape[1]
    cut = 3 * own_width
    here, shard = place.block(0, False), place.shard(0, False)

    def columns(first, count):
        return pl.ds(pl.multiple_of(first, 128), count)

    fsdp, fc2_step = fc2.shape[:2]
    dense_step = dense.shape[1]
    units = w_fc1.shape[1] // fsdp
    first_dense = (place.c % 2) * own_width + (place.c // 2) * dense_step
    first_fc2 = place.c * fc2_step
    sources = [
        (w_dense.at[pl.ds(pl.multiple_of(first_dense, 16), dense_step)], dense_rows),
        (w_fc2.at[pl.ds(pl.multiple_of(first_fc2, 16), fc2_step)], fc2_rows),
    ]
    for part in range(3):
        take = columns(part * width + place.c * own_width, own_width)
        sources.append((w_qkv.at[:, take], in_rows.at[:, pl.ds(part * own_width, own_width)]))
    for part in range(fsdp):
        take = columns(part * units + place.c // 2 * 128, 128)
        sources.append((w_fc1.at[:, take], wide_rows.at[:, pl.ds(part * 128, 128)]))
    ready = [
        pltpu.make_async_copy(source, target, reads.at[at])
        for at, (source, target) in enumerate(sources)
    ]
    for copy in ready:
        copy.start()
    post.greet()
    for copy in ready:
        copy.wait()
    swap = Swap(place, dense_rows, piece, swap_send, swap_recv, local.at[0])
    for part in range(fsdp // 2):
        left, right = (
            wide_rows[:, at * 128 : (at + 1) * 128].astype(F32) for at in (2 * part, 2 * part + 1)
        )
        in_rows[:, cut + part * 128 : cut + (part + 1) * 128] = fold(
            left, right, place.core == 0
        ).astype(BF16)
    keeps = []

    def keep(source, target):
        copy = pltpu.make_async_copy(source, target, local.at[1 + len(keeps)])
        keeps.append(copy)
        copy.start()
        return copy

    own = [
        keep(x_in, x_all.at[here]), keep(in_rows, w_in.at[shard]), keep(turn_in, turns.at[here]),
        keep(small_in, small_all.at[shard]), keep(g_in, g_all.at[here]),
        keep(fc2_rows, fc2.at[shard]),
    ]
    x_flow = gather_ctx(post, x_in, x_all, rows // 2)
    in_flow = gather_fsdp(post, in_rows, w_in, in_rows.shape[0] // 2)
    small_flow = gather_direct(post, small_in, small_all)
    turn_flow = gather_ctx(post, turn_in, turns, rows // 2)
    def advance(*flows):
        for flow in flows:
            next(flow, None)

    advance(x_flow, in_flow, small_flow, turn_flow)
    advance(x_flow, in_flow)
    g_flow = gather_ctx(post, g_in, g_all, rows // 2)
    fc2_flow = gather_fsdp(post, fc2_rows, fc2, fc2_step // 2)
    advance(g_flow, fc2_flow)
    swap.wait()
    keep(piece, dense.at[shard])
    dense_flow = gather_fsdp(post, piece, dense, dense_step)
    advance(dense_flow)
    advance(x_flow, in_flow, g_flow, turn_flow, fc2_flow, dense_flow)
    for _ in small_flow:
        pass
    for copy in own[:4]:
        copy.wait()

    side = small_all.shape[2]
    small_out[...] = small_all[...].astype(F32)
    for at in range(small_all.shape[0]):
        vec[0:2, at * side : (at + 1) * side] = small_out[at, 0:2, :]
    for part in range(3):
        first = part * width + place.c * own_width
        count = 3 * side
        row = small_out[first // count, pl.ds(4 + (first % count) // side, 1), :]
        bias[0:1, part * own_width : (part + 1) * own_width] = jnp.where(
            first % side == 0, row[:, :own_width], row[:, own_width:]
        )
    quarter = place.c % 4
    pieces = []
    for part in range(fsdp):
        row = small_out[part, pl.ds(7 + place.c // 4, 1), :]
        row = jnp.where(quarter >= 2, row[:, 128:], row[:, :128])
        pieces.append(jnp.broadcast_to(row, (8, 128)))
    for part in range(fsdp // 2):
        row = fold(pieces[2 * part], pieces[2 * part + 1], quarter % 2 == 0)
        bias[0:1, cut + part * 128 : cut + (part + 1) * 128] = row[0:1, :]

    def normalise(block):
        lane = lax.broadcasted_iota(jnp.int32, (rows, stat.shape[1]), 1)
        target = pl.ds(pl.multiple_of(block * rows, rows), rows)
        value = x_all[block].astype(F32)
        mean = jnp.mean(value, axis=1, keepdims=True)
        centred = value - mean
        inverse = lax.rsqrt(jnp.mean(centred * centred, axis=1, keepdims=True) + NORM_EPS)
        hidden[target, :] = (centred * inverse * vec[0:1, :] + vec[1:2, :]).astype(BF16)
        stat[target, :] = jnp.where(lane < HEAD_DIM, mean, inverse)

    def normalise_each(targets):
        order = [place.block(*to) for to in targets]

        def body(at, carry):
            block = order[0]
            for number, other in enumerate(order[1:]):
                block = jnp.where(at == number + 1, other, block)
            normalise(block)
            return carry

        lax.fori_loop(0, len(order), body, 0)

    normalise_each([(0, False), (1, False), (-1, False)])
    advance(x_flow, in_flow, g_flow, turn_flow, fc2_flow, dense_flow)
    normalise_each([(0, True)])
    advance(x_flow, in_flow, g_flow, turn_flow, fc2_flow, dense_flow)
    keep(w_in, w_in_to)
    normalise_each([(2, False), (1, True), (-1, True)])
    advance(x_flow, g_flow, turn_flow, fc2_flow, dense_flow)
    normalise_each([(2, True)])
    advance(x_flow, turn_flow)
    keep(x_all, x_to)
    normalise_each([(dy, flip, True) for dy in range(4) for flip in (False, True)])
    keep(hidden, hidden_to)
    keep(stat, stat_to)
    keep(small_out, small_to)
    advance(turn_flow)
    keep(turns, turns_to)

    chunk_rows = proj.shape[0]
    group = chunk_rows // rows

    def project(chunk):
        take = slice(chunk * chunk_rows, (chunk + 1) * chunk_rows)
        weight = w_in[...].reshape(width, proj.shape[1])
        proj[...] = dot(hidden[take, :], weight)

    def settle(chunk):
        turned = turns[pl.ds(chunk * group, group)].reshape(chunk_rows, own_width)
        tables[...] = dot(turned, spread[...])
        target = slice(chunk * chunk_rows, (chunk + 1) * chunk_rows)
        value = proj[...] + bias[0:1, :]
        table = tables[...]
        q_out[target, :] = turn(value[:, :own_width], table, False).astype(BF16)
        k_out[target, :] = turn(value[:, own_width : 2 * own_width], table, False).astype(BF16)
        v_out[target, :] = value[:, 2 * own_width : cut].astype(BF16)
        up = value[:, cut:]
        square = up * up
        curve = jnp.tanh(GELU_COEF * up * (1.0 + 0.044715 * square))
        act[target, :] = (0.5 * up * (1.0 + curve)).astype(BF16)
        slope[target, :] = 0.5 * (1.0 + curve) + 0.5 * up * (1.0 - curve * curve) * (
            GELU_COEF * (1.0 + 3.0 * 0.044715 * square)
        )

    chunks = hidden.shape[0] // chunk_rows
    project(0)
    settle(0)
    project(1)
    settle(1)
    advance(g_flow)
    project(2)
    settle(2)
    project(3)
    settle(3)
    for target, source in ((q_to, q_out), (k_to, k_out), (v_to, v_out), (act_to, act)):
        keep(source, target)
    advance(fc2_flow, dense_flow)
    own[5].wait()
    keeps[6].wait()
    keep(fc2, fc2_to)
    keep(dense, dense_to)
    advance(g_flow)
    own[4].wait()
    keep(g_all, g_to)

    for chunk in range(chunks):
        grads = g_all[pl.ds(chunk * group, group)].reshape(chunk_rows, width)
        target = slice(chunk * chunk_rows, (chunk + 1) * chunk_rows)
        d_att[target, :] = nt_dot(grads, dense[...].reshape(own_width, width)).astype(BF16)
        d_act = nt_dot(grads, fc2[...].reshape(own_ff, width))
        d_up[target, :] = (d_act * slope[target, :]).astype(BF16)
    keep(d_att, d_att_to)
    keep(d_up, d_up_to)
    for copy in keeps[7:]:
        copy.wait()
    post.close()


def first(tokens, cotangent, turns, w_qkv, w_fc1, w_dense, w_fc2, small, spread, ctx, fsdp):
    rows, width = tokens.shape
    seq = ctx * rows
    own_width, own_ff = turns.shape[1], w_fc1.shape[1] // ctx
    columns = 3 * own_width + own_ff
    side = width // fsdp
    many = 3 * 16 + 3 * 9 + fsdp - 1
    any_, vmem = pl.BlockSpec(memory_space=pl.ANY), pl.BlockSpec(memory_space=pltpu.VMEM)

    def low(*shape):
        return jax.ShapeDtypeStruct(shape, BF16)

    def wide(*shape):
        return jax.ShapeDtypeStruct(shape, F32)

    outs = [
        low(ctx, rows, width), low(ctx, rows, width), low(seq, width), wide(seq, 128),
        low(seq, own_width), low(seq, own_width), low(seq, own_width), low(seq, own_width),
        low(seq, own_ff), low(seq, own_ff), low(fsdp, side, columns),
        low(fsdp, own_ff // fsdp, width), low(fsdp, own_width // fsdp, width),
        low(ctx, rows, own_width), wide(*((fsdp,) + small.shape)),
    ]
    chunk_rows = 4 * rows
    return pl.pallas_call(
        first_kernel,
        out_shape=tuple(outs),
        in_specs=[any_] * 8 + [vmem],
        out_specs=(any_,) * len(outs),
        scratch_shapes=[pltpu.VMEM(out.shape, out.dtype) for out in outs]
        + [
            pltpu.VMEM((side, fsdp * 128), BF16),
            pltpu.VMEM((side, columns), BF16),
            pltpu.VMEM((own_ff // fsdp, width), BF16),
            pltpu.VMEM((own_width // fsdp, width), BF16),
            pltpu.VMEM((own_width // fsdp, width), BF16),
            pltpu.VMEM((fsdp,) + small.shape, BF16),
            pltpu.VMEM((chunk_rows, 3 * own_width), F32),
            pltpu.VMEM((chunk_rows, columns), F32),
            pltpu.VMEM((seq, own_ff), F32),
            pltpu.VMEM((8, width), F32),
            pltpu.VMEM((8, columns), F32),
            pltpu.SemaphoreType.DMA((many,)),
            pltpu.SemaphoreType.DMA((many,)),
            pltpu.SemaphoreType.DMA((24,)),
            pltpu.SemaphoreType.DMA((5 + fsdp,)),
            pltpu.SemaphoreType.DMA,
            pltpu.SemaphoreType.DMA,
        ],
        compiler_params=pltpu.CompilerParams(
            collective_id=0, has_side_effects=True, vmem_limit_bytes=60 * MIB
        ),
        name="first",
    )(tokens, cotangent, turns, w_qkv, w_fc1, w_dense, w_fc2, small, spread)


def attention_kernel(
    block, order, q_hbm, k_hbm, v_hbm, g_hbm, turns_hbm, spread, o_to, d_to,
    q_in, k_in, v_in, g_in, turns, o_out, d_out, loads, qs, ks, vs, gs, os, dqs, dks, dvs, kt, vt, table,
):
    rows, width = q_in.shape
    blocks = rows // block
    reads = [
        pltpu.make_async_copy(source, target, loads.at[at])
        for at, (source, target) in enumerate(
            [(q_hbm, q_in), (k_hbm, k_in), (v_hbm, v_in), (g_hbm, g_in), (turns_hbm, turns)]
        )
    ]
    for copy in reads:
        copy.start()
    for copy in reads[:4]:
        copy.wait()

    def collect(at, carry):
        src = pl.ds(pl.multiple_of(at * block, block), block)
        dst = pl.ds(pl.multiple_of(order[at] * block, block), block)
        qs[dst, :] = q_in[src, :]
        ks[dst, :] = k_in[src, :]
        vs[dst, :] = v_in[src, :]
        gs[dst, :] = g_in[src, :]
        return carry

    lax.fori_loop(0, blocks, collect, 0, unroll=4)
    dks[...] = jnp.zeros_like(dks)
    dvs[...] = jnp.zeros_like(dvs)
    heads = width // HEAD_DIM
    scale = HEAD_DIM ** (-0.5)
    q_pos = lax.broadcasted_iota(jnp.int32, (STRIP, STRIP), 0)
    k_pos = lax.broadcasted_iota(jnp.int32, (STRIP, STRIP), 1)
    diagonal = q_pos <= k_pos
    reads[4].wait()
    table[...] = dot(turns[...], spread[...])
    kt[...] = ks[...].T
    vt[...] = vs[...].T
    sides = [slice(head * HEAD_DIM, (head + 1) * HEAD_DIM) for head in range(heads)]
    strips = rows // STRIP

    def begin(strip):
        here = slice(strip * STRIP, (strip + 1) * STRIP)
        count = (strip + 1) * STRIP
        query = [qs[here, cols] * jnp.asarray(scale, BF16) for cols in sides]
        part = [nt_dot(ks[:count, cols], query[h]) for h, cols in enumerate(sides)]
        return query, part

    ready = begin(0)
    for strip in range(strips):
        here = slice(strip * STRIP, (strip + 1) * STRIP)
        count = (strip + 1) * STRIP
        query, part = ready
        edge = [jnp.where(diagonal, p[count - STRIP :, :], -1e30) for p in part]
        part = [jnp.concatenate([p[: count - STRIP, :], e], axis=0) if strip else e for p, e in zip(part, edge)]
        part = [jnp.exp(p - jnp.max(p, axis=0, keepdims=True)) for p in part]
        inverse = [1.0 / jnp.sum(p, axis=0, keepdims=True) for p in part]
        low = [p.astype(BF16) for p in part]
        mixed = [dot(vt[cols, :count], low[h]) * inverse[h] for h, cols in enumerate(sides)]
        grad = [gs[here, cols].astype(F32).T * inverse[h] for h, cols in enumerate(sides)]
        centre = [jnp.sum(g * m, axis=0, keepdims=True) for g, m in zip(grad, mixed)]
        os[here, :] = jnp.concatenate(mixed, axis=0).T.astype(BF16)
        grad = [g.astype(BF16) for g in grad]
        if strip + 1 < strips:
            ready = begin(strip + 1)
        d_score = [(part[h] * (dot(vs[:count, cols], grad[h]) - centre[h])).astype(BF16) for h, cols in enumerate(sides)]
        dqs[here, :] = jnp.concatenate([dot(kt[cols, :count], d_score[h]) for h, cols in enumerate(sides)], axis=0).T * scale
        dks[:count, :] += jnp.concatenate([dot(d_score[h], query[h]) for h in range(heads)], axis=1)
        dvs[:count, :] += jnp.concatenate([nt_dot(low[h], grad[h]) for h in range(heads)], axis=1)

    def give(at, carry):
        src = pl.ds(pl.multiple_of(order[at] * block, block), block)
        dst = pl.ds(pl.multiple_of(at * block, block), block)
        tables = table[dst, :]
        o_out[dst, :] = os[src, :]
        d_out[dst, :width] = turn(dqs[src, :], tables, True).astype(BF16)
        d_out[dst, width : 2 * width] = turn(dks[src, :], tables, True).astype(BF16)
        d_out[dst, 2 * width :] = dvs[src, :].astype(BF16)
        return carry

    writes = []
    parts = 4
    for part in range(parts):
        lax.fori_loop(part * blocks // parts, (part + 1) * blocks // parts, give, 0, unroll=4)
        take = pl.ds(part * rows // parts, rows // parts)
        for number, (source, target) in enumerate(((o_out, o_to), (d_out, d_to))):
            copy = pltpu.make_async_copy(
                source.at[take], target.at[take], loads.at[5 + 2 * part + number]
            )
            copy.start()
            writes.append(copy)
    for copy in writes:
        copy.wait()


def attention(order, block, queries, keys, values, grads, turns, spread):
    rows, width = queries.shape
    vmem = pl.BlockSpec(memory_space=pltpu.VMEM)
    smem = pl.BlockSpec(memory_space=pltpu.SMEM)
    any_ = pl.BlockSpec(memory_space=pl.ANY)
    return pl.pallas_call(
        functools.partial(attention_kernel, block),
        out_shape=(
            jax.ShapeDtypeStruct((rows, width), BF16),
            jax.ShapeDtypeStruct((rows, 3 * width), BF16),
        ),
        in_specs=[smem] + [any_] * 5 + [vmem],
        out_specs=(any_, any_),
        scratch_shapes=[pltpu.VMEM((rows, width), BF16)] * 6
        + [pltpu.VMEM((rows, 3 * width), BF16), pltpu.SemaphoreType.DMA((13,))]
        + [pltpu.VMEM((rows, width), BF16)] * 5
        + [pltpu.VMEM((rows, width), F32)] * 3
        + [pltpu.VMEM((width, rows), BF16), pltpu.VMEM((width, rows), BF16)]
        + [pltpu.VMEM((rows, 3 * width), F32)],
        compiler_params=pltpu.CompilerParams(vmem_limit_bytes=60 * MIB),
        cost_estimate=pl.CostEstimate(
            flops=6 * rows * rows * width,
            bytes_accessed=rows * width * 22,
            transcendentals=rows * rows * width // HEAD_DIM // 2,
        ),
        name="attention",
    )(order, queries, keys, values, grads, turns, spread)


ORDER = [(2, True), (1, True), (-1, True), (2, False), (0, True), (1, False), (-1, False), (0, False)]
SHARDS = [(2, True), (2, False), (1, True), (-1, True), (1, False), (-1, False), (0, True), (0, False)]


def add_into(target, *parts):
    step = 64 if target.shape[0] % 64 == 0 else target.shape[0]
    plain = len(parts) == 2 and target.dtype == BF16

    def body(at, carry):
        take = pl.ds(pl.multiple_of(at * step, step), step)
        if plain:
            target[take, :] = parts[0][take, :] + parts[1][take, :]
            return carry
        total = parts[0][take, :].astype(F32)
        for part in parts[1:]:
            total = total + part[take, :].astype(F32)
        target[take, :] = total.astype(target.dtype)
        return carry

    lax.fori_loop(0, target.shape[0] // step, body, 0)


def reduce_ctx(post, own, core, crossed, pair_in, half_in, ring_in, cross_in, last_in, total):
    place = post.place
    cut = half_in.shape[1]
    up, down, pair = place.to_ctx(1, False), place.to_ctx(-1, False), place.to_ctx(0, True)

    def meet(at, *more):
        crossed[at].wait_recv()
        add_into(core.at[at], own.at[at], core.at[at], *more)

    meet(0)
    far = post.copy(core.at[0], pair_in, pair)
    yield
    meet(1)
    cross_next = post.copy(core.at[1], cross_in.at[0], up)
    meet(2)
    cross_last = post.copy(core.at[2], cross_in.at[1], down)
    yield
    far.wait_recv()
    meet(3, pair_in)
    low = post.copy(core.at[3, pl.ds(0, cut)], half_in.at[0], up)
    high = post.copy(core.at[3, pl.ds(cut, cut)], half_in.at[1], down)
    yield
    cross_next.wait_recv()
    cross_last.wait_recv()
    meet(4, cross_in.at[0], cross_in.at[1])
    last = post.copy(core.at[4], last_in, pair)
    yield
    meet(5)
    low.wait_recv()
    lower = core.at[5, pl.ds(0, cut)]
    add_into(lower, lower, half_in.at[0])
    ring_next = post.copy(core.at[5], ring_in.at[0], up)
    meet(6)
    high.wait_recv()
    upper = core.at[6, pl.ds(cut, cut)]
    add_into(upper, upper, half_in.at[1])
    ring_last = post.copy(core.at[6], ring_in.at[1], down)
    yield
    crossed[7].wait_recv()
    last.wait_recv()
    ring_next.wait_recv()
    ring_last.wait_recv()
    add_into(total, own.at[7], core.at[7], ring_in.at[0], ring_in.at[1], last_in)


def reduce_fsdp(post, part, low_in, high_in, ring_in, pair_in, total):
    place = post.place
    cut, rest = low_in.shape[1], high_in.shape[1]
    lower, upper = pl.ds(0, cut), pl.ds(cut, rest)
    up, down, pair = place.to_fsdp(1, False), place.to_fsdp(-1, False), place.to_fsdp(0, True)
    halves = [
        (
            post.copy(part.at[side, lower], low_in.at[side], up),
            post.copy(part.at[side, upper], high_in.at[side], down),
        )
        for side in range(2)
    ]
    yield
    rings = []
    for side in range(2):
        low, high = halves[side]
        after, before = part.at[2 + 2 * side], part.at[3 + 2 * side]
        low.wait_recv()
        add_into(after.at[lower], after.at[lower], low_in.at[side])
        to_next = post.copy(after, ring_in.at[side, 0], up)
        high.wait_recv()
        add_into(before.at[upper], before.at[upper], high_in.at[side])
        to_last = post.copy(before, ring_in.at[side, 1], down)
        rings.append((to_next, to_last))
        yield
    for copy in rings[0]:
        copy.wait_recv()
    add_into(part.at[6], part.at[6], ring_in.at[0, 0], ring_in.at[0, 1])
    across = post.copy(part.at[6], pair_in, pair)
    yield
    for copy in rings[1]:
        copy.wait_recv()
    across.wait_recv()
    add_into(total, part.at[7], ring_in.at[1, 0], ring_in.at[1, 1], pair_in)


def run(*flows):
    flows = list(flows)
    while flows:
        flows = [flow for flow in flows if next(flow, flows) is not flows]


def second_kernel(
    att_in, act_in, d_proj_in, d_up_in, w_in_in, w_fc2_in, w_dense_in, stat_in, g_own_in, x_all, g_all, hidden,
    out_total, hid_total, in_all, fc2_all, dense_all, vector_all,
    att, act, d_proj, d_up, w_in, w_fc2, w_dense, stat, g_own,
    own_a, own_b, core_a, core_b, slot_a, slot_b,
    pair_a, half_a, ring_a, cross_a, last_a, pair_b, half_b, ring_b, cross_b, last_b,
    in_part, in_low, in_high, in_ring, in_pair, in_sum,
    out_part, out_low, out_high, out_ring, out_pair, out_sum, out_piece,
    column, x_block, total_a, total_b, gain_sum, shift_sum,
    vector, vector_shards, vector_sum,
    send, recv, local, loads, reads, swap_send, swap_recv,
):
    place = Place()
    post = Post(place, send, recv)
    rows, width = g_own.shape
    cut = d_proj.shape[1]
    side = in_part.shape[1]
    here, shard = place.block(0, False), place.shard(0, False)
    keeps, numbers = [], iter(range(7))

    def keep(source, target):
        copy = pltpu.make_async_copy(source, target, local.at[next(numbers)])
        keeps.append(copy)
        copy.start()
        return copy

    operands = [
        pltpu.make_async_copy(source, target, reads.at[at])
        for at, (source, target) in enumerate(
            [
                (d_proj_in, d_proj), (d_up_in, d_up), (att_in, att), (act_in, act), (w_fc2_in, w_fc2),
                (w_dense_in, w_dense),
                (w_in_in, w_in), (stat_in, stat), (g_own_in, g_own),
            ]
        )
    ]

    def load_x(at):
        dy, flip = ORDER[at]
        block = place.block(dy, flip) // 2
        copy = pltpu.make_async_copy(
            x_all.at[pl.ds(2 * block, 2)], x_block.at[at % 2], loads.at[at % 2]
        )
        copy.start()
        return copy

    ahead = column.shape[0]

    def load_column(at):
        if at < len(SHARDS):
            first = pl.multiple_of(place.shard(*SHARDS[at]) * side, side)
            source = hidden.at[:, pl.ds(first, side)]
        else:
            source = g_all.at[:, pl.ds((at - len(SHARDS)) * side, side)]
        copy = pltpu.make_async_copy(source, column.at[at % ahead], loads.at[2 + at % ahead])
        copy.start()
        return copy

    for copy in operands[:2]:
        copy.start()
    pending_column = [load_column(at) for at in range(ahead - 1)]
    pending_x = [load_x(0)]
    for copy in operands[2:]:
        copy.start()
    post.greet()
    gain_sum[...] = jnp.zeros_like(gain_sum)
    shift_sum[...] = jnp.zeros_like(shift_sum)
    crossed_a, crossed_b, slots = {}, {}, {}
    partner = place.to_ctx(0, False, True)
    depth = slot_a.shape[0]

    def produce(at):
        dy, flip = ORDER[at]
        block = place.block(dy, flip) // 2
        pending_x.pop().wait()
        if at + 1 < len(ORDER):
            pending_x.append(load_x(at + 1))
        slot = at % depth
        if at >= depth:
            for copy in slots[at - depth]:
                post.has_left(copy)
        other_rows = pl.ds(pl.multiple_of(block * (2 * rows) + (1 - place.core) * rows, rows), rows)
        own_rows = pl.ds(pl.multiple_of(block * (2 * rows) + place.core * rows, rows), rows)

        def both(ref):
            return jnp.concatenate([ref[other_rows, :], ref[own_rows, :]], axis=0)

        left, right = both(att), both(act)
        span = width // 2
        for first in range(0, width, span):
            take = slice(first, first + span)
            value = dot(left, w_dense[:, take]) + dot(right, w_fc2[:, take])
            slot_a[slot, :, take] = value[:rows].astype(BF16)
            own_a[at, :, take] = value[rows:].astype(BF16)
        left, right, stats = both(d_proj), both(d_up), both(stat)
        mean, inverse = stats[:, 0:1], stats[:, HEAD_DIM : HEAD_DIM + 1]
        span = width // 4
        for first in range(0, width, span):
            take = slice(first, first + span)
            value = nt_dot(left, w_in[take, :cut]) + nt_dot(right, w_in[take, cut:])
            slot_b[slot, :, take] = value[:rows].astype(BF16)
            own_b[at, :, take] = value[rows:].astype(BF16)
            tokens = jnp.concatenate(
                [x_block[at % 2, 1 - place.core, :, take], x_block[at % 2, place.core, :, take]],
                axis=0,
            )
            normed = (tokens.astype(F32) - mean) * inverse
            parts = (2 * rows // 8, 8, span)
            gain_sum[:, take] += jnp.sum((value * normed).reshape(parts), axis=0)
            shift_sum[:, take] += jnp.sum(value.reshape(parts), axis=0)
        crossed_a[at] = post.copy(slot_a.at[slot], core_a.at[at], partner)
        crossed_b[at] = post.copy(slot_b.at[slot], core_b.at[at], partner)
        slots[at] = (crossed_a[at], crossed_b[at])

    def next_column(at):
        pending_column.pop(0).wait()
        if at + ahead - 1 < 2 * len(SHARDS):
            pending_column.append(load_column(at + ahead - 1))
        return column[at % ahead]

    def grad_in(at):
        rows_of = next_column(at)
        in_part[at, :, :cut] = tn_dot(rows_of, d_proj[...]).astype(BF16)
        in_part[at, :, cut:] = tn_dot(rows_of, d_up[...]).astype(BF16)

    def grad_out(at):
        columns = next_column(len(SHARDS) + at)
        take = slice(at * side, (at + 1) * side)
        dense = tn_dot(att[...], columns).astype(BF16)
        fc2 = tn_dot(act[...], columns).astype(BF16)
        dense_step, fc2_step = dense.shape[0] // len(SHARDS), fc2.shape[0] // len(SHARDS)
        for to in range(len(SHARDS)):
            out_part[to, :dense_step, take] = dense[to * dense_step : (to + 1) * dense_step]
            out_part[to, dense_step:, take] = fc2[to * fc2_step : (to + 1) * fc2_step]

    class ByShard:
        @property
        def at(self):
            return self

        def __getitem__(self, index):
            if isinstance(index, tuple):
                return out_part.at[(place.shard(*SHARDS[index[0]]),) + index[1:]]
            return out_part.at[place.shard(*SHARDS[index])]

    def in_flow():
        yield from reduce_fsdp(post, in_part, in_low, in_high, in_ring, in_pair, in_sum)
        keep(in_sum, in_all.at[here])
        yield from gather_ctx(post, in_sum, in_all, in_sum.shape[0] // 2)

    def out_flow():
        yield from reduce_fsdp(post, ByShard(), out_low, out_high, out_ring, out_pair, out_sum)
        first, count = dense_all.shape[1], fc2_all.shape[1]
        swap = Swap(
            place, out_sum.at[pl.ds(0, first)], out_piece, swap_send, swap_recv, local.at[7]
        )
        fc2_own = out_sum.at[pl.ds(first, count)]
        keep(fc2_own, fc2_all.at[here])
        flows = [gather_ctx(post, fc2_own, fc2_all, count // 2)]
        next(flows[0])
        yield
        next(flows[0])
        swap.wait()
        keep(out_piece, dense_all.at[here])
        flows.append(gather_ctx(post, out_piece, dense_all, first))
        while flows:
            flows = [flow for flow in flows if next(flow, flows) is not flows]
            yield

    def vector_flow():
        mine = keep(vector, vector_shards.at[shard])
        yield from gather_fsdp(post, vector, vector_shards, 8)
        mine.wait()
        keeps[:] = [kept for kept in keeps if kept is not mine]
        total = vector_shards[0]
        for at in range(1, vector_shards.shape[0]):
            total = total + vector_shards[at]
        vector_sum[...] = total
        keep(vector_sum, vector_all.at[here])
        yield from gather_ctx(post, vector_sum, vector_all, 8)

    def rows_flow(own, core, crossed, pair, half, ring, cross, last, total, target):
        yield from reduce_ctx(post, own, core, crossed, pair, half, ring, cross, last, total)
        keep(total, target)

    ins, outs = in_flow(), out_flow()
    a = rows_flow(
        own_a, core_a, crossed_a, pair_a, half_a, ring_a, cross_a, last_a, total_a, out_total
    )
    b = rows_flow(
        own_b, core_b, crossed_b, pair_b, half_b, ring_b, cross_b, last_b, total_b, hid_total
    )

    def both_next():
        next(a)
        next(b)

    for copy in operands[:2]:
        copy.wait()
    grad_in(0)
    grad_in(1)
    next(ins)
    for copy in operands[2:]:
        copy.wait()
    produce(0)
    produce(1)
    both_next()
    produce(2)
    both_next()
    for at in range(2, 8):
        grad_in(at)
    produce(3)
    next(ins)
    next(ins)
    for at in range(8):
        grad_out(at)
    next(outs)
    both_next()
    produce(4)
    next(ins)
    produce(5)
    both_next()
    produce(6)
    next(ins)
    next(outs)
    both_next()
    next(outs)
    produce(7)

    half = vector.shape[1]
    ones = jnp.ones((16, att.shape[0]), BF16)
    columns = jnp.concatenate([dot(ones, d_proj[...])[:1], dot(ones, d_up[...])[:1]], axis=1)
    vector[...] = jnp.zeros_like(vector)
    sums = [
        jnp.sum(gain_sum[...], axis=0, keepdims=True),
        jnp.sum(shift_sum[...], axis=0, keepdims=True),
        dot(ones[:, :rows], g_own[...])[:1],
    ]
    for at, row in enumerate(sums):
        vector[2 * at : 2 * at + 1, :] = row[:, :half]
        vector[2 * at + 1 : 2 * at + 2, :] = row[:, half:]
    vector[6:7, : columns.shape[1]] = columns
    vectors = vector_flow()
    next(vectors)
    run(ins, outs, a, b, vectors)

    for kept in keeps:
        kept.wait()
    post.close()


def second(att, act, d_proj, d_up, w_in, w_fc2, w_dense, stat, cotangent, x_all, g_all, hidden, fsdp):
    rows, width = cotangent.shape
    ctx = x_all.shape[0]
    side = width // fsdp
    in_columns = w_in.shape[1]
    fc2_rows, dense_rows = w_fc2.shape[0] // fsdp, w_dense.shape[0] // fsdp
    out_rows = fc2_rows + dense_rows
    any_ = pl.BlockSpec(memory_space=pl.ANY)

    def low(*shape):
        return pltpu.VMEM(shape, BF16)

    def wide(*shape):
        return pltpu.VMEM(shape, F32)

    def ctx_slots():
        return [
            low(rows, width), low(2, rows // 2, width), low(2, rows, width), low(2, rows, width),
            low(rows, width),
        ]

    def fsdp_slots(depth, columns, cut):
        return [
            low(fsdp, depth, columns), low(2, cut, columns), low(2, depth - cut, columns),
            low(2, 2, depth, columns), low(depth, columns), low(depth, columns),
        ]

    vector = (16, width // 2)
    many = 2 * 16 + 2 * 9 + 3 * 16 + 9 + 16
    ahead = 4
    operands = (att, act, d_proj, d_up, w_in, w_fc2, w_dense, stat, cotangent)
    return pl.pallas_call(
        second_kernel,
        out_shape=(
            jax.ShapeDtypeStruct((rows, width), F32),
            jax.ShapeDtypeStruct((rows, width), F32),
            jax.ShapeDtypeStruct((ctx, side, in_columns), BF16),
            jax.ShapeDtypeStruct((ctx, fc2_rows, width), BF16),
            jax.ShapeDtypeStruct((ctx, dense_rows, width), BF16),
            jax.ShapeDtypeStruct((ctx,) + vector, F32),
        ),
        in_specs=[any_] * 12,
        out_specs=(any_,) * 6,
        scratch_shapes=[pltpu.VMEM(operand.shape, operand.dtype) for operand in operands]
        + [low(ctx // 2, rows, width)] * 4
        + [low(2, rows, width)] * 2
        + ctx_slots()
        + ctx_slots()
        + fsdp_slots(side, in_columns, side // 2)
        + fsdp_slots(out_rows, width, 48)
        + [low(dense_rows, width)]
        + [
            low(ahead, ctx * rows, side), low(2, 2, rows, width), wide(rows, width),
            wide(rows, width), wide(8, width), wide(8, width),
            wide(*vector), wide(fsdp, *vector), wide(*vector),
            pltpu.SemaphoreType.DMA((many,)),
            pltpu.SemaphoreType.DMA((many,)),
            pltpu.SemaphoreType.DMA((8,)),
            pltpu.SemaphoreType.DMA((2 + ahead,)),
            pltpu.SemaphoreType.DMA((len(operands),)),
            pltpu.SemaphoreType.DMA,
            pltpu.SemaphoreType.DMA,
        ],
        compiler_params=pltpu.CompilerParams(
            collective_id=1, has_side_effects=True, vmem_limit_bytes=63 * MIB
        ),
        name="second",
    )(*operands, x_all, g_all.reshape(ctx * rows, width), hidden)


def widen_kernel(
    in_all, fc2_all, dense_all, branches_in, d_hidden_in, x_in, g_in, small_in,
    qkv, fc1, dense, fc2, result_to, input_grad_to,
    in_low, fc2_low, dense_low, qkv_wide, fc1_wide, fc2_wide, dense_wide,
    vec, branches, d_hidden, x_own, g_own, small, result, input_grad, loads, stores, reads,
):
    count = in_all.shape[0] // 2
    slots = in_low.shape[0]
    own = qkv.shape[1] // 3 // count
    units = fc1.shape[1] // count
    fc2_step, dense_step = fc2.shape[0] // count, dense.shape[0] // count // 2
    cut = 3 * own // 2

    def load(at):
        slot = at % slots
        copies = [
            pltpu.make_async_copy(source.at[pl.ds(2 * at, 2)], target.at[slot], loads.at[slot, number])
            for number, (source, target) in enumerate(
                [(in_all, in_low), (fc2_all, fc2_low), (dense_all, dense_low)]
            )
        ]
        for copy in copies:
            copy.start()
        return copies

    ahead = [load(at) for at in range(slots - 1)]
    stored = []
    own_rows = [
        pltpu.make_async_copy(source, target, reads.at[at])
        for at, (source, target) in enumerate(
            [
                (branches_in, branches), (d_hidden_in, d_hidden), (x_in, x_own), (g_in, g_own),
                (small_in, small),
            ]
        )
    ]
    for copy in own_rows:
        copy.start()

    side = small.shape[2]

    def finish():
        take = slice(None)
        token = x_own[take, :].astype(F32)
        result[take, :] = (token + branches[take, :] + vec[2:3, :] + vec[3:4, :]).astype(BF16)
        centred = token - jnp.mean(token, axis=1, keepdims=True)
        inverse = lax.rsqrt(jnp.mean(centred * centred, axis=1, keepdims=True) + NORM_EPS)
        normed = centred * inverse
        scaled = d_hidden[take, :] * vec[0:1, :]
        input_grad[take, :] = g_own[take, :].astype(F32) + inverse * (
            scaled
            - jnp.mean(scaled, axis=1, keepdims=True)
            - normed * jnp.mean(scaled * normed, axis=1, keepdims=True)
        )

    for at in range(count):
        slot = at % slots
        for copy in ahead[at]:
            copy.wait()
        if at + slots - 1 < count:
            ahead.append(load(at + slots - 1))
        if at >= slots:
            for copy in stored[at - slots]:
                copy.wait()
        half = own // 2
        for core in range(2):
            for part in range(3):
                first = part * own + core * half
                qkv_wide[slot, :, first : first + half] = in_low[
                    slot, core, :, part * half : (part + 1) * half
                ].astype(F32)
            fc2_wide[slot, core * (fc2_step // 2) : (core + 1) * (fc2_step // 2), :] = fc2_low[
                slot, core
            ].astype(F32)
            dense_wide[slot, core] = dense_low[slot, core].astype(F32)
        for part in range(count // 2):
            first = cut + part * 128
            left = in_low[slot, 0, :, first : first + 128].astype(F32)
            right = in_low[slot, 1, :, first : first + 128].astype(F32)
            fc1_wide[slot, :, 2 * part * 128 : (2 * part + 1) * 128] = fold(left, right, True)
            fc1_wide[slot, :, (2 * part + 1) * 128 : (2 * part + 2) * 128] = fold(left, right, False)
        targets = [
            (
                qkv_wide.at[slot, :, pl.ds(part * own, own)],
                qkv.at[:, pl.ds((part * count + at) * own, own)],
            )
            for part in range(3)
        ] + [
            (
                fc1_wide.at[slot, :, pl.ds(part * 128, 128)],
                fc1.at[:, pl.ds(part * units + at * 128, 128)],
            )
            for part in range(count)
        ] + [
            (fc2_wide.at[slot], fc2.at[pl.ds(at * fc2_step, fc2_step)]),
        ] + [
            (
                dense_wide.at[slot, core],
                dense.at[pl.ds((core * count + at) * dense_step, dense_step)],
            )
            for core in range(2)
        ]
        copies = [
            pltpu.make_async_copy(source, target, stores.at[slot, number])
            for number, (source, target) in enumerate(targets)
        ]
        for copy in copies:
            copy.start()
        stored.append(copies)
        if at == 2:
            for copy in own_rows:
                copy.wait()
            for shard in range(small.shape[0]):
                vec[0:4, shard * side : (shard + 1) * side] = small[shard, 0:4, :]
            finish()
    writes = [
        pltpu.make_async_copy(result, result_to, reads.at[0]),
        pltpu.make_async_copy(input_grad, input_grad_to, reads.at[1]),
    ]
    for copy in writes:
        copy.start()
    for copies in stored[-slots:]:
        for copy in copies:
            copy.wait()
    for copy in writes:
        copy.wait()


def widen(in_all, fc2_all, dense_all, branches, d_hidden, tokens, cotangent, small, ff):
    any_ = pl.BlockSpec(memory_space=pl.ANY)
    rows, width = tokens.shape
    fsdp = small.shape[0]
    slots = 3
    side = width // fsdp
    shapes = [(side, 3 * width), (side, ff), (side, width), (ff // fsdp, width)]
    return pl.pallas_call(
        widen_kernel,
        out_shape=tuple(jax.ShapeDtypeStruct(shape, F32) for shape in shapes)
        + (jax.ShapeDtypeStruct((rows, width), BF16), jax.ShapeDtypeStruct((rows, width), F32)),
        in_specs=[any_] * 8,
        out_specs=(any_,) * 6,
        scratch_shapes=[
            pltpu.VMEM((slots, 2) + in_all.shape[1:], BF16),
            pltpu.VMEM((slots, 2) + fc2_all.shape[1:], BF16),
            pltpu.VMEM((slots, 2) + dense_all.shape[1:], BF16),
            pltpu.VMEM((slots, side, 3 * width // fsdp), F32),
            pltpu.VMEM((slots, side, ff // fsdp), F32),
            pltpu.VMEM((slots, ff // fsdp // fsdp, width), F32),
            pltpu.VMEM((slots, 2) + dense_all.shape[1:], F32),
            pltpu.VMEM((8, width), F32),
            pltpu.VMEM((rows, width), F32),
            pltpu.VMEM((rows, width), F32),
            pltpu.VMEM((rows, width), BF16),
            pltpu.VMEM((rows, width), BF16),
            pltpu.VMEM(small.shape, F32),
            pltpu.VMEM((rows, width), BF16),
            pltpu.VMEM((rows, width), F32),
            pltpu.SemaphoreType.DMA((slots, 3)),
            pltpu.SemaphoreType.DMA((slots, 14)),
            pltpu.SemaphoreType.DMA((5,)),
        ],
        compiler_params=pltpu.CompilerParams(vmem_limit_bytes=62 * MIB),
        name="widen",
    )(in_all, fc2_all, dense_all, branches, d_hidden, tokens, cotangent, small)


def on_device(
    tokens, cotangent, block_order, positions, ln_gain, ln_bias, w_qkv, b_qkv, w_dense, b_dense,
    w_fc1, b_fc1, w_fc2, b_fc2,
):
    ctx, fsdp = lax.axis_size("ctx"), lax.axis_size("fsdp")
    f = lax.axis_index("fsdp")
    rows, width = tokens.shape[1:]
    seq = rows * ctx
    ff = w_fc1.shape[1]
    own_width, own_ff = width // ctx, ff // ctx
    own_rows = width // fsdp
    cut = 3 * own_width
    tokens = tokens.reshape(rows, width)
    cotangent = cotangent.reshape(rows, width)

    vectors = (ln_gain, ln_bias, b_dense, b_fc2, b_qkv, b_fc1)
    small, used = jnp.zeros((32 * own_rows,), BF16), 0
    for vector in vectors:
        left = small.shape[0] - used - vector.shape[0]
        small = small + jnp.pad(vector, (used, left))
        used += vector.shape[0]
    small = small.reshape(32, own_rows)
    spread = turn_spread(own_width)
    (
        x_all, g_all, hidden, stat, queries, keys, values, d_att, act, d_up, w_in, fc2, dense, turns,
        small,
    ) = first(
        tokens, cotangent, turn_rows(positions.reshape(rows), own_width), w_qkv, w_fc1, w_dense, w_fc2,
        small, spread, ctx, fsdp,
    )
    att, d_proj = attention(
        block_order, seq // block_order.shape[0], queries, keys, values, d_att,
        turns.reshape(seq, own_width), spread,
    )
    branches, d_hidden, in_all, fc2_all, dense_all, vector = second(
        att, act, d_proj, d_up, w_in.reshape(width, -1), fc2.reshape(own_ff, width),
        dense.reshape(own_width, width), stat, cotangent, x_all, g_all, hidden, fsdp,
    )
    grad_qkv, grad_fc1, grad_dense, grad_fc2, result, input_grad = widen(
        in_all, fc2_all, dense_all, branches, d_hidden, tokens, cotangent, small, ff
    )

    vector = vector.reshape(ctx, -1)
    sums = jnp.sum(vector[:, : 3 * width], axis=0).reshape(3, width)
    sums = lax.dynamic_slice_in_dim(sums, f * own_rows, own_rows, 1)
    columns = vector[:, 3 * width : 3 * width + cut].reshape(ctx, 3, own_width)
    columns = columns.transpose(1, 0, 2).reshape(3 * width)
    units = vector[:, 3 * width + cut : 3 * width + cut + own_ff].reshape(ctx, fsdp, -1)
    units = lax.dynamic_slice_in_dim(units, f, 1, 1).reshape(ff // fsdp)
    return (
        result.reshape(1, rows, width),
        input_grad.reshape(1, rows, width),
        sums[0],
        sums[1],
        grad_qkv,
        lax.dynamic_slice_in_dim(columns, f * (3 * own_rows), 3 * own_rows, 0),
        grad_dense,
        sums[2],
        grad_fc1,
        units,
        grad_fc2,
        sums[2],
    )


def solution(mesh):
    split = P("fsdp", "ctx", None)
    matrix = P("fsdp", None)
    vector = P("fsdp")
    return jax.shard_map(
        on_device,
        mesh=mesh,
        in_specs=(split, split, P(), P("fsdp", "ctx"), vector, vector)
        + (matrix, vector) * 4,
        out_specs=(split, split, vector, vector) + (matrix, vector) * 4,
        check_vma=False,
    )
```

```python
import functools

import jax
import jax.numpy as jnp
import numpy as np
from jax import lax
from jax.experimental import pallas as pl
from jax.experimental.pallas import tpu as pltpu
from jax.sharding import PartitionSpec as P

HEAD_DIM = 64
ROTARY = 32
NORM_EPS = 1e-05
ROPE_BASE = 10000.0
GELU_COEF = 0.7978845608028654
F32 = jnp.float32
BF16 = jnp.bfloat16
STRIP = 256
NT = (((1,), (1,)), ((), ()))
TN = (((0,), (0,)), ((), ()))
MESH = pl.DeviceIdType.MESH
MIB = 1024 * 1024


def nt_dot(left, right):
    return lax.dot_general(left, right, NT, preferred_element_type=F32)


def tn_dot(left, right):
    return lax.dot_general(left, right, TN, preferred_element_type=F32)


def dot(left, right):
    return jnp.dot(left, right, preferred_element_type=F32)


def turn_rows(positions, width):
    half = ROTARY // 2
    frequency = ROPE_BASE ** (-(jnp.arange(half, dtype=F32) * (2.0 / ROTARY)))
    turned = positions.astype(F32)[:, None] * frequency
    both = jnp.concatenate([jnp.cos(turned), jnp.sin(turned)], axis=1)
    coarse = both.astype(BF16)
    fine = (both - coarse.astype(F32)).astype(BF16)
    rows = positions.shape[0]
    used = 4 * half + 1
    return jnp.concatenate(
        [coarse, fine, jnp.ones((rows, 1), BF16), jnp.zeros((rows, width - used), BF16)], axis=1
    )


def turn_spread(width):
    half = ROTARY // 2
    table = np.zeros((width, 3 * width), np.float32)
    for column in range(width):
        at = column % HEAD_DIM
        if at >= ROTARY:
            table[4 * half, column] = 1.0
            continue
        for part in (0, 2 * half):
            table[part + at % half, column] = 1.0
            if at < half:
                table[part + half + at, width + column] = -1.0
            else:
                table[part + half + at - half, 2 * width + column] = 1.0
    return jnp.asarray(table, BF16)


def turn(values, tables, back):
    width = values.shape[1]
    half = ROTARY // 2
    same, after, before = (tables[:, at * width : (at + 1) * width] for at in range(3))
    moved = pltpu.roll(values, width - half, 1) * after + pltpu.roll(values, half, 1) * before
    return values * same - moved if back else values * same + moved


AWAY = [(dx, flip) for dx in range(4) for flip in (False, True) if dx or flip]


def fold(left, right, first):
    lane = lax.broadcasted_iota(jnp.int32, left.shape, 1)
    half = left.shape[1] // 2
    return jnp.where(
        lane < half,
        jnp.where(first, left, pltpu.roll(left, half, 1)),
        jnp.where(first, pltpu.roll(right, half, 1), right),
    )


class Place:
    def __init__(self):
        self.c, self.f = lax.axis_index("ctx"), lax.axis_index("fsdp")
        self.y, self.z, self.core = self.c // 4, (self.c // 2) % 2, self.c % 2
        self.x, self.half = self.f // 2, self.f % 2

    def block(self, dy, flip, other=False):
        core = 1 - self.core if other else self.core
        return ((self.y + dy) % 4) * 4 + (1 - self.z if flip else self.z) * 2 + core

    def shard(self, dx, flip):
        return ((self.x + dx) % 4) * 2 + (1 - self.half if flip else self.half)

    def to_ctx(self, dy, flip, other=False):
        return (self.block(dy, flip, other), self.f)

    def to_fsdp(self, dx, flip):
        return (self.c, self.shard(dx, flip))

    def to_swap(self):
        return (2 * self.f + self.c % 2, self.c // 2)


class Post:
    def __init__(self, place, send, recv):
        self.place, self.send, self.recv, self.started = place, send, recv, []
        self.left = set()

    def copy(self, source, target, device):
        at = len(self.started)
        copy = pltpu.make_async_remote_copy(
            src_ref=source, dst_ref=target, send_sem=self.send.at[at], recv_sem=self.recv.at[at],
            device_id=device, device_id_type=MESH,
        )
        self.started.append(copy)
        copy.start()
        return copy

    def greet(self):
        place = self.place
        barrier = pltpu.get_barrier_semaphore()
        partners = [
            place.to_ctx(1, False), place.to_ctx(-1, False), place.to_ctx(0, True),
            place.to_ctx(0, False, True),
        ] + [place.to_fsdp(*to) for to in AWAY]
        for partner in partners:
            pl.semaphore_signal(barrier, inc=1, device_id=partner, device_id_type=MESH)
        swap = place.to_swap()
        same = jnp.logical_and(swap[0] == place.c, swap[1] == place.f)

        @pl.when(jnp.logical_not(same))
        def _():
            pl.semaphore_signal(barrier, inc=1, device_id=swap, device_id_type=MESH)

        pl.semaphore_wait(barrier, len(partners) + jnp.where(same, 0, 1))

    def has_left(self, copy):
        copy.wait_send()
        self.left.add(id(copy))

    def close(self):
        for copy in self.started:
            if id(copy) not in self.left:
                copy.wait_send()


def gather_ctx(post, own, buf, cut, early=False):
    place = post.place
    here = post.place.block(0, False)
    crossed = []

    def send(at, *to):
        return post.copy(buf.at[at], buf.at[at], place.to_ctx(*to))

    def cross(at):
        crossed.append(post.copy(buf.at[at], buf.at[at], place.to_ctx(0, False, True)))

    def first(*to):
        return post.copy(own, buf.at[here], place.to_ctx(*to))

    to_next, to_last, to_pair = first(1, False), first(-1, False), first(0, True)
    crossed.append(first(0, False, True))
    yield
    last, after = place.block(-1, False), place.block(1, False)
    rest = buf.shape[1] - cut
    lower, upper = pl.ds(0, cut), pl.ds(cut, rest)
    to_next.wait_recv()
    halves = [post.copy(buf.at[last, lower], buf.at[last, lower], place.to_ctx(1, False))]
    to_last.wait_recv()
    if rest:
        piece = buf.at[after, upper]
        halves.append(post.copy(piece, piece, place.to_ctx(-1, False)))
    cross(last)
    cross(after)
    yield
    to_pair.wait_recv()
    pair = place.block(0, True)
    pair_next, pair_last = send(pair, 1, False), send(pair, -1, False)
    cross(pair)
    yield
    for copy in halves:
        copy.wait_recv()
    far = place.block(2, False)
    pair_far = send(far, 0, True)
    cross(far)
    waited = 0
    if early:
        waited = 4
        for copy in crossed[:4]:
            copy.wait_recv()
    yield
    pair_next.wait_recv()
    cross(place.block(-1, True))
    pair_last.wait_recv()
    cross(place.block(1, True))
    yield
    pair_far.wait_recv()
    cross(place.block(2, True))
    if early:
        waited = 7
        for copy in crossed[4:7]:
            copy.wait_recv()
    yield
    for copy in crossed[waited:]:
        copy.wait_recv()


def gather_fsdp(post, own, buf, cut):
    place = post.place
    here = place.shard(0, False)
    rest = buf.shape[1] - cut

    def whole(at, dx):
        return post.copy(buf.at[at], buf.at[at], place.to_fsdp(dx, False))

    def lower(at):
        piece = buf.at[at, pl.ds(0, cut)]
        return post.copy(piece, piece, place.to_fsdp(1, False))

    def upper(at):
        piece = buf.at[at, pl.ds(cut, rest)]
        return post.copy(piece, piece, place.to_fsdp(-1, False))

    to_pair = post.copy(own, buf.at[here], place.to_fsdp(0, True))
    to_next = post.copy(own, buf.at[here], place.to_fsdp(1, False))
    to_last = post.copy(own, buf.at[here], place.to_fsdp(-1, False))
    yield
    to_next.wait_recv()
    halves = [lower(place.shard(-1, False))]
    to_last.wait_recv()
    if rest:
        halves.append(upper(place.shard(1, False)))
    yield
    to_pair.wait_recv()
    pair = place.shard(0, True)
    pair_next, pair_last = whole(pair, 1), whole(pair, -1)
    yield
    pair_next.wait_recv()
    halves.append(lower(place.shard(-1, True)))
    pair_last.wait_recv()
    if rest:
        halves.append(upper(place.shard(1, True)))
    yield
    for copy in halves:
        copy.wait_recv()


def gather_direct(post, own, buf):
    place = post.place
    here = place.shard(0, False)
    copies = [post.copy(own, buf.at[here], place.to_fsdp(*to)) for to in AWAY]
    yield
    for copy in copies:
        copy.wait_recv()


class Swap:
    def __init__(self, place, source, target, send, recv, local):
        device = place.to_swap()
        self.same = jnp.logical_and(device[0] == place.c, device[1] == place.f)
        self.away = pltpu.make_async_remote_copy(
            src_ref=source, dst_ref=target, send_sem=send, recv_sem=recv, device_id=device,
            device_id_type=MESH,
        )
        self.stay = pltpu.make_async_copy(source, target, local)
        pl.when(jnp.logical_not(self.same))(lambda: self.away.start())
        pl.when(self.same)(lambda: self.stay.start())

    def wait(self):
        pl.when(jnp.logical_not(self.same))(lambda: self.away.wait())
        pl.when(self.same)(lambda: self.stay.wait())


def first_kernel(
    x_in, g_in, turn_in, w_qkv, w_fc1, w_dense, w_fc2, small_in, spread,
    x_to, g_to, hidden_to, stat_to, q_to, k_to, v_to, d_att_to, act_to, d_up_to, w_in_to, fc2_to,
    dense_to,
    turns_to, small_to,
    x_all, g_all, hidden, stat, q_out, k_out, v_out, d_att, act, d_up, w_in, fc2, dense,
    turns, small_out,
    wide_rows, in_rows, fc2_rows, dense_rows, piece, small_all, tables, proj, slope, vec, bias,
    send, recv, local, reads, swap_send, swap_recv,
):
    place = Place()
    post = Post(place, send, recv)
    rows, width = x_in.shape
    own_width = q_out.shape[1]
    own_ff = act.shape[1]
    cut = 3 * own_width
    here, shard = place.block(0, False), place.shard(0, False)

    def columns(first, count):
        return pl.ds(pl.multiple_of(first, 128), count)

    fsdp, fc2_step = fc2.shape[:2]
    dense_step = dense.shape[1]
    units = w_fc1.shape[1] // fsdp
    first_dense = (place.c % 2) * own_width + (place.c // 2) * dense_step
    first_fc2 = place.c * fc2_step
    sources = [
        (w_dense.at[pl.ds(pl.multiple_of(first_dense, 16), dense_step)], dense_rows),
        (w_fc2.at[pl.ds(pl.multiple_of(first_fc2, 16), fc2_step)], fc2_rows),
    ]
    for part in range(3):
        take = columns(part * width + place.c * own_width, own_width)
        sources.append((w_qkv.at[:, take], in_rows.at[:, pl.ds(part * own_width, own_width)]))
    for part in range(fsdp):
        take = columns(part * units + place.c // 2 * 128, 128)
        sources.append((w_fc1.at[:, take], wide_rows.at[:, pl.ds(part * 128, 128)]))
    ready = [
        pltpu.make_async_copy(source, target, reads.at[at])
        for at, (source, target) in enumerate(sources)
    ]
    for copy in ready:
        copy.start()
    post.greet()
    for copy in ready:
        copy.wait()
    swap = Swap(place, dense_rows, piece, swap_send, swap_recv, local.at[0])
    for part in range(fsdp // 2):
        left, right = (
            wide_rows[:, at * 128 : (at + 1) * 128].astype(F32) for at in (2 * part, 2 * part + 1)
        )
        in_rows[:, cut + part * 128 : cut + (part + 1) * 128] = fold(
            left, right, place.core == 0
        ).astype(BF16)
    keeps = []

    def keep(source, target):
        copy = pltpu.make_async_copy(source, target, local.at[1 + len(keeps)])
        keeps.append(copy)
        copy.start()
        return copy

    own = [
        keep(x_in, x_all.at[here]), keep(in_rows, w_in.at[shard]), keep(turn_in, turns.at[here]),
        keep(small_in, small_all.at[shard]), keep(g_in, g_all.at[here]),
        keep(fc2_rows, fc2.at[shard]),
    ]
    x_flow = gather_ctx(post, x_in, x_all, rows // 2, early=True)
    in_flow = gather_fsdp(post, in_rows, w_in, in_rows.shape[0] // 2)
    small_flow = gather_direct(post, small_in, small_all)
    turn_flow = gather_ctx(post, turn_in, turns, rows // 2)
    def advance(*flows):
        for flow in flows:
            next(flow, None)

    advance(x_flow, in_flow, small_flow, turn_flow)
    advance(x_flow, in_flow)
    swap.wait()
    keep(piece, dense.at[shard])
    dense_flow = gather_fsdp(post, piece, dense, dense_step)
    advance(dense_flow, x_flow, in_flow, turn_flow)
    g_flow = gather_ctx(post, g_in, g_all, rows // 2)
    fc2_flow = gather_fsdp(post, fc2_rows, fc2, fc2_step // 2)
    advance(g_flow, fc2_flow)
    for _ in small_flow:
        pass
    for copy in own[:4]:
        copy.wait()

    side = small_all.shape[2]
    small_out[...] = small_all[...].astype(F32)
    for at in range(small_all.shape[0]):
        vec[0:2, at * side : (at + 1) * side] = small_out[at, 0:2, :]
    for part in range(3):
        first = part * width + place.c * own_width
        count = 3 * side
        row = small_out[first // count, pl.ds(4 + (first % count) // side, 1), :]
        bias[0:1, part * own_width : (part + 1) * own_width] = jnp.where(
            first % side == 0, row[:, :own_width], row[:, own_width:]
        )
    quarter = place.c % 4
    pieces = []
    for part in range(fsdp):
        row = small_out[part, pl.ds(7 + place.c // 4, 1), :]
        row = jnp.where(quarter >= 2, row[:, 128:], row[:, :128])
        pieces.append(jnp.broadcast_to(row, (8, 128)))
    for part in range(fsdp // 2):
        row = fold(pieces[2 * part], pieces[2 * part + 1], quarter % 2 == 0)
        bias[0:1, cut + part * 128 : cut + (part + 1) * 128] = row[0:1, :]

    def normalise(block):
        lane = lax.broadcasted_iota(jnp.int32, (rows, stat.shape[1]), 1)
        target = pl.ds(pl.multiple_of(block * rows, rows), rows)
        value = x_all[block].astype(F32)
        mean = jnp.mean(value, axis=1, keepdims=True)
        centred = value - mean
        inverse = lax.rsqrt(jnp.mean(centred * centred, axis=1, keepdims=True) + NORM_EPS)
        hidden[target, :] = (centred * inverse * vec[0:1, :] + vec[1:2, :]).astype(BF16)
        stat[target, :] = jnp.where(lane < HEAD_DIM, mean, inverse)

    def normalise_each(targets):
        order = [place.block(*to) for to in targets]

        def body(at, carry):
            block = order[0]
            for number, other in enumerate(order[1:]):
                block = jnp.where(at == number + 1, other, block)
            normalise(block)
            return carry

        lax.fori_loop(0, len(order), body, 0)

    chunk_rows = proj.shape[0]
    group = chunk_rows // rows

    def project(chunk):
        take = pl.ds(pl.multiple_of(chunk * chunk_rows, chunk_rows), chunk_rows)
        weight = w_in[...].reshape(width, proj.shape[1])
        proj[...] = dot(hidden[take, :], weight)
        settle(chunk)

    def settle(chunk):
        turned = turns[pl.ds(chunk * group, group)].reshape(chunk_rows, own_width)
        tables[...] = dot(turned, spread[...])
        target = pl.ds(pl.multiple_of(chunk * chunk_rows, chunk_rows), chunk_rows)
        value = proj[...] + bias[0:1, :]
        table = tables[...]
        q_out[target, :] = turn(value[:, :own_width], table, False).astype(BF16)
        k_out[target, :] = turn(value[:, own_width : 2 * own_width], table, False).astype(BF16)
        v_out[target, :] = value[:, 2 * own_width : cut].astype(BF16)
        up = value[:, cut:]
        square = up * up
        curve = jnp.tanh(GELU_COEF * up * (1.0 + 0.044715 * square))
        act[target, :] = (0.5 * up * (1.0 + curve)).astype(BF16)
        slope[target, :] = 0.5 * (1.0 + curve) + 0.5 * up * (1.0 - curve * curve) * (
            GELU_COEF * (1.0 + 3.0 * 0.044715 * square)
        )

    chunks = hidden.shape[0] // chunk_rows
    normalise_each([(0, False), (1, False), (-1, False)])
    advance(x_flow, in_flow, turn_flow, g_flow, fc2_flow, dense_flow)
    normalise_each([(0, True), (0, False, True), (0, True, True)])
    for flow in (in_flow, turn_flow):
        for _ in flow:
            pass
    keep(w_in, w_in_to)
    keep(turns, turns_to)
    keep(small_out, small_to)
    advance(x_flow, g_flow, fc2_flow, dense_flow)
    project(place.y)
    advance(x_flow)
    normalise_each([(1, True), (1, False, True), (1, True, True), (2, False)])
    advance(g_flow)
    project((place.y + 1) % 4)
    advance(fc2_flow, dense_flow, x_flow)
    keep(x_all, x_to)
    normalise_each([(-1, True), (-1, False, True), (-1, True, True), (2, True)])
    project((place.y + 3) % 4)
    advance(g_flow)
    normalise_each([(2, False, True), (2, True, True)])
    keep(hidden, hidden_to)
    keep(stat, stat_to)
    project((place.y + 2) % 4)
    advance(g_flow)
    for target, source in ((q_to, q_out), (k_to, k_out), (v_to, v_out), (act_to, act)):
        keep(source, target)
    advance(fc2_flow, dense_flow)
    own[5].wait()
    keeps[6].wait()
    keep(fc2, fc2_to)
    keep(dense, dense_to)
    advance(g_flow)
    own[4].wait()
    keep(g_all, g_to)

    for chunk in range(chunks):
        grads = g_all[pl.ds(chunk * group, group)].reshape(chunk_rows, width)
        target = slice(chunk * chunk_rows, (chunk + 1) * chunk_rows)
        d_att[target, :] = nt_dot(grads, dense[...].reshape(own_width, width)).astype(BF16)
        d_act = nt_dot(grads, fc2[...].reshape(own_ff, width))
        d_up[target, :] = (d_act * slope[target, :]).astype(BF16)
    keep(d_att, d_att_to)
    keep(d_up, d_up_to)
    for copy in keeps[7:]:
        copy.wait()
    post.close()


def first(tokens, cotangent, turns, w_qkv, w_fc1, w_dense, w_fc2, small, spread, ctx, fsdp):
    rows, width = tokens.shape
    seq = ctx * rows
    own_width, own_ff = turns.shape[1], w_fc1.shape[1] // ctx
    columns = 3 * own_width + own_ff
    side = width // fsdp
    many = 3 * 16 + 3 * 9 + fsdp - 1
    any_, vmem = pl.BlockSpec(memory_space=pl.ANY), pl.BlockSpec(memory_space=pltpu.VMEM)

    def low(*shape):
        return jax.ShapeDtypeStruct(shape, BF16)

    def wide(*shape):
        return jax.ShapeDtypeStruct(shape, F32)

    outs = [
        low(ctx, rows, width), low(ctx, rows, width), low(seq, width), wide(seq, 128),
        low(seq, own_width), low(seq, own_width), low(seq, own_width), low(seq, own_width),
        low(seq, own_ff), low(seq, own_ff), low(fsdp, side, columns),
        low(fsdp, own_ff // fsdp, width), low(fsdp, own_width // fsdp, width),
        low(ctx, rows, own_width), wide(*((fsdp,) + small.shape)),
    ]
    chunk_rows = 4 * rows
    return pl.pallas_call(
        first_kernel,
        out_shape=tuple(outs),
        in_specs=[any_] * 8 + [vmem],
        out_specs=(any_,) * len(outs),
        scratch_shapes=[pltpu.VMEM(out.shape, out.dtype) for out in outs]
        + [
            pltpu.VMEM((side, fsdp * 128), BF16),
            pltpu.VMEM((side, columns), BF16),
            pltpu.VMEM((own_ff // fsdp, width), BF16),
            pltpu.VMEM((own_width // fsdp, width), BF16),
            pltpu.VMEM((own_width // fsdp, width), BF16),
            pltpu.VMEM((fsdp,) + small.shape, BF16),
            pltpu.VMEM((chunk_rows, 3 * own_width), F32),
            pltpu.VMEM((chunk_rows, columns), F32),
            pltpu.VMEM((seq, own_ff), F32),
            pltpu.VMEM((8, width), F32),
            pltpu.VMEM((8, columns), F32),
            pltpu.SemaphoreType.DMA((many,)),
            pltpu.SemaphoreType.DMA((many,)),
            pltpu.SemaphoreType.DMA((24,)),
            pltpu.SemaphoreType.DMA((5 + fsdp,)),
            pltpu.SemaphoreType.DMA,
            pltpu.SemaphoreType.DMA,
        ],
        compiler_params=pltpu.CompilerParams(
            collective_id=0, has_side_effects=True, vmem_limit_bytes=60 * MIB
        ),
        name="first",
    )(tokens, cotangent, turns, w_qkv, w_fc1, w_dense, w_fc2, small, spread)


def attention_kernel(
    block, order, q_hbm, k_hbm, v_hbm, g_hbm, turns_hbm, spread, o_to, d_to,
    q_in, k_in, v_in, g_in, turns, o_out, d_out, loads, qs, ks, vs, gs, os, dqs, dks, dvs, kt, vt, table,
):
    rows, width = q_in.shape
    blocks = rows // block
    reads = [
        pltpu.make_async_copy(source, target, loads.at[at])
        for at, (source, target) in enumerate(
            [(q_hbm, q_in), (k_hbm, k_in), (v_hbm, v_in), (g_hbm, g_in), (turns_hbm, turns)]
        )
    ]
    for copy in reads:
        copy.start()
    for copy in reads[:4]:
        copy.wait()

    def collect(at, carry):
        src = pl.ds(pl.multiple_of(at * block, block), block)
        dst = pl.ds(pl.multiple_of(order[at] * block, block), block)
        qs[dst, :] = q_in[src, :]
        ks[dst, :] = k_in[src, :]
        vs[dst, :] = v_in[src, :]
        gs[dst, :] = g_in[src, :]
        return carry

    lax.fori_loop(0, blocks, collect, 0, unroll=4)
    dks[...] = jnp.zeros_like(dks)
    dvs[...] = jnp.zeros_like(dvs)
    heads = width // HEAD_DIM
    scale = HEAD_DIM ** (-0.5)
    q_pos = lax.broadcasted_iota(jnp.int32, (STRIP, STRIP), 0)
    k_pos = lax.broadcasted_iota(jnp.int32, (STRIP, STRIP), 1)
    diagonal = q_pos <= k_pos
    reads[4].wait()
    table[...] = dot(turns[...], spread[...])
    kt[...] = ks[...].T
    vt[...] = vs[...].T
    sides = [slice(head * HEAD_DIM, (head + 1) * HEAD_DIM) for head in range(heads)]
    strips = rows // STRIP

    def begin(strip):
        here = slice(strip * STRIP, (strip + 1) * STRIP)
        count = (strip + 1) * STRIP
        query = [qs[here, cols] * jnp.asarray(scale, BF16) for cols in sides]
        part = [nt_dot(ks[:count, cols], query[h]) for h, cols in enumerate(sides)]
        return query, part

    ready = begin(0)
    for strip in range(strips):
        here = slice(strip * STRIP, (strip + 1) * STRIP)
        count = (strip + 1) * STRIP
        query, part = ready
        edge = [jnp.where(diagonal, p[count - STRIP :, :], -1e30) for p in part]
        part = [jnp.concatenate([p[: count - STRIP, :], e], axis=0) if strip else e for p, e in zip(part, edge)]
        part = [jnp.exp(p - jnp.max(p, axis=0, keepdims=True)) for p in part]
        inverse = [1.0 / jnp.sum(p, axis=0, keepdims=True) for p in part]
        low = [p.astype(BF16) for p in part]
        mixed = [dot(vt[cols, :count], low[h]) * inverse[h] for h, cols in enumerate(sides)]
        grad = [gs[here, cols].astype(F32).T * inverse[h] for h, cols in enumerate(sides)]
        centre = [jnp.sum(g * m, axis=0, keepdims=True) for g, m in zip(grad, mixed)]
        os[here, :] = jnp.concatenate(mixed, axis=0).T.astype(BF16)
        grad = [g.astype(BF16) for g in grad]
        if strip + 1 < strips:
            ready = begin(strip + 1)
        d_score = [(part[h] * (dot(vs[:count, cols], grad[h]) - centre[h])).astype(BF16) for h, cols in enumerate(sides)]
        dqs[here, :] = jnp.concatenate([dot(kt[cols, :count], d_score[h]) for h, cols in enumerate(sides)], axis=0).T * scale
        dks[:count, :] += jnp.concatenate([dot(d_score[h], query[h]) for h in range(heads)], axis=1)
        dvs[:count, :] += jnp.concatenate([nt_dot(low[h], grad[h]) for h in range(heads)], axis=1)

    def give(at, carry):
        src = pl.ds(pl.multiple_of(order[at] * block, block), block)
        dst = pl.ds(pl.multiple_of(at * block, block), block)
        tables = table[dst, :]
        o_out[dst, :] = os[src, :]
        d_out[dst, :width] = turn(dqs[src, :], tables, True).astype(BF16)
        d_out[dst, width : 2 * width] = turn(dks[src, :], tables, True).astype(BF16)
        d_out[dst, 2 * width :] = dvs[src, :].astype(BF16)
        return carry

    writes = []
    parts = 4
    for part in range(parts):
        lax.fori_loop(part * blocks // parts, (part + 1) * blocks // parts, give, 0, unroll=4)
        take = pl.ds(part * rows // parts, rows // parts)
        for number, (source, target) in enumerate(((o_out, o_to), (d_out, d_to))):
            copy = pltpu.make_async_copy(
                source.at[take], target.at[take], loads.at[5 + 2 * part + number]
            )
            copy.start()
            writes.append(copy)
    for copy in writes:
        copy.wait()


def attention(order, block, queries, keys, values, grads, turns, spread):
    rows, width = queries.shape
    vmem = pl.BlockSpec(memory_space=pltpu.VMEM)
    smem = pl.BlockSpec(memory_space=pltpu.SMEM)
    any_ = pl.BlockSpec(memory_space=pl.ANY)
    return pl.pallas_call(
        functools.partial(attention_kernel, block),
        out_shape=(
            jax.ShapeDtypeStruct((rows, width), BF16),
            jax.ShapeDtypeStruct((rows, 3 * width), BF16),
        ),
        in_specs=[smem] + [any_] * 5 + [vmem],
        out_specs=(any_, any_),
        scratch_shapes=[pltpu.VMEM((rows, width), BF16)] * 6
        + [pltpu.VMEM((rows, 3 * width), BF16), pltpu.SemaphoreType.DMA((13,))]
        + [pltpu.VMEM((rows, width), BF16)] * 5
        + [pltpu.VMEM((rows, width), F32)] * 3
        + [pltpu.VMEM((width, rows), BF16), pltpu.VMEM((width, rows), BF16)]
        + [pltpu.VMEM((rows, 3 * width), F32)],
        compiler_params=pltpu.CompilerParams(vmem_limit_bytes=60 * MIB),
        cost_estimate=pl.CostEstimate(
            flops=6 * rows * rows * width,
            bytes_accessed=rows * width * 22,
            transcendentals=rows * rows * width // HEAD_DIM // 2,
        ),
        name="attention",
    )(order, queries, keys, values, grads, turns, spread)


ORDER = [(2, True), (1, True), (-1, True), (2, False), (0, True), (1, False), (-1, False), (0, False)]
SHARDS = [(2, True), (2, False), (1, True), (-1, True), (1, False), (-1, False), (0, True), (0, False)]


def add_into(target, *parts):
    step = 64 if target.shape[0] % 64 == 0 else target.shape[0]
    plain = len(parts) == 2 and target.dtype == BF16

    def body(at, carry):
        take = pl.ds(pl.multiple_of(at * step, step), step)
        if plain:
            target[take, :] = parts[0][take, :] + parts[1][take, :]
            return carry
        total = parts[0][take, :].astype(F32)
        for part in parts[1:]:
            total = total + part[take, :].astype(F32)
        target[take, :] = total.astype(target.dtype)
        return carry

    lax.fori_loop(0, target.shape[0] // step, body, 0)


def reduce_ctx(post, own, core, crossed, pair_in, half_in, ring_in, cross_in, last_in, total):
    place = post.place
    cut = half_in.shape[1]
    up, down, pair = place.to_ctx(1, False), place.to_ctx(-1, False), place.to_ctx(0, True)

    def meet(at, *more):
        crossed[at].wait_recv()
        add_into(core.at[at], own.at[at], core.at[at], *more)

    meet(0)
    far = post.copy(core.at[0], pair_in, pair)
    yield
    meet(1)
    cross_next = post.copy(core.at[1], cross_in.at[0], up)
    meet(2)
    cross_last = post.copy(core.at[2], cross_in.at[1], down)
    yield
    far.wait_recv()
    meet(3, pair_in)
    low = post.copy(core.at[3, pl.ds(0, cut)], half_in.at[0], up)
    high = post.copy(core.at[3, pl.ds(cut, cut)], half_in.at[1], down)
    yield
    cross_next.wait_recv()
    cross_last.wait_recv()
    meet(4, cross_in.at[0], cross_in.at[1])
    last = post.copy(core.at[4], last_in, pair)
    yield
    meet(5)
    low.wait_recv()
    lower = core.at[5, pl.ds(0, cut)]
    add_into(lower, lower, half_in.at[0])
    ring_next = post.copy(core.at[5], ring_in.at[0], up)
    meet(6)
    high.wait_recv()
    upper = core.at[6, pl.ds(cut, cut)]
    add_into(upper, upper, half_in.at[1])
    ring_last = post.copy(core.at[6], ring_in.at[1], down)
    yield
    crossed[7].wait_recv()
    last.wait_recv()
    ring_next.wait_recv()
    ring_last.wait_recv()
    add_into(total, own.at[7], core.at[7], ring_in.at[0], ring_in.at[1], last_in)


def reduce_fsdp(post, part, low_in, high_in, ring_in, pair_in, total):
    place = post.place
    cut, rest = low_in.shape[1], high_in.shape[1]
    lower, upper = pl.ds(0, cut), pl.ds(cut, rest)
    up, down, pair = place.to_fsdp(1, False), place.to_fsdp(-1, False), place.to_fsdp(0, True)
    halves = [
        (
            post.copy(part.at[side, lower], low_in.at[side], up),
            post.copy(part.at[side, upper], high_in.at[side], down),
        )
        for side in range(2)
    ]
    yield
    rings = []
    for side in range(2):
        low, high = halves[side]
        after, before = part.at[2 + 2 * side], part.at[3 + 2 * side]
        low.wait_recv()
        add_into(after.at[lower], after.at[lower], low_in.at[side])
        to_next = post.copy(after, ring_in.at[side, 0], up)
        high.wait_recv()
        add_into(before.at[upper], before.at[upper], high_in.at[side])
        to_last = post.copy(before, ring_in.at[side, 1], down)
        rings.append((to_next, to_last))
        yield
    for copy in rings[0]:
        copy.wait_recv()
    add_into(part.at[6], part.at[6], ring_in.at[0, 0], ring_in.at[0, 1])
    across = post.copy(part.at[6], pair_in, pair)
    yield
    for copy in rings[1]:
        copy.wait_recv()
    across.wait_recv()
    add_into(total, part.at[7], ring_in.at[1, 0], ring_in.at[1, 1], pair_in)


def run(*flows):
    flows = list(flows)
    while flows:
        flows = [flow for flow in flows if next(flow, flows) is not flows]


def second_kernel(
    att_in, act_in, d_proj_in, d_up_in, w_in_in, w_fc2_in, w_dense_in, stat_in, g_own_in, x_all, g_all, hidden,
    out_total, hid_total, in_all, fc2_all, dense_all, vector_all,
    att, act, d_proj, d_up, w_in, w_fc2, w_dense, stat, g_own,
    own_a, own_b, core_a, core_b, slot_a, slot_b,
    pair_a, half_a, ring_a, cross_a, last_a, pair_b, half_b, ring_b, cross_b, last_b,
    in_part, in_low, in_high, in_ring, in_pair, in_sum,
    out_part, out_low, out_high, out_ring, out_pair, out_sum, out_piece,
    column, x_block, total_a, total_b, gain_sum, shift_sum,
    vector, vector_shards, vector_sum,
    send, recv, local, loads, reads, swap_send, swap_recv,
):
    place = Place()
    post = Post(place, send, recv)
    rows, width = g_own.shape
    cut = d_proj.shape[1]
    side = in_part.shape[1]
    here, shard = place.block(0, False), place.shard(0, False)
    keeps, numbers = [], iter(range(7))

    def keep(source, target):
        copy = pltpu.make_async_copy(source, target, local.at[next(numbers)])
        keeps.append(copy)
        copy.start()
        return copy

    operands = [
        pltpu.make_async_copy(source, target, reads.at[at])
        for at, (source, target) in enumerate(
            [
                (d_proj_in, d_proj), (d_up_in, d_up), (att_in, att), (act_in, act), (w_fc2_in, w_fc2),
                (w_dense_in, w_dense),
                (w_in_in, w_in), (stat_in, stat), (g_own_in, g_own),
            ]
        )
    ]

    def load_x(at):
        dy, flip = ORDER[at]
        block = place.block(dy, flip) // 2
        copy = pltpu.make_async_copy(
            x_all.at[pl.ds(2 * block, 2)], x_block.at[at % 2], loads.at[at % 2]
        )
        copy.start()
        return copy

    ahead = column.shape[0]

    def load_column(at):
        if at < len(SHARDS):
            first = pl.multiple_of(place.shard(*SHARDS[at]) * side, side)
            source = hidden.at[:, pl.ds(first, side)]
        else:
            source = g_all.at[:, pl.ds((at - len(SHARDS)) * side, side)]
        copy = pltpu.make_async_copy(source, column.at[at % ahead], loads.at[2 + at % ahead])
        copy.start()
        return copy

    for copy in operands[:2]:
        copy.start()
    pending_column = [load_column(at) for at in range(ahead - 1)]
    pending_x = [load_x(0)]
    for copy in operands[2:]:
        copy.start()
    post.greet()
    gain_sum[...] = jnp.zeros_like(gain_sum)
    shift_sum[...] = jnp.zeros_like(shift_sum)
    crossed_a, crossed_b, slots = {}, {}, {}
    partner = place.to_ctx(0, False, True)
    depth = slot_a.shape[0]

    def produce(at):
        dy, flip = ORDER[at]
        block = place.block(dy, flip) // 2
        pending_x.pop().wait()
        if at + 1 < len(ORDER):
            pending_x.append(load_x(at + 1))
        slot = at % depth
        if at >= depth:
            for copy in slots[at - depth]:
                post.has_left(copy)
        other_rows = pl.ds(pl.multiple_of(block * (2 * rows) + (1 - place.core) * rows, rows), rows)
        own_rows = pl.ds(pl.multiple_of(block * (2 * rows) + place.core * rows, rows), rows)

        def both(ref):
            return jnp.concatenate([ref[other_rows, :], ref[own_rows, :]], axis=0)

        left, right = both(att), both(act)
        span = width // 2
        for first in range(0, width, span):
            take = slice(first, first + span)
            value = dot(left, w_dense[:, take]) + dot(right, w_fc2[:, take])
            slot_a[slot, :, take] = value[:rows].astype(BF16)
            own_a[at, :, take] = value[rows:].astype(BF16)
        left, right, stats = both(d_proj), both(d_up), both(stat)
        mean, inverse = stats[:, 0:1], stats[:, HEAD_DIM : HEAD_DIM + 1]
        span = width // 4
        for first in range(0, width, span):
            take = slice(first, first + span)
            value = nt_dot(left, w_in[take, :cut]) + nt_dot(right, w_in[take, cut:])
            slot_b[slot, :, take] = value[:rows].astype(BF16)
            own_b[at, :, take] = value[rows:].astype(BF16)
            tokens = jnp.concatenate(
                [x_block[at % 2, 1 - place.core, :, take], x_block[at % 2, place.core, :, take]],
                axis=0,
            )
            normed = (tokens.astype(F32) - mean) * inverse
            parts = (2 * rows // 8, 8, span)
            gain_sum[:, take] += jnp.sum((value * normed).reshape(parts), axis=0)
            shift_sum[:, take] += jnp.sum(value.reshape(parts), axis=0)
        crossed_a[at] = post.copy(slot_a.at[slot], core_a.at[at], partner)
        crossed_b[at] = post.copy(slot_b.at[slot], core_b.at[at], partner)
        slots[at] = (crossed_a[at], crossed_b[at])

    def next_column(at):
        pending_column.pop(0).wait()
        if at + ahead - 1 < 2 * len(SHARDS):
            pending_column.append(load_column(at + ahead - 1))
        return column[at % ahead]

    def grad_in(at):
        rows_of = next_column(at)
        in_part[at, :, :cut] = tn_dot(rows_of, d_proj[...]).astype(BF16)
        in_part[at, :, cut:] = tn_dot(rows_of, d_up[...]).astype(BF16)

    def grad_out(at):
        columns = next_column(len(SHARDS) + at)
        take = slice(at * side, (at + 1) * side)
        dense = tn_dot(att[...], columns).astype(BF16)
        fc2 = tn_dot(act[...], columns).astype(BF16)
        dense_step, fc2_step = dense.shape[0] // len(SHARDS), fc2.shape[0] // len(SHARDS)
        for to in range(len(SHARDS)):
            out_part[to, :dense_step, take] = dense[to * dense_step : (to + 1) * dense_step]
            out_part[to, dense_step:, take] = fc2[to * fc2_step : (to + 1) * fc2_step]

    class ByShard:
        @property
        def at(self):
            return self

        def __getitem__(self, index):
            if isinstance(index, tuple):
                return out_part.at[(place.shard(*SHARDS[index[0]]),) + index[1:]]
            return out_part.at[place.shard(*SHARDS[index])]

    def in_flow():
        yield from reduce_fsdp(post, in_part, in_low, in_high, in_ring, in_pair, in_sum)
        keep(in_sum, in_all.at[here])
        yield from gather_ctx(post, in_sum, in_all, in_sum.shape[0] // 2)

    def out_flow():
        yield from reduce_fsdp(post, ByShard(), out_low, out_high, out_ring, out_pair, out_sum)
        first, count = dense_all.shape[1], fc2_all.shape[1]
        swap = Swap(
            place, out_sum.at[pl.ds(0, first)], out_piece, swap_send, swap_recv, local.at[7]
        )
        fc2_own = out_sum.at[pl.ds(first, count)]
        keep(fc2_own, fc2_all.at[here])
        flows = [gather_ctx(post, fc2_own, fc2_all, count // 2)]
        next(flows[0])
        yield
        next(flows[0])
        swap.wait()
        keep(out_piece, dense_all.at[here])
        flows.append(gather_ctx(post, out_piece, dense_all, first))
        while flows:
            flows = [flow for flow in flows if next(flow, flows) is not flows]
            yield

    def vector_flow():
        mine = keep(vector, vector_shards.at[shard])
        yield from gather_fsdp(post, vector, vector_shards, 8)
        mine.wait()
        keeps[:] = [kept for kept in keeps if kept is not mine]
        total = vector_shards[0]
        for at in range(1, vector_shards.shape[0]):
            total = total + vector_shards[at]
        vector_sum[...] = total
        keep(vector_sum, vector_all.at[here])
        yield from gather_ctx(post, vector_sum, vector_all, 8)

    def rows_flow(own, core, crossed, pair, half, ring, cross, last, total, target):
        yield from reduce_ctx(post, own, core, crossed, pair, half, ring, cross, last, total)
        keep(total, target)

    ins, outs = in_flow(), out_flow()
    a = rows_flow(
        own_a, core_a, crossed_a, pair_a, half_a, ring_a, cross_a, last_a, total_a, out_total
    )
    b = rows_flow(
        own_b, core_b, crossed_b, pair_b, half_b, ring_b, cross_b, last_b, total_b, hid_total
    )

    def both_next():
        next(a)
        next(b)

    for copy in operands[:2]:
        copy.wait()
    grad_in(0)
    grad_in(1)
    next(ins)
    for copy in operands[2:]:
        copy.wait()
    produce(0)
    produce(1)
    both_next()
    produce(2)
    both_next()
    for at in range(2, 8):
        grad_in(at)
    produce(3)
    next(ins)
    next(ins)
    for at in range(4):
        grad_out(at)
    both_next()
    next(ins)
    for at in range(4, 8):
        grad_out(at)
    next(outs)
    produce(4)
    produce(5)
    next(ins)
    both_next()
    produce(6)
    next(outs)
    next(ins)
    both_next()
    next(outs)
    produce(7)

    half = vector.shape[1]
    ones = jnp.ones((16, att.shape[0]), BF16)
    columns = jnp.concatenate([dot(ones, d_proj[...])[:1], dot(ones, d_up[...])[:1]], axis=1)
    vector[...] = jnp.zeros_like(vector)
    sums = [
        jnp.sum(gain_sum[...], axis=0, keepdims=True),
        jnp.sum(shift_sum[...], axis=0, keepdims=True),
        dot(ones[:, :rows], g_own[...])[:1],
    ]
    for at, row in enumerate(sums):
        vector[2 * at : 2 * at + 1, :] = row[:, :half]
        vector[2 * at + 1 : 2 * at + 2, :] = row[:, half:]
    vector[6:7, : columns.shape[1]] = columns
    vectors = vector_flow()
    next(vectors)
    run(ins, outs, a, b, vectors)

    for kept in keeps:
        kept.wait()
    post.close()


def second(att, act, d_proj, d_up, w_in, w_fc2, w_dense, stat, cotangent, x_all, g_all, hidden, fsdp):
    rows, width = cotangent.shape
    ctx = x_all.shape[0]
    side = width // fsdp
    in_columns = w_in.shape[1]
    fc2_rows, dense_rows = w_fc2.shape[0] // fsdp, w_dense.shape[0] // fsdp
    out_rows = fc2_rows + dense_rows
    any_ = pl.BlockSpec(memory_space=pl.ANY)

    def low(*shape):
        return pltpu.VMEM(shape, BF16)

    def wide(*shape):
        return pltpu.VMEM(shape, F32)

    def ctx_slots():
        return [
            low(rows, width), low(2, rows // 2, width), low(2, rows, width), low(2, rows, width),
            low(rows, width),
        ]

    def fsdp_slots(depth, columns, cut):
        return [
            low(fsdp, depth, columns), low(2, cut, columns), low(2, depth - cut, columns),
            low(2, 2, depth, columns), low(depth, columns), low(depth, columns),
        ]

    vector = (16, width // 2)
    many = 2 * 16 + 2 * 9 + 3 * 16 + 9 + 16
    ahead = 4
    operands = (att, act, d_proj, d_up, w_in, w_fc2, w_dense, stat, cotangent)
    return pl.pallas_call(
        second_kernel,
        out_shape=(
            jax.ShapeDtypeStruct((rows, width), F32),
            jax.ShapeDtypeStruct((rows, width), F32),
            jax.ShapeDtypeStruct((ctx, side, in_columns), BF16),
            jax.ShapeDtypeStruct((ctx, fc2_rows, width), BF16),
            jax.ShapeDtypeStruct((ctx, dense_rows, width), BF16),
            jax.ShapeDtypeStruct((ctx,) + vector, F32),
        ),
        in_specs=[any_] * 12,
        out_specs=(any_,) * 6,
        scratch_shapes=[pltpu.VMEM(operand.shape, operand.dtype) for operand in operands]
        + [low(ctx // 2, rows, width)] * 4
        + [low(2, rows, width)] * 2
        + ctx_slots()
        + ctx_slots()
        + fsdp_slots(side, in_columns, side // 2)
        + fsdp_slots(out_rows, width, 48)
        + [low(dense_rows, width)]
        + [
            low(ahead, ctx * rows, side), low(2, 2, rows, width), wide(rows, width),
            wide(rows, width), wide(8, width), wide(8, width),
            wide(*vector), wide(fsdp, *vector), wide(*vector),
            pltpu.SemaphoreType.DMA((many,)),
            pltpu.SemaphoreType.DMA((many,)),
            pltpu.SemaphoreType.DMA((8,)),
            pltpu.SemaphoreType.DMA((2 + ahead,)),
            pltpu.SemaphoreType.DMA((len(operands),)),
            pltpu.SemaphoreType.DMA,
            pltpu.SemaphoreType.DMA,
        ],
        compiler_params=pltpu.CompilerParams(
            collective_id=1, has_side_effects=True, vmem_limit_bytes=63 * MIB
        ),
        name="second",
    )(*operands, x_all, g_all.reshape(ctx * rows, width), hidden)


def widen_kernel(
    in_all, fc2_all, dense_all, branches_in, d_hidden_in, x_in, g_in, small_in,
    qkv, fc1, dense, fc2, result_to, input_grad_to,
    in_low, fc2_low, dense_low, qkv_wide, fc1_wide, fc2_wide, dense_wide,
    vec, branches, d_hidden, x_own, g_own, small, result, input_grad, loads, stores, reads,
):
    count = in_all.shape[0] // 2
    slots = in_low.shape[0]
    own = qkv.shape[1] // 3 // count
    units = fc1.shape[1] // count
    fc2_step, dense_step = fc2.shape[0] // count, dense.shape[0] // count // 2
    cut = 3 * own // 2

    def load(at):
        slot = at % slots
        copies = [
            pltpu.make_async_copy(source.at[pl.ds(2 * at, 2)], target.at[slot], loads.at[slot, number])
            for number, (source, target) in enumerate(
                [(in_all, in_low), (fc2_all, fc2_low), (dense_all, dense_low)]
            )
        ]
        for copy in copies:
            copy.start()
        return copies

    ahead = [load(at) for at in range(slots - 1)]
    stored = []
    own_rows = [
        pltpu.make_async_copy(source, target, reads.at[at])
        for at, (source, target) in enumerate(
            [
                (branches_in, branches), (d_hidden_in, d_hidden), (x_in, x_own), (g_in, g_own),
                (small_in, small),
            ]
        )
    ]
    for copy in own_rows:
        copy.start()

    side = small.shape[2]

    def finish():
        take = slice(None)
        token = x_own[take, :].astype(F32)
        result[take, :] = (token + branches[take, :] + vec[2:3, :] + vec[3:4, :]).astype(BF16)
        centred = token - jnp.mean(token, axis=1, keepdims=True)
        inverse = lax.rsqrt(jnp.mean(centred * centred, axis=1, keepdims=True) + NORM_EPS)
        normed = centred * inverse
        scaled = d_hidden[take, :] * vec[0:1, :]
        input_grad[take, :] = g_own[take, :].astype(F32) + inverse * (
            scaled
            - jnp.mean(scaled, axis=1, keepdims=True)
            - normed * jnp.mean(scaled * normed, axis=1, keepdims=True)
        )

    for at in range(count):
        slot = at % slots
        for copy in ahead[at]:
            copy.wait()
        if at + slots - 1 < count:
            ahead.append(load(at + slots - 1))
        if at >= slots:
            for copy in stored[at - slots]:
                copy.wait()
        half = own // 2
        for core in range(2):
            for part in range(3):
                first = part * own + core * half
                qkv_wide[slot, :, first : first + half] = in_low[
                    slot, core, :, part * half : (part + 1) * half
                ].astype(F32)
            fc2_wide[slot, core * (fc2_step // 2) : (core + 1) * (fc2_step // 2), :] = fc2_low[
                slot, core
            ].astype(F32)
            dense_wide[slot, core] = dense_low[slot, core].astype(F32)
        for part in range(count // 2):
            first = cut + part * 128
            left = in_low[slot, 0, :, first : first + 128].astype(F32)
            right = in_low[slot, 1, :, first : first + 128].astype(F32)
            fc1_wide[slot, :, 2 * part * 128 : (2 * part + 1) * 128] = fold(left, right, True)
            fc1_wide[slot, :, (2 * part + 1) * 128 : (2 * part + 2) * 128] = fold(left, right, False)
        targets = [
            (
                qkv_wide.at[slot, :, pl.ds(part * own, own)],
                qkv.at[:, pl.ds((part * count + at) * own, own)],
            )
            for part in range(3)
        ] + [
            (
                fc1_wide.at[slot, :, pl.ds(part * 128, 128)],
                fc1.at[:, pl.ds(part * units + at * 128, 128)],
            )
            for part in range(count)
        ] + [
            (fc2_wide.at[slot], fc2.at[pl.ds(at * fc2_step, fc2_step)]),
        ] + [
            (
                dense_wide.at[slot, core],
                dense.at[pl.ds((core * count + at) * dense_step, dense_step)],
            )
            for core in range(2)
        ]
        copies = [
            pltpu.make_async_copy(source, target, stores.at[slot, number])
            for number, (source, target) in enumerate(targets)
        ]
        for copy in copies:
            copy.start()
        stored.append(copies)
        if at == 2:
            for copy in own_rows:
                copy.wait()
            for shard in range(small.shape[0]):
                vec[0:4, shard * side : (shard + 1) * side] = small[shard, 0:4, :]
            finish()
    writes = [
        pltpu.make_async_copy(result, result_to, reads.at[0]),
        pltpu.make_async_copy(input_grad, input_grad_to, reads.at[1]),
    ]
    for copy in writes:
        copy.start()
    for copies in stored[-slots:]:
        for copy in copies:
            copy.wait()
    for copy in writes:
        copy.wait()


def widen(in_all, fc2_all, dense_all, branches, d_hidden, tokens, cotangent, small, ff):
    any_ = pl.BlockSpec(memory_space=pl.ANY)
    rows, width = tokens.shape
    fsdp = small.shape[0]
    slots = 3
    side = width // fsdp
    shapes = [(side, 3 * width), (side, ff), (side, width), (ff // fsdp, width)]
    return pl.pallas_call(
        widen_kernel,
        out_shape=tuple(jax.ShapeDtypeStruct(shape, F32) for shape in shapes)
        + (jax.ShapeDtypeStruct((rows, width), BF16), jax.ShapeDtypeStruct((rows, width), F32)),
        in_specs=[any_] * 8,
        out_specs=(any_,) * 6,
        scratch_shapes=[
            pltpu.VMEM((slots, 2) + in_all.shape[1:], BF16),
            pltpu.VMEM((slots, 2) + fc2_all.shape[1:], BF16),
            pltpu.VMEM((slots, 2) + dense_all.shape[1:], BF16),
            pltpu.VMEM((slots, side, 3 * width // fsdp), F32),
            pltpu.VMEM((slots, side, ff // fsdp), F32),
            pltpu.VMEM((slots, ff // fsdp // fsdp, width), F32),
            pltpu.VMEM((slots, 2) + dense_all.shape[1:], F32),
            pltpu.VMEM((8, width), F32),
            pltpu.VMEM((rows, width), F32),
            pltpu.VMEM((rows, width), F32),
            pltpu.VMEM((rows, width), BF16),
            pltpu.VMEM((rows, width), BF16),
            pltpu.VMEM(small.shape, F32),
            pltpu.VMEM((rows, width), BF16),
            pltpu.VMEM((rows, width), F32),
            pltpu.SemaphoreType.DMA((slots, 3)),
            pltpu.SemaphoreType.DMA((slots, 14)),
            pltpu.SemaphoreType.DMA((5,)),
        ],
        compiler_params=pltpu.CompilerParams(vmem_limit_bytes=62 * MIB),
        name="widen",
    )(in_all, fc2_all, dense_all, branches, d_hidden, tokens, cotangent, small)


def on_device(
    tokens, cotangent, block_order, positions, ln_gain, ln_bias, w_qkv, b_qkv, w_dense, b_dense,
    w_fc1, b_fc1, w_fc2, b_fc2,
):
    ctx, fsdp = lax.axis_size("ctx"), lax.axis_size("fsdp")
    f = lax.axis_index("fsdp")
    rows, width = tokens.shape[1:]
    seq = rows * ctx
    ff = w_fc1.shape[1]
    own_width, own_ff = width // ctx, ff // ctx
    own_rows = width // fsdp
    cut = 3 * own_width
    tokens = tokens.reshape(rows, width)
    cotangent = cotangent.reshape(rows, width)

    vectors = (ln_gain, ln_bias, b_dense, b_fc2, b_qkv, b_fc1)
    small, used = jnp.zeros((32 * own_rows,), BF16), 0
    for vector in vectors:
        left = small.shape[0] - used - vector.shape[0]
        small = small + jnp.pad(vector, (used, left))
        used += vector.shape[0]
    small = small.reshape(32, own_rows)
    spread = turn_spread(own_width)
    (
        x_all, g_all, hidden, stat, queries, keys, values, d_att, act, d_up, w_in, fc2, dense, turns,
        small,
    ) = first(
        tokens, cotangent, turn_rows(positions.reshape(rows), own_width), w_qkv, w_fc1, w_dense, w_fc2,
        small, spread, ctx, fsdp,
    )
    att, d_proj = attention(
        block_order, seq // block_order.shape[0], queries, keys, values, d_att,
        turns.reshape(seq, own_width), spread,
    )
    branches, d_hidden, in_all, fc2_all, dense_all, vector = second(
        att, act, d_proj, d_up, w_in.reshape(width, -1), fc2.reshape(own_ff, width),
        dense.reshape(own_width, width), stat, cotangent, x_all, g_all, hidden, fsdp,
    )
    grad_qkv, grad_fc1, grad_dense, grad_fc2, result, input_grad = widen(
        in_all, fc2_all, dense_all, branches, d_hidden, tokens, cotangent, small, ff
    )

    vector = vector.reshape(ctx, -1)
    sums = jnp.sum(vector[:, : 3 * width], axis=0).reshape(3, width)
    sums = lax.dynamic_slice_in_dim(sums, f * own_rows, own_rows, 1)
    columns = vector[:, 3 * width : 3 * width + cut].reshape(ctx, 3, own_width)
    columns = columns.transpose(1, 0, 2).reshape(3 * width)
    units = vector[:, 3 * width + cut : 3 * width + cut + own_ff].reshape(ctx, fsdp, -1)
    units = lax.dynamic_slice_in_dim(units, f, 1, 1).reshape(ff // fsdp)
    return (
        result.reshape(1, rows, width),
        input_grad.reshape(1, rows, width),
        sums[0],
        sums[1],
        grad_qkv,
        lax.dynamic_slice_in_dim(columns, f * (3 * own_rows), 3 * own_rows, 0),
        grad_dense,
        sums[2],
        grad_fc1,
        units,
        grad_fc2,
        sums[2],
    )


def solution(mesh):
    split = P("fsdp", "ctx", None)
    matrix = P("fsdp", None)
    vector = P("fsdp")
    return jax.shard_map(
        on_device,
        mesh=mesh,
        in_specs=(split, split, P(), P("fsdp", "ctx"), vector, vector)
        + (matrix, vector) * 4,
        out_specs=(split, split, vector, vector) + (matrix, vector) * 4,
        check_vma=False,
    )
```

```python
import functools

import jax
import jax.numpy as jnp
import numpy as np
from jax import lax
from jax.experimental import pallas as pl
from jax.experimental.pallas import tpu as pltpu
from jax.sharding import PartitionSpec as P

HEAD_DIM = 64
ROTARY = 32
NORM_EPS = 1e-05
ROPE_BASE = 10000.0
GELU_COEF = 0.7978845608028654
F32 = jnp.float32
BF16 = jnp.bfloat16
STRIP = 256
NT = (((1,), (1,)), ((), ()))
TN = (((0,), (0,)), ((), ()))
MESH = pl.DeviceIdType.MESH
MIB = 1024 * 1024


def nt_dot(left, right):
    return lax.dot_general(left, right, NT, preferred_element_type=F32)


def tn_dot(left, right):
    return lax.dot_general(left, right, TN, preferred_element_type=F32)


def dot(left, right):
    return jnp.dot(left, right, preferred_element_type=F32)


def turn_rows(positions, width):
    half = ROTARY // 2
    frequency = ROPE_BASE ** (-(jnp.arange(half, dtype=F32) * (2.0 / ROTARY)))
    turned = positions.astype(F32)[:, None] * frequency
    both = jnp.concatenate([jnp.cos(turned), jnp.sin(turned)], axis=1)
    coarse = both.astype(BF16)
    fine = (both - coarse.astype(F32)).astype(BF16)
    rows = positions.shape[0]
    used = 4 * half + 1
    return jnp.concatenate(
        [coarse, fine, jnp.ones((rows, 1), BF16), jnp.zeros((rows, width - used), BF16)], axis=1
    )


def turn_spread(width):
    half = ROTARY // 2
    table = np.zeros((width, 3 * width), np.float32)
    for column in range(width):
        at = column % HEAD_DIM
        if at >= ROTARY:
            table[4 * half, column] = 1.0
            continue
        for part in (0, 2 * half):
            table[part + at % half, column] = 1.0
            if at < half:
                table[part + half + at, width + column] = -1.0
            else:
                table[part + half + at - half, 2 * width + column] = 1.0
    return jnp.asarray(table, BF16)


def turn(values, tables, back):
    width = values.shape[1]
    half = ROTARY // 2
    same, after, before = (tables[:, at * width : (at + 1) * width] for at in range(3))
    moved = pltpu.roll(values, width - half, 1) * after + pltpu.roll(values, half, 1) * before
    return values * same - moved if back else values * same + moved


AWAY = [(dx, flip) for dx in range(4) for flip in (False, True) if dx or flip]


def fold(left, right, first):
    lane = lax.broadcasted_iota(jnp.int32, left.shape, 1)
    half = left.shape[1] // 2
    return jnp.where(
        lane < half,
        jnp.where(first, left, pltpu.roll(left, half, 1)),
        jnp.where(first, pltpu.roll(right, half, 1), right),
    )


class Place:
    def __init__(self):
        self.c, self.f = lax.axis_index("ctx"), lax.axis_index("fsdp")
        self.y, self.z, self.core = self.c // 4, (self.c // 2) % 2, self.c % 2
        self.x, self.half = self.f // 2, self.f % 2

    def block(self, dy, flip, other=False):
        core = 1 - self.core if other else self.core
        return ((self.y + dy) % 4) * 4 + (1 - self.z if flip else self.z) * 2 + core

    def shard(self, dx, flip):
        return ((self.x + dx) % 4) * 2 + (1 - self.half if flip else self.half)

    def to_ctx(self, dy, flip, other=False):
        return (self.block(dy, flip, other), self.f)

    def to_fsdp(self, dx, flip):
        return (self.c, self.shard(dx, flip))

    def to_swap(self):
        return (2 * self.f + self.c % 2, self.c // 2)


class Post:
    def __init__(self, place, send, recv):
        self.place, self.send, self.recv, self.started = place, send, recv, []
        self.left = set()

    def copy(self, source, target, device):
        at = len(self.started)
        copy = pltpu.make_async_remote_copy(
            src_ref=source, dst_ref=target, send_sem=self.send.at[at], recv_sem=self.recv.at[at],
            device_id=device, device_id_type=MESH,
        )
        self.started.append(copy)
        copy.start()
        return copy

    def greet(self):
        place = self.place
        barrier = pltpu.get_barrier_semaphore()
        partners = [
            place.to_ctx(1, False), place.to_ctx(-1, False), place.to_ctx(0, True),
            place.to_ctx(0, False, True),
        ] + [place.to_fsdp(*to) for to in AWAY]
        for partner in partners:
            pl.semaphore_signal(barrier, inc=1, device_id=partner, device_id_type=MESH)
        swap = place.to_swap()
        same = jnp.logical_and(swap[0] == place.c, swap[1] == place.f)

        @pl.when(jnp.logical_not(same))
        def _():
            pl.semaphore_signal(barrier, inc=1, device_id=swap, device_id_type=MESH)

        pl.semaphore_wait(barrier, len(partners) + jnp.where(same, 0, 1))

    def has_left(self, copy):
        copy.wait_send()
        self.left.add(id(copy))

    def close(self):
        for copy in self.started:
            if id(copy) not in self.left:
                copy.wait_send()


def gather_ctx(post, own, buf, cut, early=False):
    place = post.place
    here = post.place.block(0, False)
    crossed = []

    def send(at, *to):
        return post.copy(buf.at[at], buf.at[at], place.to_ctx(*to))

    def cross(at):
        crossed.append(post.copy(buf.at[at], buf.at[at], place.to_ctx(0, False, True)))

    def first(*to):
        return post.copy(own, buf.at[here], place.to_ctx(*to))

    to_next, to_last, to_pair = first(1, False), first(-1, False), first(0, True)
    crossed.append(first(0, False, True))
    yield
    last, after = place.block(-1, False), place.block(1, False)
    rest = buf.shape[1] - cut
    lower, upper = pl.ds(0, cut), pl.ds(cut, rest)
    to_next.wait_recv()
    halves = [post.copy(buf.at[last, lower], buf.at[last, lower], place.to_ctx(1, False))]
    to_last.wait_recv()
    if rest:
        piece = buf.at[after, upper]
        halves.append(post.copy(piece, piece, place.to_ctx(-1, False)))
    cross(last)
    cross(after)
    yield
    to_pair.wait_recv()
    pair = place.block(0, True)
    pair_next, pair_last = send(pair, 1, False), send(pair, -1, False)
    cross(pair)
    yield
    for copy in halves:
        copy.wait_recv()
    far = place.block(2, False)
    pair_far = send(far, 0, True)
    cross(far)
    waited = 0
    if early:
        waited = 4
        for copy in crossed[:4]:
            copy.wait_recv()
    yield
    pair_next.wait_recv()
    cross(place.block(-1, True))
    pair_last.wait_recv()
    cross(place.block(1, True))
    yield
    pair_far.wait_recv()
    cross(place.block(2, True))
    if early:
        waited = 7
        for copy in crossed[4:7]:
            copy.wait_recv()
    yield
    for copy in crossed[waited:]:
        copy.wait_recv()


def gather_fsdp(post, own, buf, cut):
    place = post.place
    here = place.shard(0, False)
    rest = buf.shape[1] - cut

    def whole(at, dx):
        return post.copy(buf.at[at], buf.at[at], place.to_fsdp(dx, False))

    def lower(at):
        piece = buf.at[at, pl.ds(0, cut)]
        return post.copy(piece, piece, place.to_fsdp(1, False))

    def upper(at):
        piece = buf.at[at, pl.ds(cut, rest)]
        return post.copy(piece, piece, place.to_fsdp(-1, False))

    to_pair = post.copy(own, buf.at[here], place.to_fsdp(0, True))
    to_next = post.copy(own, buf.at[here], place.to_fsdp(1, False))
    to_last = post.copy(own, buf.at[here], place.to_fsdp(-1, False))
    yield
    to_next.wait_recv()
    halves = [lower(place.shard(-1, False))]
    to_last.wait_recv()
    if rest:
        halves.append(upper(place.shard(1, False)))
    yield
    to_pair.wait_recv()
    pair = place.shard(0, True)
    pair_next, pair_last = whole(pair, 1), whole(pair, -1)
    yield
    pair_next.wait_recv()
    halves.append(lower(place.shard(-1, True)))
    pair_last.wait_recv()
    if rest:
        halves.append(upper(place.shard(1, True)))
    yield
    for copy in halves:
        copy.wait_recv()


def gather_direct(post, own, buf):
    place = post.place
    here = place.shard(0, False)
    copies = [post.copy(own, buf.at[here], place.to_fsdp(*to)) for to in AWAY]
    yield
    for copy in copies:
        copy.wait_recv()


class Swap:
    def __init__(self, place, source, target, send, recv, local):
        device = place.to_swap()
        self.same = jnp.logical_and(device[0] == place.c, device[1] == place.f)
        self.away = pltpu.make_async_remote_copy(
            src_ref=source, dst_ref=target, send_sem=send, recv_sem=recv, device_id=device,
            device_id_type=MESH,
        )
        self.stay = pltpu.make_async_copy(source, target, local)
        pl.when(jnp.logical_not(self.same))(lambda: self.away.start())
        pl.when(self.same)(lambda: self.stay.start())

    def wait(self):
        pl.when(jnp.logical_not(self.same))(lambda: self.away.wait())
        pl.when(self.same)(lambda: self.stay.wait())


def first_kernel(
    x_in, g_in, turn_in, w_qkv, w_fc1, w_dense, w_fc2, small_in, spread,
    x_to, g_to, hidden_to, stat_to, q_to, k_to, v_to, d_att_to, act_to, d_up_to, w_in_to, fc2_to,
    dense_to,
    turns_to, small_to,
    x_all, g_all, hidden, stat, q_out, k_out, v_out, d_att, act, d_up, w_in, fc2, dense,
    turns, small_out,
    wide_rows, in_rows, fc2_rows, dense_rows, piece, small_all, tables, proj, slope, vec, bias,
    send, recv, local, reads, swap_send, swap_recv,
):
    place = Place()
    post = Post(place, send, recv)
    rows, width = x_in.shape
    own_width = q_out.shape[1]
    own_ff = act.shape[1]
    cut = 3 * own_width
    here, shard = place.block(0, False), place.shard(0, False)

    def columns(first, count):
        return pl.ds(pl.multiple_of(first, 128), count)

    fsdp, fc2_step = fc2.shape[:2]
    dense_step = dense.shape[1]
    units = w_fc1.shape[1] // fsdp
    first_dense = (place.c % 2) * own_width + (place.c // 2) * dense_step
    first_fc2 = place.c * fc2_step
    sources = [
        (w_dense.at[pl.ds(pl.multiple_of(first_dense, 16), dense_step)], dense_rows),
        (w_fc2.at[pl.ds(pl.multiple_of(first_fc2, 16), fc2_step)], fc2_rows),
    ]
    for part in range(3):
        take = columns(part * width + place.c * own_width, own_width)
        sources.append((w_qkv.at[:, take], in_rows.at[:, pl.ds(part * own_width, own_width)]))
    for part in range(fsdp):
        take = columns(part * units + place.c // 2 * 128, 128)
        sources.append((w_fc1.at[:, take], wide_rows.at[:, pl.ds(part * 128, 128)]))
    ready = [
        pltpu.make_async_copy(source, target, reads.at[at])
        for at, (source, target) in enumerate(sources)
    ]
    for copy in ready:
        copy.start()
    post.greet()
    for copy in ready:
        copy.wait()
    swap = Swap(place, dense_rows, piece, swap_send, swap_recv, local.at[0])
    for part in range(fsdp // 2):
        left, right = (
            wide_rows[:, at * 128 : (at + 1) * 128].astype(F32) for at in (2 * part, 2 * part + 1)
        )
        in_rows[:, cut + part * 128 : cut + (part + 1) * 128] = fold(
            left, right, place.core == 0
        ).astype(BF16)
    keeps = []

    def keep(source, target):
        copy = pltpu.make_async_copy(source, target, local.at[1 + len(keeps)])
        keeps.append(copy)
        copy.start()
        return copy

    own = [
        keep(x_in, x_all.at[here]), keep(in_rows, w_in.at[shard]), keep(turn_in, turns.at[here]),
        keep(small_in, small_all.at[shard]), keep(g_in, g_all.at[here]),
        keep(fc2_rows, fc2.at[shard]),
    ]
    x_flow = gather_ctx(post, x_in, x_all, rows // 2, early=True)
    in_flow = gather_fsdp(post, in_rows, w_in, in_rows.shape[0] // 2)
    small_flow = gather_direct(post, small_in, small_all)
    turn_flow = gather_ctx(post, turn_in, turns, rows // 2)
    def advance(*flows):
        for flow in flows:
            next(flow, None)

    advance(x_flow, in_flow, small_flow, turn_flow)
    advance(x_flow, in_flow)
    swap.wait()
    keep(piece, dense.at[shard])
    dense_flow = gather_fsdp(post, piece, dense, dense_step)
    advance(dense_flow, x_flow, in_flow, turn_flow)
    g_flow = gather_ctx(post, g_in, g_all, rows // 2, early=True)
    fc2_flow = gather_fsdp(post, fc2_rows, fc2, fc2_step // 2)
    advance(g_flow, fc2_flow)
    for _ in small_flow:
        pass
    for copy in own[:4]:
        copy.wait()

    side = small_all.shape[2]
    small_out[...] = small_all[...].astype(F32)
    for at in range(small_all.shape[0]):
        vec[0:2, at * side : (at + 1) * side] = small_out[at, 0:2, :]
    for part in range(3):
        first = part * width + place.c * own_width
        count = 3 * side
        row = small_out[first // count, pl.ds(4 + (first % count) // side, 1), :]
        bias[0:1, part * own_width : (part + 1) * own_width] = jnp.where(
            first % side == 0, row[:, :own_width], row[:, own_width:]
        )
    quarter = place.c % 4
    pieces = []
    for part in range(fsdp):
        row = small_out[part, pl.ds(7 + place.c // 4, 1), :]
        row = jnp.where(quarter >= 2, row[:, 128:], row[:, :128])
        pieces.append(jnp.broadcast_to(row, (8, 128)))
    for part in range(fsdp // 2):
        row = fold(pieces[2 * part], pieces[2 * part + 1], quarter % 2 == 0)
        bias[0:1, cut + part * 128 : cut + (part + 1) * 128] = row[0:1, :]

    def normalise(block):
        lane = lax.broadcasted_iota(jnp.int32, (rows, stat.shape[1]), 1)
        target = pl.ds(pl.multiple_of(block * rows, rows), rows)
        value = x_all[block].astype(F32)
        mean = jnp.mean(value, axis=1, keepdims=True)
        centred = value - mean
        inverse = lax.rsqrt(jnp.mean(centred * centred, axis=1, keepdims=True) + NORM_EPS)
        hidden[target, :] = (centred * inverse * vec[0:1, :] + vec[1:2, :]).astype(BF16)
        stat[target, :] = jnp.where(lane < HEAD_DIM, mean, inverse)

    def normalise_each(targets):
        order = [place.block(*to) for to in targets]

        def body(at, carry):
            block = order[0]
            for number, other in enumerate(order[1:]):
                block = jnp.where(at == number + 1, other, block)
            normalise(block)
            return carry

        lax.fori_loop(0, len(order), body, 0)

    chunk_rows = proj.shape[0]
    group = chunk_rows // rows

    def project(chunk):
        take = pl.ds(pl.multiple_of(chunk * chunk_rows, chunk_rows), chunk_rows)
        keep(hidden.at[take], hidden_to.at[take])
        weight = w_in[...].reshape(width, proj.shape[1])
        proj[...] = dot(hidden[take, :], weight)
        settle(chunk)

    def settle(chunk):
        turned = turns[pl.ds(chunk * group, group)].reshape(chunk_rows, own_width)
        tables[...] = dot(turned, spread[...])
        target = pl.ds(pl.multiple_of(chunk * chunk_rows, chunk_rows), chunk_rows)
        value = proj[...] + bias[0:1, :]
        table = tables[...]
        q_out[target, :] = turn(value[:, :own_width], table, False).astype(BF16)
        k_out[target, :] = turn(value[:, own_width : 2 * own_width], table, False).astype(BF16)
        v_out[target, :] = value[:, 2 * own_width : cut].astype(BF16)
        up = value[:, cut:]
        square = up * up
        curve = jnp.tanh(GELU_COEF * up * (1.0 + 0.044715 * square))
        act[target, :] = (0.5 * up * (1.0 + curve)).astype(BF16)
        slope[target, :] = 0.5 * (1.0 + curve) + 0.5 * up * (1.0 - curve * curve) * (
            GELU_COEF * (1.0 + 3.0 * 0.044715 * square)
        )

    chunks = hidden.shape[0] // chunk_rows
    def keep_grads(*targets):
        for to in targets:
            chip = pl.ds(place.block(*to) // 2 * 2, 2)
            keep(g_all.at[chip], g_to.at[chip])

    normalise_each([(0, False), (1, False), (-1, False)])
    advance(x_flow, in_flow, turn_flow, g_flow, fc2_flow, dense_flow)
    normalise_each([(0, True), (0, False, True), (0, True, True)])
    for flow in (in_flow, turn_flow):
        for _ in flow:
            pass
    keep(w_in, w_in_to)
    keep(turns, turns_to)
    keep(small_out, small_to)
    advance(x_flow, g_flow, fc2_flow, dense_flow)
    project(place.y)
    advance(x_flow)
    normalise_each([(1, True), (1, False, True), (1, True, True), (2, False)])
    advance(g_flow)
    own[4].wait()
    keep_grads((0, False), (-1, False), (1, False), (0, True))
    project((place.y + 1) % 4)
    advance(fc2_flow, dense_flow, x_flow)
    keep(x_all, x_to)
    normalise_each([(-1, True), (-1, False, True), (-1, True, True), (2, True)])
    project((place.y + 3) % 4)
    advance(g_flow)
    normalise_each([(2, False, True), (2, True, True)])
    keep(stat, stat_to)
    project((place.y + 2) % 4)
    advance(g_flow)
    keep_grads((2, False), (-1, True), (1, True))
    for target, source in ((q_to, q_out), (k_to, k_out), (v_to, v_out), (act_to, act)):
        keep(source, target)
    advance(fc2_flow, dense_flow)
    own[5].wait()
    keeps[6].wait()
    keep(fc2, fc2_to)
    keep(dense, dense_to)
    advance(g_flow)
    keep_grads((2, True))

    for chunk in range(chunks):
        grads = g_all[pl.ds(chunk * group, group)].reshape(chunk_rows, width)
        target = pl.ds(chunk * chunk_rows, chunk_rows)
        d_att[target, :] = nt_dot(grads, dense[...].reshape(own_width, width)).astype(BF16)
        d_act = nt_dot(grads, fc2[...].reshape(own_ff, width))
        d_up[target, :] = (d_act * slope[target, :]).astype(BF16)
        keep(d_att.at[target], d_att_to.at[target])
        keep(d_up.at[target], d_up_to.at[target])
    for copy in keeps[7:]:
        copy.wait()
    post.close()


def first(tokens, cotangent, turns, w_qkv, w_fc1, w_dense, w_fc2, small, spread, ctx, fsdp):
    rows, width = tokens.shape
    seq = ctx * rows
    own_width, own_ff = turns.shape[1], w_fc1.shape[1] // ctx
    columns = 3 * own_width + own_ff
    side = width // fsdp
    many = 3 * 16 + 3 * 9 + fsdp - 1
    any_, vmem = pl.BlockSpec(memory_space=pl.ANY), pl.BlockSpec(memory_space=pltpu.VMEM)

    def low(*shape):
        return jax.ShapeDtypeStruct(shape, BF16)

    def wide(*shape):
        return jax.ShapeDtypeStruct(shape, F32)

    outs = [
        low(ctx, rows, width), low(ctx, rows, width), low(seq, width), wide(seq, 128),
        low(seq, own_width), low(seq, own_width), low(seq, own_width), low(seq, own_width),
        low(seq, own_ff), low(seq, own_ff), low(fsdp, side, columns),
        low(fsdp, own_ff // fsdp, width), low(fsdp, own_width // fsdp, width),
        low(ctx, rows, own_width), wide(*((fsdp,) + small.shape)),
    ]
    chunk_rows = 4 * rows
    return pl.pallas_call(
        first_kernel,
        out_shape=tuple(outs),
        in_specs=[any_] * 8 + [vmem],
        out_specs=(any_,) * len(outs),
        scratch_shapes=[pltpu.VMEM(out.shape, out.dtype) for out in outs]
        + [
            pltpu.VMEM((side, fsdp * 128), BF16),
            pltpu.VMEM((side, columns), BF16),
            pltpu.VMEM((own_ff // fsdp, width), BF16),
            pltpu.VMEM((own_width // fsdp, width), BF16),
            pltpu.VMEM((own_width // fsdp, width), BF16),
            pltpu.VMEM((fsdp,) + small.shape, BF16),
            pltpu.VMEM((chunk_rows, 3 * own_width), F32),
            pltpu.VMEM((chunk_rows, columns), F32),
            pltpu.VMEM((seq, own_ff), F32),
            pltpu.VMEM((8, width), F32),
            pltpu.VMEM((8, columns), F32),
            pltpu.SemaphoreType.DMA((many,)),
            pltpu.SemaphoreType.DMA((many,)),
            pltpu.SemaphoreType.DMA((40,)),
            pltpu.SemaphoreType.DMA((5 + fsdp,)),
            pltpu.SemaphoreType.DMA,
            pltpu.SemaphoreType.DMA,
        ],
        compiler_params=pltpu.CompilerParams(
            collective_id=0, has_side_effects=True, vmem_limit_bytes=60 * MIB
        ),
        name="first",
    )(tokens, cotangent, turns, w_qkv, w_fc1, w_dense, w_fc2, small, spread)


def attention_kernel(
    block, order, q_hbm, k_hbm, v_hbm, g_hbm, turns_hbm, spread, o_to, d_to,
    q_in, k_in, v_in, g_in, turns, o_out, d_out, loads, qs, ks, vs, gs, os, dqs, dks, dvs, kt, vt, table,
):
    rows, width = q_in.shape
    blocks = rows // block
    reads = [
        pltpu.make_async_copy(source, target, loads.at[at])
        for at, (source, target) in enumerate(
            [(q_hbm, q_in), (k_hbm, k_in), (v_hbm, v_in), (g_hbm, g_in), (turns_hbm, turns)]
        )
    ]
    for copy in reads:
        copy.start()
    for copy in reads[:4]:
        copy.wait()

    def collect(at, carry):
        src = pl.ds(pl.multiple_of(at * block, block), block)
        dst = pl.ds(pl.multiple_of(order[at] * block, block), block)
        qs[dst, :] = q_in[src, :]
        ks[dst, :] = k_in[src, :]
        vs[dst, :] = v_in[src, :]
        gs[dst, :] = g_in[src, :]
        return carry

    lax.fori_loop(0, blocks, collect, 0, unroll=4)
    dks[...] = jnp.zeros_like(dks)
    dvs[...] = jnp.zeros_like(dvs)
    heads = width // HEAD_DIM
    scale = HEAD_DIM ** (-0.5)
    q_pos = lax.broadcasted_iota(jnp.int32, (STRIP, STRIP), 0)
    k_pos = lax.broadcasted_iota(jnp.int32, (STRIP, STRIP), 1)
    diagonal = q_pos <= k_pos
    reads[4].wait()
    table[...] = dot(turns[...], spread[...])
    kt[...] = ks[...].T
    vt[...] = vs[...].T
    sides = [slice(head * HEAD_DIM, (head + 1) * HEAD_DIM) for head in range(heads)]
    strips = rows // STRIP

    def begin(strip):
        here = slice(strip * STRIP, (strip + 1) * STRIP)
        count = (strip + 1) * STRIP
        query = [qs[here, cols] * jnp.asarray(scale, BF16) for cols in sides]
        part = [nt_dot(ks[:count, cols], query[h]) for h, cols in enumerate(sides)]
        return query, part

    ready = begin(0)
    for strip in range(strips):
        here = slice(strip * STRIP, (strip + 1) * STRIP)
        count = (strip + 1) * STRIP
        query, part = ready
        edge = [jnp.where(diagonal, p[count - STRIP :, :], -1e30) for p in part]
        part = [jnp.concatenate([p[: count - STRIP, :], e], axis=0) if strip else e for p, e in zip(part, edge)]
        part = [jnp.exp(p - jnp.max(p, axis=0, keepdims=True)) for p in part]
        inverse = [1.0 / jnp.sum(p, axis=0, keepdims=True) for p in part]
        low = [p.astype(BF16) for p in part]
        mixed = [dot(vt[cols, :count], low[h]) * inverse[h] for h, cols in enumerate(sides)]
        grad = [gs[here, cols].astype(F32).T * inverse[h] for h, cols in enumerate(sides)]
        centre = [jnp.sum(g * m, axis=0, keepdims=True) for g, m in zip(grad, mixed)]
        os[here, :] = jnp.concatenate(mixed, axis=0).T.astype(BF16)
        grad = [g.astype(BF16) for g in grad]
        if strip + 1 < strips:
            ready = begin(strip + 1)
        d_score = [(part[h] * (dot(vs[:count, cols], grad[h]) - centre[h])).astype(BF16) for h, cols in enumerate(sides)]
        dqs[here, :] = jnp.concatenate([dot(kt[cols, :count], d_score[h]) for h, cols in enumerate(sides)], axis=0).T * scale
        dks[:count, :] += jnp.concatenate([dot(d_score[h], query[h]) for h in range(heads)], axis=1)
        dvs[:count, :] += jnp.concatenate([nt_dot(low[h], grad[h]) for h in range(heads)], axis=1)

    def give(at, carry):
        src = pl.ds(pl.multiple_of(order[at] * block, block), block)
        dst = pl.ds(pl.multiple_of(at * block, block), block)
        tables = table[dst, :]
        o_out[dst, :] = os[src, :]
        d_out[dst, :width] = turn(dqs[src, :], tables, True).astype(BF16)
        d_out[dst, width : 2 * width] = turn(dks[src, :], tables, True).astype(BF16)
        d_out[dst, 2 * width :] = dvs[src, :].astype(BF16)
        return carry

    writes = []
    parts = 4
    for part in range(parts):
        lax.fori_loop(part * blocks // parts, (part + 1) * blocks // parts, give, 0, unroll=4)
        take = pl.ds(part * rows // parts, rows // parts)
        for number, (source, target) in enumerate(((o_out, o_to), (d_out, d_to))):
            copy = pltpu.make_async_copy(
                source.at[take], target.at[take], loads.at[5 + 2 * part + number]
            )
            copy.start()
            writes.append(copy)
    for copy in writes:
        copy.wait()


def attention(order, block, queries, keys, values, grads, turns, spread):
    rows, width = queries.shape
    vmem = pl.BlockSpec(memory_space=pltpu.VMEM)
    smem = pl.BlockSpec(memory_space=pltpu.SMEM)
    any_ = pl.BlockSpec(memory_space=pl.ANY)
    return pl.pallas_call(
        functools.partial(attention_kernel, block),
        out_shape=(
            jax.ShapeDtypeStruct((rows, width), BF16),
            jax.ShapeDtypeStruct((rows, 3 * width), BF16),
        ),
        in_specs=[smem] + [any_] * 5 + [vmem],
        out_specs=(any_, any_),
        scratch_shapes=[pltpu.VMEM((rows, width), BF16)] * 6
        + [pltpu.VMEM((rows, 3 * width), BF16), pltpu.SemaphoreType.DMA((13,))]
        + [pltpu.VMEM((rows, width), BF16)] * 5
        + [pltpu.VMEM((rows, width), F32)] * 3
        + [pltpu.VMEM((width, rows), BF16), pltpu.VMEM((width, rows), BF16)]
        + [pltpu.VMEM((rows, 3 * width), F32)],
        compiler_params=pltpu.CompilerParams(vmem_limit_bytes=60 * MIB),
        cost_estimate=pl.CostEstimate(
            flops=6 * rows * rows * width,
            bytes_accessed=rows * width * 22,
            transcendentals=rows * rows * width // HEAD_DIM // 2,
        ),
        name="attention",
    )(order, queries, keys, values, grads, turns, spread)


ORDER = [(2, True), (1, True), (-1, True), (2, False), (0, True), (1, False), (-1, False), (0, False)]
SHARDS = [(2, True), (2, False), (1, True), (-1, True), (1, False), (-1, False), (0, True), (0, False)]


def add_into(target, *parts):
    step = 64 if target.shape[0] % 64 == 0 else target.shape[0]
    plain = len(parts) == 2 and target.dtype == BF16

    def body(at, carry):
        take = pl.ds(pl.multiple_of(at * step, step), step)
        if plain:
            target[take, :] = parts[0][take, :] + parts[1][take, :]
            return carry
        total = parts[0][take, :].astype(F32)
        for part in parts[1:]:
            total = total + part[take, :].astype(F32)
        target[take, :] = total.astype(target.dtype)
        return carry

    lax.fori_loop(0, target.shape[0] // step, body, 0)


def reduce_ctx(post, own, core, crossed, pair_in, half_in, ring_in, cross_in, last_in, total):
    place = post.place
    cut = half_in.shape[1]
    up, down, pair = place.to_ctx(1, False), place.to_ctx(-1, False), place.to_ctx(0, True)

    def meet(at, *more):
        crossed[at].wait_recv()
        add_into(core.at[at], own.at[at], core.at[at], *more)

    meet(0)
    far = post.copy(core.at[0], pair_in, pair)
    yield
    meet(1)
    cross_next = post.copy(core.at[1], cross_in.at[0], up)
    meet(2)
    cross_last = post.copy(core.at[2], cross_in.at[1], down)
    yield
    far.wait_recv()
    meet(3, pair_in)
    low = post.copy(core.at[3, pl.ds(0, cut)], half_in.at[0], up)
    high = post.copy(core.at[3, pl.ds(cut, cut)], half_in.at[1], down)
    yield
    cross_next.wait_recv()
    cross_last.wait_recv()
    meet(4, cross_in.at[0], cross_in.at[1])
    last = post.copy(core.at[4], last_in, pair)
    yield
    meet(5)
    low.wait_recv()
    lower = core.at[5, pl.ds(0, cut)]
    add_into(lower, lower, half_in.at[0])
    ring_next = post.copy(core.at[5], ring_in.at[0], up)
    meet(6)
    high.wait_recv()
    upper = core.at[6, pl.ds(cut, cut)]
    add_into(upper, upper, half_in.at[1])
    ring_last = post.copy(core.at[6], ring_in.at[1], down)
    yield
    crossed[7].wait_recv()
    last.wait_recv()
    ring_next.wait_recv()
    ring_last.wait_recv()
    add_into(total, own.at[7], core.at[7], ring_in.at[0], ring_in.at[1], last_in)


def reduce_fsdp(post, part, low_in, high_in, ring_in, pair_in, total):
    place = post.place
    cut, rest = low_in.shape[1], high_in.shape[1]
    lower, upper = pl.ds(0, cut), pl.ds(cut, rest)
    up, down, pair = place.to_fsdp(1, False), place.to_fsdp(-1, False), place.to_fsdp(0, True)
    halves = [
        (
            post.copy(part.at[side, lower], low_in.at[side], up),
            post.copy(part.at[side, upper], high_in.at[side], down),
        )
        for side in range(2)
    ]
    yield
    rings = []
    for side in range(2):
        low, high = halves[side]
        after, before = part.at[2 + 2 * side], part.at[3 + 2 * side]
        low.wait_recv()
        add_into(after.at[lower], after.at[lower], low_in.at[side])
        to_next = post.copy(after, ring_in.at[side, 0], up)
        high.wait_recv()
        add_into(before.at[upper], before.at[upper], high_in.at[side])
        to_last = post.copy(before, ring_in.at[side, 1], down)
        rings.append((to_next, to_last))
        yield
    for copy in rings[0]:
        copy.wait_recv()
    add_into(part.at[6], part.at[6], ring_in.at[0, 0], ring_in.at[0, 1])
    across = post.copy(part.at[6], pair_in, pair)
    yield
    for copy in rings[1]:
        copy.wait_recv()
    across.wait_recv()
    add_into(total, part.at[7], ring_in.at[1, 0], ring_in.at[1, 1], pair_in)


def run(*flows):
    flows = list(flows)
    while flows:
        flows = [flow for flow in flows if next(flow, flows) is not flows]


def second_kernel(
    att_in, act_in, d_proj_in, d_up_in, w_in_in, w_fc2_in, w_dense_in, stat_in, g_own_in, x_all, g_all, hidden,
    out_total, hid_total, in_all, fc2_all, dense_all, vector_all,
    att, act, d_proj, d_up, w_in, w_fc2, w_dense, stat, g_own,
    own_a, own_b, core_a, core_b, slot_a, slot_b,
    pair_a, half_a, ring_a, cross_a, last_a, pair_b, half_b, ring_b, cross_b, last_b,
    in_part, in_low, in_high, in_ring, in_pair, in_sum,
    out_part, out_low, out_high, out_ring, out_pair, out_sum, out_piece,
    column, x_block, total_a, total_b, gain_sum, shift_sum,
    vector, vector_shards, vector_sum,
    send, recv, local, loads, reads, swap_send, swap_recv,
):
    place = Place()
    post = Post(place, send, recv)
    rows, width = g_own.shape
    cut = d_proj.shape[1]
    side = in_part.shape[1]
    here, shard = place.block(0, False), place.shard(0, False)
    keeps, numbers = [], iter(range(7))

    def keep(source, target):
        copy = pltpu.make_async_copy(source, target, local.at[next(numbers)])
        keeps.append(copy)
        copy.start()
        return copy

    operands = [
        pltpu.make_async_copy(source, target, reads.at[at])
        for at, (source, target) in enumerate(
            [
                (d_proj_in, d_proj), (d_up_in, d_up), (att_in, att), (act_in, act), (w_fc2_in, w_fc2),
                (w_dense_in, w_dense),
                (w_in_in, w_in), (stat_in, stat), (g_own_in, g_own),
            ]
        )
    ]

    def load_x(at):
        dy, flip = ORDER[at]
        block = place.block(dy, flip) // 2
        copy = pltpu.make_async_copy(
            x_all.at[pl.ds(2 * block, 2)], x_block.at[at % 2], loads.at[at % 2]
        )
        copy.start()
        return copy

    ahead = column.shape[0]

    def load_column(at):
        if at < len(SHARDS):
            first = pl.multiple_of(place.shard(*SHARDS[at]) * side, side)
            source = hidden.at[:, pl.ds(first, side)]
        else:
            source = g_all.at[:, pl.ds((at - len(SHARDS)) * side, side)]
        copy = pltpu.make_async_copy(source, column.at[at % ahead], loads.at[2 + at % ahead])
        copy.start()
        return copy

    for copy in operands[:2]:
        copy.start()
    pending_column = [load_column(at) for at in range(ahead - 1)]
    pending_x = [load_x(0)]
    for copy in operands[2:]:
        copy.start()
    post.greet()
    gain_sum[...] = jnp.zeros_like(gain_sum)
    shift_sum[...] = jnp.zeros_like(shift_sum)
    crossed_a, crossed_b, slots = {}, {}, {}
    partner = place.to_ctx(0, False, True)
    depth = slot_a.shape[0]

    def produce(at):
        dy, flip = ORDER[at]
        block = place.block(dy, flip) // 2
        pending_x.pop().wait()
        if at + 1 < len(ORDER):
            pending_x.append(load_x(at + 1))
        slot = at % depth
        if at >= depth:
            for copy in slots[at - depth]:
                post.has_left(copy)
        other_rows = pl.ds(pl.multiple_of(block * (2 * rows) + (1 - place.core) * rows, rows), rows)
        own_rows = pl.ds(pl.multiple_of(block * (2 * rows) + place.core * rows, rows), rows)

        def both(ref):
            return jnp.concatenate([ref[other_rows, :], ref[own_rows, :]], axis=0)

        left, right = both(att), both(act)
        span = width // 2
        for first in range(0, width, span):
            take = slice(first, first + span)
            value = dot(left, w_dense[:, take]) + dot(right, w_fc2[:, take])
            slot_a[slot, :, take] = value[:rows].astype(BF16)
            own_a[at, :, take] = value[rows:].astype(BF16)
        left, right, stats = both(d_proj), both(d_up), both(stat)
        mean, inverse = stats[:, 0:1], stats[:, HEAD_DIM : HEAD_DIM + 1]
        span = width // 4
        for first in range(0, width, span):
            take = slice(first, first + span)
            value = nt_dot(left, w_in[take, :cut]) + nt_dot(right, w_in[take, cut:])
            slot_b[slot, :, take] = value[:rows].astype(BF16)
            own_b[at, :, take] = value[rows:].astype(BF16)
            tokens = jnp.concatenate(
                [x_block[at % 2, 1 - place.core, :, take], x_block[at % 2, place.core, :, take]],
                axis=0,
            )
            normed = (tokens.astype(F32) - mean) * inverse
            parts = (2 * rows // 8, 8, span)
            gain_sum[:, take] += jnp.sum((value * normed).reshape(parts), axis=0)
            shift_sum[:, take] += jnp.sum(value.reshape(parts), axis=0)
        crossed_a[at] = post.copy(slot_a.at[slot], core_a.at[at], partner)
        crossed_b[at] = post.copy(slot_b.at[slot], core_b.at[at], partner)
        slots[at] = (crossed_a[at], crossed_b[at])

    def next_column(at):
        pending_column.pop(0).wait()
        if at + ahead - 1 < 2 * len(SHARDS):
            pending_column.append(load_column(at + ahead - 1))
        return column[at % ahead]

    def grad_in(at):
        rows_of = next_column(at)
        in_part[at, :, :cut] = tn_dot(rows_of, d_proj[...]).astype(BF16)
        in_part[at, :, cut:] = tn_dot(rows_of, d_up[...]).astype(BF16)

    def grad_out(at):
        columns = next_column(len(SHARDS) + at)
        take = slice(at * side, (at + 1) * side)
        dense = tn_dot(att[...], columns).astype(BF16)
        fc2 = tn_dot(act[...], columns).astype(BF16)
        dense_step, fc2_step = dense.shape[0] // len(SHARDS), fc2.shape[0] // len(SHARDS)
        for to in range(len(SHARDS)):
            out_part[to, :dense_step, take] = dense[to * dense_step : (to + 1) * dense_step]
            out_part[to, dense_step:, take] = fc2[to * fc2_step : (to + 1) * fc2_step]

    class ByShard:
        @property
        def at(self):
            return self

        def __getitem__(self, index):
            if isinstance(index, tuple):
                return out_part.at[(place.shard(*SHARDS[index[0]]),) + index[1:]]
            return out_part.at[place.shard(*SHARDS[index])]

    def in_flow():
        yield from reduce_fsdp(post, in_part, in_low, in_high, in_ring, in_pair, in_sum)
        keep(in_sum, in_all.at[here])
        yield from gather_ctx(post, in_sum, in_all, in_sum.shape[0] // 2)

    def out_flow():
        yield from reduce_fsdp(post, ByShard(), out_low, out_high, out_ring, out_pair, out_sum)
        first, count = dense_all.shape[1], fc2_all.shape[1]
        swap = Swap(
            place, out_sum.at[pl.ds(0, first)], out_piece, swap_send, swap_recv, local.at[7]
        )
        fc2_own = out_sum.at[pl.ds(first, count)]
        keep(fc2_own, fc2_all.at[here])
        flows = [gather_ctx(post, fc2_own, fc2_all, count // 2)]
        next(flows[0])
        yield
        next(flows[0])
        swap.wait()
        keep(out_piece, dense_all.at[here])
        flows.append(gather_ctx(post, out_piece, dense_all, first))
        while flows:
            flows = [flow for flow in flows if next(flow, flows) is not flows]
            yield

    def vector_flow():
        mine = keep(vector, vector_shards.at[shard])
        yield from gather_fsdp(post, vector, vector_shards, 8)
        mine.wait()
        keeps[:] = [kept for kept in keeps if kept is not mine]
        total = vector_shards[0]
        for at in range(1, vector_shards.shape[0]):
            total = total + vector_shards[at]
        vector_sum[...] = total
        keep(vector_sum, vector_all.at[here])
        yield from gather_ctx(post, vector_sum, vector_all, 8)

    def rows_flow(own, core, crossed, pair, half, ring, cross, last, total, target):
        yield from reduce_ctx(post, own, core, crossed, pair, half, ring, cross, last, total)
        keep(total, target)

    ins, outs = in_flow(), out_flow()
    a = rows_flow(
        own_a, core_a, crossed_a, pair_a, half_a, ring_a, cross_a, last_a, total_a, out_total
    )
    b = rows_flow(
        own_b, core_b, crossed_b, pair_b, half_b, ring_b, cross_b, last_b, total_b, hid_total
    )

    def both_next():
        next(a)
        next(b)

    for copy in operands[:2]:
        copy.wait()
    grad_in(0)
    grad_in(1)
    next(ins)
    for copy in operands[2:]:
        copy.wait()
    produce(0)
    produce(1)
    both_next()
    produce(2)
    both_next()
    for at in range(2, 8):
        grad_in(at)
    produce(3)
    next(ins)
    next(ins)
    for at in range(4):
        grad_out(at)
    both_next()
    next(ins)
    for at in range(4, 8):
        grad_out(at)
    next(outs)
    produce(4)
    produce(5)
    next(ins)
    both_next()
    produce(6)
    next(outs)
    next(ins)
    both_next()
    next(outs)
    produce(7)

    half = vector.shape[1]
    ones = jnp.ones((16, att.shape[0]), BF16)
    columns = jnp.concatenate([dot(ones, d_proj[...])[:1], dot(ones, d_up[...])[:1]], axis=1)
    vector[...] = jnp.zeros_like(vector)
    sums = [
        jnp.sum(gain_sum[...], axis=0, keepdims=True),
        jnp.sum(shift_sum[...], axis=0, keepdims=True),
        dot(ones[:, :rows], g_own[...])[:1],
    ]
    for at, row in enumerate(sums):
        vector[2 * at : 2 * at + 1, :] = row[:, :half]
        vector[2 * at + 1 : 2 * at + 2, :] = row[:, half:]
    vector[6:7, : columns.shape[1]] = columns
    vectors = vector_flow()
    next(vectors)
    run(ins, outs, a, b, vectors)

    for kept in keeps:
        kept.wait()
    post.close()


def second(att, act, d_proj, d_up, w_in, w_fc2, w_dense, stat, cotangent, x_all, g_all, hidden, fsdp):
    rows, width = cotangent.shape
    ctx = x_all.shape[0]
    side = width // fsdp
    in_columns = w_in.shape[1]
    fc2_rows, dense_rows = w_fc2.shape[0] // fsdp, w_dense.shape[0] // fsdp
    out_rows = fc2_rows + dense_rows
    any_ = pl.BlockSpec(memory_space=pl.ANY)

    def low(*shape):
        return pltpu.VMEM(shape, BF16)

    def wide(*shape):
        return pltpu.VMEM(shape, F32)

    def ctx_slots():
        return [
            low(rows, width), low(2, rows // 2, width), low(2, rows, width), low(2, rows, width),
            low(rows, width),
        ]

    def fsdp_slots(depth, columns, cut):
        return [
            low(fsdp, depth, columns), low(2, cut, columns), low(2, depth - cut, columns),
            low(2, 2, depth, columns), low(depth, columns), low(depth, columns),
        ]

    vector = (16, width // 2)
    many = 2 * 16 + 2 * 9 + 3 * 16 + 9 + 16
    ahead = 4
    operands = (att, act, d_proj, d_up, w_in, w_fc2, w_dense, stat, cotangent)
    return pl.pallas_call(
        second_kernel,
        out_shape=(
            jax.ShapeDtypeStruct((rows, width), F32),
            jax.ShapeDtypeStruct((rows, width), F32),
            jax.ShapeDtypeStruct((ctx, side, in_columns), BF16),
            jax.ShapeDtypeStruct((ctx, fc2_rows, width), BF16),
            jax.ShapeDtypeStruct((ctx, dense_rows, width), BF16),
            jax.ShapeDtypeStruct((ctx,) + vector, F32),
        ),
        in_specs=[any_] * 12,
        out_specs=(any_,) * 6,
        scratch_shapes=[pltpu.VMEM(operand.shape, operand.dtype) for operand in operands]
        + [low(ctx // 2, rows, width)] * 4
        + [low(2, rows, width)] * 2
        + ctx_slots()
        + ctx_slots()
        + fsdp_slots(side, in_columns, side // 2)
        + fsdp_slots(out_rows, width, 48)
        + [low(dense_rows, width)]
        + [
            low(ahead, ctx * rows, side), low(2, 2, rows, width), wide(rows, width),
            wide(rows, width), wide(8, width), wide(8, width),
            wide(*vector), wide(fsdp, *vector), wide(*vector),
            pltpu.SemaphoreType.DMA((many,)),
            pltpu.SemaphoreType.DMA((many,)),
            pltpu.SemaphoreType.DMA((8,)),
            pltpu.SemaphoreType.DMA((2 + ahead,)),
            pltpu.SemaphoreType.DMA((len(operands),)),
            pltpu.SemaphoreType.DMA,
            pltpu.SemaphoreType.DMA,
        ],
        compiler_params=pltpu.CompilerParams(
            collective_id=1, has_side_effects=True, vmem_limit_bytes=63 * MIB
        ),
        name="second",
    )(*operands, x_all, g_all.reshape(ctx * rows, width), hidden)


def widen_kernel(
    in_all, fc2_all, dense_all, branches_in, d_hidden_in, x_in, g_in, small_in,
    qkv, fc1, dense, fc2, result_to, input_grad_to,
    in_low, fc2_low, dense_low, qkv_wide, fc1_wide, fc2_wide, dense_wide,
    vec, branches, d_hidden, x_own, g_own, small, result, input_grad, loads, stores, reads,
):
    count = in_all.shape[0] // 2
    slots = in_low.shape[0]
    own = qkv.shape[1] // 3 // count
    units = fc1.shape[1] // count
    fc2_step, dense_step = fc2.shape[0] // count, dense.shape[0] // count // 2
    cut = 3 * own // 2

    def load(at):
        slot = at % slots
        copies = [
            pltpu.make_async_copy(source.at[pl.ds(2 * at, 2)], target.at[slot], loads.at[slot, number])
            for number, (source, target) in enumerate(
                [(in_all, in_low), (fc2_all, fc2_low), (dense_all, dense_low)]
            )
        ]
        for copy in copies:
            copy.start()
        return copies

    ahead = [load(at) for at in range(slots - 1)]
    stored = []
    own_rows = [
        pltpu.make_async_copy(source, target, reads.at[at])
        for at, (source, target) in enumerate(
            [
                (branches_in, branches), (d_hidden_in, d_hidden), (x_in, x_own), (g_in, g_own),
                (small_in, small),
            ]
        )
    ]
    for copy in own_rows:
        copy.start()

    side = small.shape[2]

    def finish():
        take = slice(None)
        token = x_own[take, :].astype(F32)
        result[take, :] = (token + branches[take, :] + vec[2:3, :] + vec[3:4, :]).astype(BF16)
        centred = token - jnp.mean(token, axis=1, keepdims=True)
        inverse = lax.rsqrt(jnp.mean(centred * centred, axis=1, keepdims=True) + NORM_EPS)
        normed = centred * inverse
        scaled = d_hidden[take, :] * vec[0:1, :]
        input_grad[take, :] = g_own[take, :].astype(F32) + inverse * (
            scaled
            - jnp.mean(scaled, axis=1, keepdims=True)
            - normed * jnp.mean(scaled * normed, axis=1, keepdims=True)
        )

    for at in range(count):
        slot = at % slots
        for copy in ahead[at]:
            copy.wait()
        if at + slots - 1 < count:
            ahead.append(load(at + slots - 1))
        if at >= slots:
            for copy in stored[at - slots]:
                copy.wait()
        half = own // 2
        for core in range(2):
            for part in range(3):
                first = part * own + core * half
                qkv_wide[slot, :, first : first + half] = in_low[
                    slot, core, :, part * half : (part + 1) * half
                ].astype(F32)
            fc2_wide[slot, core * (fc2_step // 2) : (core + 1) * (fc2_step // 2), :] = fc2_low[
                slot, core
            ].astype(F32)
            dense_wide[slot, core] = dense_low[slot, core].astype(F32)
        for part in range(count // 2):
            first = cut + part * 128
            left = in_low[slot, 0, :, first : first + 128].astype(F32)
            right = in_low[slot, 1, :, first : first + 128].astype(F32)
            fc1_wide[slot, :, 2 * part * 128 : (2 * part + 1) * 128] = fold(left, right, True)
            fc1_wide[slot, :, (2 * part + 1) * 128 : (2 * part + 2) * 128] = fold(left, right, False)
        targets = [
            (
                qkv_wide.at[slot, :, pl.ds(part * own, own)],
                qkv.at[:, pl.ds((part * count + at) * own, own)],
            )
            for part in range(3)
        ] + [
            (
                fc1_wide.at[slot, :, pl.ds(part * 128, 128)],
                fc1.at[:, pl.ds(part * units + at * 128, 128)],
            )
            for part in range(count)
        ] + [
            (fc2_wide.at[slot], fc2.at[pl.ds(at * fc2_step, fc2_step)]),
        ] + [
            (
                dense_wide.at[slot, core],
                dense.at[pl.ds((core * count + at) * dense_step, dense_step)],
            )
            for core in range(2)
        ]
        copies = [
            pltpu.make_async_copy(source, target, stores.at[slot, number])
            for number, (source, target) in enumerate(targets)
        ]
        for copy in copies:
            copy.start()
        stored.append(copies)
        if at == 2:
            for copy in own_rows:
                copy.wait()
            for shard in range(small.shape[0]):
                vec[0:4, shard * side : (shard + 1) * side] = small[shard, 0:4, :]
            finish()
    writes = [
        pltpu.make_async_copy(result, result_to, reads.at[0]),
        pltpu.make_async_copy(input_grad, input_grad_to, reads.at[1]),
    ]
    for copy in writes:
        copy.start()
    for copies in stored[-slots:]:
        for copy in copies:
            copy.wait()
    for copy in writes:
        copy.wait()


def widen(in_all, fc2_all, dense_all, branches, d_hidden, tokens, cotangent, small, ff):
    any_ = pl.BlockSpec(memory_space=pl.ANY)
    rows, width = tokens.shape
    fsdp = small.shape[0]
    slots = 3
    side = width // fsdp
    shapes = [(side, 3 * width), (side, ff), (side, width), (ff // fsdp, width)]
    return pl.pallas_call(
        widen_kernel,
        out_shape=tuple(jax.ShapeDtypeStruct(shape, F32) for shape in shapes)
        + (jax.ShapeDtypeStruct((rows, width), BF16), jax.ShapeDtypeStruct((rows, width), F32)),
        in_specs=[any_] * 8,
        out_specs=(any_,) * 6,
        scratch_shapes=[
            pltpu.VMEM((slots, 2) + in_all.shape[1:], BF16),
            pltpu.VMEM((slots, 2) + fc2_all.shape[1:], BF16),
            pltpu.VMEM((slots, 2) + dense_all.shape[1:], BF16),
            pltpu.VMEM((slots, side, 3 * width // fsdp), F32),
            pltpu.VMEM((slots, side, ff // fsdp), F32),
            pltpu.VMEM((slots, ff // fsdp // fsdp, width), F32),
            pltpu.VMEM((slots, 2) + dense_all.shape[1:], F32),
            pltpu.VMEM((8, width), F32),
            pltpu.VMEM((rows, width), F32),
            pltpu.VMEM((rows, width), F32),
            pltpu.VMEM((rows, width), BF16),
            pltpu.VMEM((rows, width), BF16),
            pltpu.VMEM(small.shape, F32),
            pltpu.VMEM((rows, width), BF16),
            pltpu.VMEM((rows, width), F32),
            pltpu.SemaphoreType.DMA((slots, 3)),
            pltpu.SemaphoreType.DMA((slots, 14)),
            pltpu.SemaphoreType.DMA((5,)),
        ],
        compiler_params=pltpu.CompilerParams(vmem_limit_bytes=62 * MIB),
        name="widen",
    )(in_all, fc2_all, dense_all, branches, d_hidden, tokens, cotangent, small)


def on_device(
    tokens, cotangent, block_order, positions, ln_gain, ln_bias, w_qkv, b_qkv, w_dense, b_dense,
    w_fc1, b_fc1, w_fc2, b_fc2,
):
    ctx, fsdp = lax.axis_size("ctx"), lax.axis_size("fsdp")
    f = lax.axis_index("fsdp")
    rows, width = tokens.shape[1:]
    seq = rows * ctx
    ff = w_fc1.shape[1]
    own_width, own_ff = width // ctx, ff // ctx
    own_rows = width // fsdp
    cut = 3 * own_width
    tokens = tokens.reshape(rows, width)
    cotangent = cotangent.reshape(rows, width)

    vectors = (ln_gain, ln_bias, b_dense, b_fc2, b_qkv, b_fc1)
    small, used = jnp.zeros((32 * own_rows,), BF16), 0
    for vector in vectors:
        left = small.shape[0] - used - vector.shape[0]
        small = small + jnp.pad(vector, (used, left))
        used += vector.shape[0]
    small = small.reshape(32, own_rows)
    spread = turn_spread(own_width)
    (
        x_all, g_all, hidden, stat, queries, keys, values, d_att, act, d_up, w_in, fc2, dense, turns,
        small,
    ) = first(
        tokens, cotangent, turn_rows(positions.reshape(rows), own_width), w_qkv, w_fc1, w_dense, w_fc2,
        small, spread, ctx, fsdp,
    )
    att, d_proj = attention(
        block_order, seq // block_order.shape[0], queries, keys, values, d_att,
        turns.reshape(seq, own_width), spread,
    )
    branches, d_hidden, in_all, fc2_all, dense_all, vector = second(
        att, act, d_proj, d_up, w_in.reshape(width, -1), fc2.reshape(own_ff, width),
        dense.reshape(own_width, width), stat, cotangent, x_all, g_all, hidden, fsdp,
    )
    grad_qkv, grad_fc1, grad_dense, grad_fc2, result, input_grad = widen(
        in_all, fc2_all, dense_all, branches, d_hidden, tokens, cotangent, small, ff
    )

    vector = vector.reshape(ctx, -1)
    sums = jnp.sum(vector[:, : 3 * width], axis=0).reshape(3, width)
    sums = lax.dynamic_slice_in_dim(sums, f * own_rows, own_rows, 1)
    columns = vector[:, 3 * width : 3 * width + cut].reshape(ctx, 3, own_width)
    columns = columns.transpose(1, 0, 2).reshape(3 * width)
    units = vector[:, 3 * width + cut : 3 * width + cut + own_ff].reshape(ctx, fsdp, -1)
    units = lax.dynamic_slice_in_dim(units, f, 1, 1).reshape(ff // fsdp)
    return (
        result.reshape(1, rows, width),
        input_grad.reshape(1, rows, width),
        sums[0],
        sums[1],
        grad_qkv,
        lax.dynamic_slice_in_dim(columns, f * (3 * own_rows), 3 * own_rows, 0),
        grad_dense,
        sums[2],
        grad_fc1,
        units,
        grad_fc2,
        sums[2],
    )


def solution(mesh):
    split = P("fsdp", "ctx", None)
    matrix = P("fsdp", None)
    vector = P("fsdp")
    return jax.shard_map(
        on_device,
        mesh=mesh,
        in_specs=(split, split, P(), P("fsdp", "ctx"), vector, vector)
        + (matrix, vector) * 4,
        out_specs=(split, split, vector, vector) + (matrix, vector) * 4,
        check_vma=False,
    )
```
